256 devices in a mesh: ia: 8 (over y, core), wa: 8 (over x, z_hi), ao: 4 (over z_lo).
Axes of the slice: x: 4, y: 4, z: 8 (z_hi: 2, z_lo: 4; z = z_hi * 4 + z_lo), core: 2. Of those that a mesh axis runs over, the one named last changes fastest.
Arguments:
- residual: bfloat16 [2048, 14848], P(('ia', 'wa'), 'ao'), may hold values from -6 to 6
- context: bfloat16 [2048, 14848], P('ia', 'wa'), may hold values from -6 to 6
- proj_weight: bfloat16 [8, 1856, 14848], P('wa', 'ia', 'ao'), may hold values from -0.046875 to 0.046875
- out_grad: bfloat16 [2048, 14848], P(('ia', 'wa'), 'ao'), may hold values from -4 to 4
Outputs:
- updated: bfloat16 [2048, 14848], P(('ia', 'wa'), 'ao')
- context_grad: bfloat16 [2048, 14848], P(('ia', 'ao'), 'wa')
- weight_grad: bfloat16 [8, 1856, 14848], P('wa', 'ia', 'ao')
The draws below stay inside these ranges and needn't reach their ends.
All inputs are finite; a program needn't handle non-finite values.
Results may differ from the reference program's by a relative error of at most 0.017.
Values may be sent and summed in bfloat16 or wider, within the bound.
A program may use at most 128 MiB of HBM per device.

```python
import jax
import jax.numpy as jnp
from jax import lax

D = 14848
TOK_DEV = 256
TOKENS = 2048
N_IA = 8
N_WA = 8


def block_levels(stream_key, extent, split, smallest, largest):
    level, own = 1.0, jax.random.fold_in(stream_key, 6)
    for dim, blocks in split:
        steps = jnp.exp(jax.random.uniform(jax.random.fold_in(own, dim), (blocks,), jnp.float32, smallest / len(split), largest / len(split)))
        level = level * jnp.repeat(steps, extent[dim] // blocks).reshape([-1 if axis == dim else 1 for axis in range(len(extent))])
    return level


def gaussian(rng, dims, deviation, reach, shards=(), dtype=jnp.bfloat16):
    array = jax.random.normal(rng, dims, jnp.float32) * deviation
    if len(shards) > 0:
        array = block_levels(rng, dims, shards, -0.22, 0.18) * array
    return jnp.clip(array, min=-reach, max=reach).astype(dtype)


def setup_inputs(seed: int = 0) -> dict:
    key_of = jax.random.split(jax.random.key(seed), 5)
    return {
        "residual": gaussian(key_of[0], (TOKENS, D), 1.0, 6.0, ((0, 64), (1, 4))),
        "context": gaussian(key_of[1], (TOKENS, D), 1.0, 6.0, ((0, 8), (1, 8))),
        "proj_weight": gaussian(key_of[2], (N_WA, D // N_WA, D), D ** -0.5, 0.046875, ((0, 8), (1, 8), (2, 4))),
        "out_grad": gaussian(key_of[3], (TOKENS, D), 0.25, 4.0, ((0, 64), (1, 4))),
    }


def reference(residual, context, proj_weight, out_grad):
    weight = proj_weight.reshape(D, D)
    projected = jnp.dot(context, weight, preferred_element_type=jnp.float32)
    updated = (residual.astype(jnp.float32) + projected).astype(jnp.bfloat16)
    context_grad = jnp.dot(out_grad, weight.T, preferred_element_type=jnp.float32).astype(jnp.bfloat16)
    context_blocks = context.reshape(N_IA, TOK_DEV, D)
    grad_blocks = out_grad.reshape(N_IA, TOK_DEV, D)

    def accumulate(running, pair):
        products = jnp.dot(pair[0].T, pair[1], preferred_element_type=jnp.float32)
        rounded = lax.optimization_barrier(products.astype(jnp.bfloat16))
        return running + rounded.astype(jnp.float32), None

    running, _ = lax.scan(accumulate, jnp.zeros((D, D), jnp.float32), (context_blocks, grad_blocks))
    weight_grad = running.astype(jnp.bfloat16).reshape(N_WA, D // N_WA, D)
    return updated, context_grad, weight_grad
```

```python
import jax
import jax.numpy as jnp
from jax import lax
from jax.experimental import pallas as pl
from jax.experimental.pallas import tpu as pltpu
from jax.sharding import PartitionSpec as P

MESH = pl.DeviceIdType.MESH
BF16 = jnp.bfloat16
F32 = jnp.float32

ROWS = 232
D_ROW = 3712
SHIFT = 1792
WIN = 1920
NC = 3
CW = WIN // NC
TOK = 32


class Sems:
    def __init__(self):
        self.n = 0

    def take(self, count):
        base = self.n
        self.n += count
        return base


N_SEMS = 160


def kernel(
    res_ref, ctx_ref, w_ref, g_ref,
    upd_ref, cg_ref, wg_ref,
    Wb, Gb, Xs, Xb, XT,
    bufA, RA, bufB1, bufB2, RB1, RB2, PB1, PB2, PX, accP,
    bufY, RY, bufZ, RZ, bufC, RC, own,
    OWN, DY, RDY, RDC, TZ, RDZ,
    DWs, RW,
    ss, rs, ls,
):
    ia = lax.axis_index("ia")
    wa = lax.axis_index("wa")
    zl = lax.axis_index("ao")
    y, c = lax.div(ia, 2), lax.rem(ia, 2)
    x, zh = lax.div(wa, 2), lax.rem(wa, 2)
    oc, zn = 1 - c, 1 - zh

    def flip(v):
        return v + 1 - 2 * lax.rem(v, 2)

    ya, yb = flip(y), 3 - y

    def w_pair(yy, cc):
        return (1 - cc) * flip(yy) + cc * (3 - yy)

    def t_pair(yy, cc):
        return cc * flip(yy) + (1 - cc) * (3 - yy)

    wp, tp = w_pair(y, c), t_pair(y, c)
    xp, xm, x2 = lax.rem(x + 1, 4), lax.rem(x + 3, 4), lax.rem(x + 2, 4)

    def dev(yy=y, cc=c, xx=x, hh=zh, ll=zl):
        return (2 * yy + cc, 2 * xx + hh, ll)

    other_core = dev(cc=oc)
    partners = [
        other_core,
        dev(yy=ya, cc=0), dev(yy=ya, cc=1), dev(yy=yb, cc=0), dev(yy=yb, cc=1),
        dev(xx=xp), dev(xx=xm),
        dev(hh=zn), dev(hh=zn, cc=oc),
    ] + [dev(ll=lax.rem(zl + m, 4)) for m in (1, 2, 3)]

    barrier = pltpu.get_barrier_semaphore()
    for p in partners:
        pl.semaphore_signal(barrier, inc=1, device_id=p, device_id_type=MESH)
    pl.semaphore_wait(barrier, len(partners))

    s_idx, r_idx, l_idx = Sems(), Sems(), Sems()
    sent = []

    def send(src, dst, r, to, s=None):
        if s is None:
            s = s_idx.take(1)
        cp = pltpu.make_async_remote_copy(
            src_ref=src, dst_ref=dst, send_sem=ss.at[s], recv_sem=rs.at[r],
            device_id=to, device_id_type=MESH,
        )
        cp.start()
        return cp

    def post(*args):
        sent.append(send(*args))

    def got(dst, r):
        pltpu.make_async_remote_copy(
            src_ref=dst, dst_ref=dst, send_sem=ss.at[0], recv_sem=rs.at[r],
            device_id=other_core, device_id_type=MESH,
        ).wait_recv()

    def local(src, dst):
        cp = pltpu.make_async_copy(src, dst, ls.at[l_idx.take(1)])
        cp.start()
        return cp

    def window(cc):
        return pl.ds(pl.multiple_of(cc * SHIFT, 128), WIN)

    r_g0 = r_idx.take(2)
    r_g1 = r_idx.take(2)
    g_own = g_ref.at[:, window(c)]
    g_oth = g_ref.at[:, window(oc)]
    g_local = local(g_own, Gb.at[0, c, x, zh])
    post(g_oth, Gb.at[0, c, x, zh], r_g0 + c, other_core)
    post(g_own, Gb.at[0, c, x, zh], r_g1 + c, dev(hh=zn))
    post(g_oth, Gb.at[0, c, x, zh], r_g1 + c, dev(hh=zn, cc=oc))

    r_w = r_idx.take(4 * NC)

    def w_cols(cc, j):
        return pl.ds(pl.multiple_of(cc * SHIFT + j * CW, 128), CW)

    w_locals = []
    for j in range(NC):
        cols = pl.ds(j * CW, CW)
        w_locals.append(local(w_ref.at[:, w_cols(c, j)], Wb.at[c, :, cols]))
        post(w_ref.at[:, w_cols(oc, j)], Wb.at[c, :, cols], r_w + c * NC + j, other_core)

    def send_w(j):
        cols = pl.ds(j * CW, CW)
        for cc, yy in ((0, ya), (1, yb)):
            post(w_ref.at[:, w_cols(cc, j)], Wb.at[2 + c, :, cols],
                 r_w + (2 + c) * NC + j, dev(yy=yy, cc=cc))

    r_y = r_idx.take(2)
    r_xp = r_idx.take(4)
    r_xm = r_idx.take(4)
    r_f = r_idx.take(4)

    def unit(p, xx, h):
        return Gb.at[p, :, xx, h]

    def to_x(p, k, h):
        post(unit(p, x, h), unit(p, x, h), r_xp + 2 * p + k, dev(xx=xp))
        post(unit(p, x, h), unit(p, x, h), r_xm + 2 * p + k, dev(xx=xm))

    def forward(k, h):
        got(unit(0, xm, h), r_xp + k)
        post(unit(0, xm, h), unit(0, xm, h), r_f + k, dev(xx=xp))
        got(unit(1, xp, h), r_xm + 2 + k)
        post(unit(1, xp, h), unit(1, xp, h), r_f + 2 + k, dev(xx=xm))

    g_local.wait()
    got(Gb.at[0, oc, x, zh], r_g0 + oc)
    post(unit(0, x, zh), unit(1, x, zh), r_y, dev(yy=tp))
    to_x(0, 0, zh)
    send_w(0)

    for g in range(8):
        piece = ctx_ref[:, g * ROWS:(g + 1) * ROWS]
        piece = jnp.concatenate([piece, jnp.zeros((256, 256 - ROWS), BF16)], axis=1)
        Xs[g] = piece.reshape(4, 64, 256)
    r_c = r_idx.take(8)

    x_locals = []
    for q, yy in enumerate((y, w_pair(y, c))):
        x_locals.append(local(Xs.at[pl.ds(2 * yy, 2)], Xb.at[pl.ds(2 * q, 2), c]))
    for q, yy in enumerate((y, w_pair(y, oc))):
        post(Xs.at[pl.ds(2 * yy, 2)], Xb.at[pl.ds(2 * q, 2), c], r_c + 2 * c + q, other_core)
    for y_to, cc in ((yb, 0), (ya, 1)):
        for q, yy in enumerate((y_to, w_pair(y_to, cc))):
            post(Xs.at[pl.ds(2 * yy, 2)], Xb.at[pl.ds(2 * q, 2), 2 + c],
                 r_c + 2 * (2 + c) + q, dev(yy=y_to, cc=cc))

    got(unit(1, x, zh), r_y)
    to_x(1, 0, zh)
    forward(0, zh)

    def got_x(blk):
        for q in range(2):
            got(Xb.at[pl.ds(2 * q, 2), blk], r_c + 2 * blk + q)

    def transpose_x(blk):
        for s in range(4):
            t = Xb[s, blk].reshape(256, 256)
            XT[s, :, blk * 256:(blk + 1) * 256] = t.T

    for cp in x_locals:
        cp.wait()
    got_x(oc)
    transpose_x(0)
    transpose_x(1)

    for core in range(2):
        got(Gb.at[0, core, x, zn], r_g1 + core)
    post(unit(0, x, zn), unit(1, x, zn), r_y + 1, dev(yy=tp))
    to_x(0, 1, zn)
    for j in range(1, NC):
        send_w(j)
    got(unit(1, x, zn), r_y + 1)
    to_x(1, 1, zn)
    forward(1, zn)

    for blk in (2, 3):
        got_x(blk)
        transpose_x(blk)

    for cp in w_locals:
        cp.wait()
    for j in range(NC):
        cols = pl.ds(j * CW, CW)
        got(Wb.at[oc, :, cols], r_w + oc * NC + j)
        for s in (2, 3):
            got(Wb.at[s, :, cols], r_w + s * NC + j)
    keep = (c == 0).astype(BF16)
    for s in range(4):
        Wb[s, :, 0:128] = Wb[s, :, 0:128] * keep

    def cols_of(j):
        return pl.ds(pl.multiple_of(j * CW, 128), CW)

    def project(d, j):
        total = None
        for s in range(4):
            a = Xb[s, :, d].reshape(256, 256)[:, :ROWS]
            part = jnp.dot(a, Wb[s, :, cols_of(j)], preferred_element_type=F32)
            total = part if total is None else total + part
        return total.reshape(2, 128, CW)

    r_a = r_idx.take(2 * NC)
    r_b1 = r_idx.take(2 * NC)
    r_b2 = r_idx.take(2 * NC)
    s_a, s_b1, s_b2 = s_idx.take(2 * NC), s_idx.take(2 * NC), s_idx.take(2 * NC)
    to_xp, to_xm = dev(xx=xp), dev(xx=xm)

    def drain(src, s):
        pltpu.make_async_remote_copy(
            src_ref=src, dst_ref=src, send_sem=ss.at[s], recv_sem=rs.at[0],
            device_id=other_core, device_id_type=MESH,
        ).wait_send()

    @pl.loop(0, NC)
    def _(j):
        bufA[j] = project(x2, j).astype(BF16)
        send(bufA.at[j, 0], RA.at[j, 0], r_a + 2 * j, to_xp, s_a + 2 * j)
        send(bufA.at[j, 1], RA.at[j, 1], r_a + 2 * j + 1, to_xm, s_a + 2 * j + 1)

    r_dy, r_dc, r_dz = r_idx.take(4), r_idx.take(16), r_idx.take(4)
    s_dz = s_idx.take(4)
    blocks = (x, xp, xm, x2)

    def back(k):
        d = blocks[k]

        @pl.loop(0, 4)
        def _(s):
            g = Gb[:, :, d].reshape(256, WIN)
            t = lax.dot_general(g, Wb[s], (((1,), (1,)), ((), ())),
                                preferred_element_type=F32).astype(BF16)
            t = jnp.concatenate([t, jnp.zeros((256, 256 - ROWS), BF16)], axis=1)
            t = t.reshape(2, 2, 64, 256)
            OWN[k, s] = t[0]
            DY[k, s] = t[1]

        post(DY.at[k], RDY.at[k], r_dy + k, dev(yy=tp))

    back(0)
    for h, k in ((zh, 0), (zn, 1)):
        got(unit(1, xm, h), r_xp + 2 + k)
        got(unit(0, xp, h), r_xm + k)
    back(1)
    back(2)

    @pl.loop(0, NC)
    def _(j):
        v = project(xp, j)
        bufB1[j, 1] = v[1].astype(BF16)
        send(bufB1.at[j, 1], RB1.at[j, 1], r_b1 + 2 * j + 1, to_xp, s_b1 + 2 * j + 1)
        PB1[j] = v[0]
        v = project(xm, j)
        bufB2[j, 0] = v[0].astype(BF16)
        send(bufB2.at[j, 0], RB2.at[j, 0], r_b2 + 2 * j, to_xm, s_b2 + 2 * j)
        PB2[j] = v[1]

    for k, h in ((0, zh), (1, zn)):
        got(unit(0, x2, h), r_f + k)
        got(unit(1, x2, h), r_f + 2 + k)
    back(3)

    r_wg = r_idx.take(4 * NC)
    s_wg = s_idx.take(3 * NC)

    def grad(s, j):
        a = XT[s]
        b = Gb[:, :, :, :, :, cols_of(j)].reshape(1024, CW)
        return jnp.dot(a, b, preferred_element_type=F32)[:ROWS].astype(BF16)

    for core in range(2):
        to = dev(yy=wp, cc=core)

        @pl.loop(0, NC)
        def _(j):
            DWs[core, j] = grad(2 + core, j)
            send(DWs.at[core, j], RW.at[c, 1, j], r_wg + (2 * c + 1) * NC + j, to, s_wg + core * NC + j)

    @pl.loop(0, NC)
    def _(j):
        got(RA.at[j, 0], r_a + 2 * j)
        bufB1[j, 0] = (PB1[j] + RA[j, 0].astype(F32)).astype(BF16)
        send(bufB1.at[j, 0], RB1.at[j, 0], r_b1 + 2 * j, to_xp, s_b1 + 2 * j)
        got(RA.at[j, 1], r_a + 2 * j + 1)
        bufB2[j, 1] = (PB2[j] + RA[j, 1].astype(F32)).astype(BF16)
        send(bufB2.at[j, 1], RB2.at[j, 1], r_b2 + 2 * j + 1, to_xm, s_b2 + 2 * j + 1)

    own_groups = (y, wp)
    got_groups = (tp, w_pair(tp, c))
    for k in range(4):
        got(RDY.at[k], r_dy + k)
        for q in range(2):
            for part, group in ((OWN, own_groups[q]), (RDY, got_groups[q])):
                post(part.at[k, pl.ds(2 * q, 2), oc], RDC.at[k, group],
                     r_dc + 4 * k + group, other_core)

    @pl.loop(0, NC)
    def _(j):
        DWs[2, j] = grad(oc, j)
        send(DWs.at[2, j], RW.at[c, 0, j], r_wg + 2 * c * NC + j, other_core, s_wg + 2 * NC + j)

    @pl.loop(0, NC)
    def _(j):
        RW[c, 0, j] = grad(c, j)

    for k in range(4):
        d = blocks[k]
        for group in range(4):
            got(RDC.at[k, group], r_dc + 4 * k + group)
        for q in range(2):
            for part, group in ((OWN, own_groups[q]), (RDY, got_groups[q])):
                TZ[k, group] = (part[k, 2 * q:2 * q + 2, c].astype(F32)
                                + RDC[k, group].astype(F32)).astype(BF16)

        @pl.when(d != zl)
        def _():
            send(TZ.at[k], RDZ.at[zl], r_dz + zl, dev(ll=d), s_dz + k)

        @pl.when(d == zl)
        def _():
            RDZ[zl] = TZ[k]

    r_py, r_pz, r_pc = r_idx.take(NC), r_idx.take(NC), r_idx.take(NC)
    s_py, s_pz, s_pc = s_idx.take(NC), s_idx.take(NC), s_idx.take(NC)

    @pl.loop(0, NC)
    def _(j):
        PX[j] = project(x, j)

    @pl.loop(0, NC)
    def _(j):
        got(RB1.at[j, 1], r_b1 + 2 * j + 1)
        got(RB2.at[j, 1], r_b2 + 2 * j + 1)
        bufY[j] = (PX[j, 1] + RB1[j, 1].astype(F32) + RB2[j, 1].astype(F32)).astype(BF16)
        send(bufY.at[j], RY.at[j], r_py + j, dev(yy=tp), s_py + j)

    @pl.loop(0, NC)
    def _(j):
        got(RB1.at[j, 0], r_b1 + 2 * j)
        got(RB2.at[j, 0], r_b2 + 2 * j)
        v = PX[j, 0] + RB1[j, 0].astype(F32) + RB2[j, 0].astype(F32)
        got(RY.at[j], r_py + j)
        v = v + RY[j].astype(F32)
        accP[j] = v.reshape(2, 2, TOK, CW)
        bufZ[j] = accP[j, :, zn].astype(BF16)
        send(bufZ.at[j], RZ.at[j], r_pz + j, dev(hh=zn), s_pz + j)

    for m in (1, 2, 3):
        src = lax.rem(zl + m, 4)
        got(RDZ.at[src], r_dz + src)
    total = RDZ[0].astype(F32)
    for m in (1, 2, 3):
        total = total + RDZ[m].astype(F32)
    cg_ref[...] = total.astype(BF16).reshape(8, 64, 256)

    @pl.loop(0, NC)
    def _(j):
        got(RZ.at[j], r_pz + j)
        own[j] = accP[j, c, zh] + RZ[j, c].astype(F32)
        bufC[j] = accP[j, oc, zh] + RZ[j, oc].astype(F32)
        send(bufC.at[j], RC.at[j], r_pc + j, other_core, s_pc + j)

    @pl.loop(0, NC)
    def _(j):
        got(RW.at[oc, 0, j], r_wg + 2 * oc * NC + j)
        for w in range(2):
            got(RW.at[w, 1, j], r_wg + (2 * w + 1) * NC + j)

    for w in range(2):
        @pl.loop(0, NC)
        def _(j):
            cols = pl.ds(pl.multiple_of(w * SHIFT + j * CW, 128), CW)
            wg_ref[:, cols] = (RW[w, 0, j].astype(F32) + RW[w, 1, j].astype(F32)).astype(BF16)

    for j in range(NC):
        got(RC.at[j], r_pc + j)
    for w in (1, 0):
        for j in range(NC):
            cols = slice(w * SHIFT + j * CW, w * SHIFT + (j + 1) * CW)
            v = jnp.where(c == w, own[j], RC[j])
            upd_ref[:, cols] = (res_ref[:, cols].astype(F32) + v).astype(BF16)

    for cp in sent:
        cp.wait_send()
    for j in range(NC):
        for h in range(2):
            drain(bufA.at[j, h], s_a + 2 * j + h)
            drain(bufB1.at[j, h], s_b1 + 2 * j + h)
            drain(bufB2.at[j, h], s_b2 + 2 * j + h)
        for s in range(3):
            drain(DWs.at[s, j], s_wg + s * NC + j)
        drain(bufY.at[j], s_py + j)
        drain(bufZ.at[j], s_pz + j)
        drain(bufC.at[j], s_pc + j)
    for k in range(4):
        @pl.when(blocks[k] != zl)
        def _():
            drain(TZ.at[k], s_dz + k)


def per_device(residual, context, proj_weight, out_grad):
    vmem = pl.BlockSpec(memory_space=pltpu.VMEM)
    anywhere = pl.BlockSpec(memory_space=pl.ANY)
    shape = jax.ShapeDtypeStruct
    updated, context_grad, weight_grad = pl.pallas_call(
        kernel,
        out_shape=(
            shape((TOK, D_ROW), BF16),
            shape((8, 64, 256), BF16),
            shape((ROWS, D_ROW), BF16),
        ),
        in_specs=[vmem, vmem, anywhere, anywhere],
        out_specs=(vmem, vmem, vmem),
        scratch_shapes=[
            pltpu.VMEM((4, ROWS, WIN), BF16),
            pltpu.VMEM((2, 2, 4, 2, TOK, WIN), BF16),
            pltpu.VMEM((8, 4, 64, 256), BF16),
            pltpu.VMEM((4, 4, 4, 64, 256), BF16),
            pltpu.VMEM((4, 256, 1024), BF16),
            pltpu.VMEM((NC, 2, 128, CW), BF16),
            pltpu.VMEM((NC, 2, 128, CW), BF16),
            pltpu.VMEM((NC, 2, 128, CW), BF16),
            pltpu.VMEM((NC, 2, 128, CW), BF16),
            pltpu.VMEM((NC, 2, 128, CW), BF16),
            pltpu.VMEM((NC, 2, 128, CW), BF16),
            pltpu.VMEM((NC, 128, CW), F32),
            pltpu.VMEM((NC, 128, CW), F32),
            pltpu.VMEM((NC, 2, 128, CW), F32),
            pltpu.VMEM((NC, 2, 2, TOK, CW), F32),
            pltpu.VMEM((NC, 128, CW), BF16),
            pltpu.VMEM((NC, 128, CW), BF16),
            pltpu.VMEM((NC, 2, TOK, CW), BF16),
            pltpu.VMEM((NC, 2, TOK, CW), BF16),
            pltpu.VMEM((NC, TOK, CW), F32),
            pltpu.VMEM((NC, TOK, CW), F32),
            pltpu.VMEM((NC, TOK, CW), F32),
            pltpu.VMEM((4, 4, 2, 64, 256), BF16),
            pltpu.VMEM((4, 4, 2, 64, 256), BF16),
            pltpu.VMEM((4, 4, 2, 64, 256), BF16),
            pltpu.VMEM((4, 4, 2, 64, 256), BF16),
            pltpu.VMEM((4, 4, 2, 64, 256), BF16),
            pltpu.VMEM((4, 4, 2, 64, 256), BF16),
            pltpu.VMEM((3, NC, ROWS, CW), BF16),
            pltpu.VMEM((2, 2, NC, ROWS, CW), BF16),
            pltpu.SemaphoreType.DMA((N_SEMS,)),
            pltpu.SemaphoreType.DMA((N_SEMS,)),
            pltpu.SemaphoreType.DMA((16,)),
        ],
        compiler_params=pltpu.CompilerParams(
            collective_id=0, has_side_effects=True, vmem_limit_bytes=60 * 2**20
        ),
        cost_estimate=pl.CostEstimate(
            flops=6 * 1024 * 928 * WIN, bytes_accessed=8 * 2**20, transcendentals=0
        ),
    )(residual, context, proj_weight[0], out_grad)
    context_grad = context_grad[:, :, :ROWS].transpose(1, 0, 2).reshape(64, 8 * ROWS)
    return updated, context_grad, weight_grad[None]


def solution(mesh):
    in_specs = (P(("ia", "wa"), "ao"), P("ia", "wa"), P("wa", "ia", "ao"), P(("ia", "wa"), "ao"))
    out_specs = (P(("ia", "wa"), "ao"), P(("ia", "ao"), "wa"), P("wa", "ia", "ao"))
    return jax.shard_map(
        per_device, mesh=mesh, in_specs=in_specs, out_specs=out_specs, check_vma=False
    )
```

```python
import jax
import jax.numpy as jnp
from jax import lax
from jax.experimental import pallas as pl
from jax.experimental.pallas import tpu as pltpu
from jax.sharding import PartitionSpec as P

MESH = pl.DeviceIdType.MESH
BF16 = jnp.bfloat16
F32 = jnp.float32

ROWS = 232
D_ROW = 3712
SHIFT = 1792
WIN = 1920
NC = 3
CW = WIN // NC
TOK = 32


class Sems:
    def __init__(self):
        self.n = 0

    def take(self, count):
        base = self.n
        self.n += count
        return base


N_SEMS = 224


def kernel(
    res_ref, ctx_ref, w_ref, g_ref,
    upd_ref, cg_ref, wg_ref,
    Wb, Gb, Xb, XT,
    bufA, RA, bufB1, bufB2, RB1, RB2, PF, accP,
    bufY, RY, bufZ, RZ, bufC, RC, own,
    OWN, DY, RDY, RDC, TZ, RDZ,
    DWs, RW,
    ss, rs, ls,
):
    ia = lax.axis_index("ia")
    wa = lax.axis_index("wa")
    zl = lax.axis_index("ao")
    y, c = lax.div(ia, 2), lax.rem(ia, 2)
    x, zh = lax.div(wa, 2), lax.rem(wa, 2)
    oc, zn = 1 - c, 1 - zh

    def flip(v):
        return v + 1 - 2 * lax.rem(v, 2)

    ya, yb = flip(y), 3 - y

    def w_pair(yy, cc):
        return (1 - cc) * flip(yy) + cc * (3 - yy)

    def t_pair(yy, cc):
        return cc * flip(yy) + (1 - cc) * (3 - yy)

    wp, tp = w_pair(y, c), t_pair(y, c)
    xp, xm, x2 = lax.rem(x + 1, 4), lax.rem(x + 3, 4), lax.rem(x + 2, 4)

    def dev(yy=y, cc=c, xx=x, hh=zh, ll=zl):
        return (2 * yy + cc, 2 * xx + hh, ll)

    other_core = dev(cc=oc)
    partners = [
        other_core,
        dev(yy=ya, cc=0), dev(yy=ya, cc=1), dev(yy=yb, cc=0), dev(yy=yb, cc=1),
        dev(xx=xp), dev(xx=xm),
        dev(hh=zn), dev(hh=zn, cc=oc),
    ] + [dev(ll=lax.rem(zl + m, 4)) for m in (1, 2, 3)]

    barrier = pltpu.get_barrier_semaphore()
    for p in partners:
        pl.semaphore_signal(barrier, inc=1, device_id=p, device_id_type=MESH)
    pl.semaphore_wait(barrier, len(partners))

    s_idx, r_idx, l_idx = Sems(), Sems(), Sems()
    sent = []

    def send(src, dst, r, to, s=None):
        if s is None:
            s = s_idx.take(1)
        cp = pltpu.make_async_remote_copy(
            src_ref=src, dst_ref=dst, send_sem=ss.at[s], recv_sem=rs.at[r],
            device_id=to, device_id_type=MESH,
        )
        cp.start()
        return cp

    def post(*args):
        sent.append(send(*args))

    def got(dst, r):
        pltpu.make_async_remote_copy(
            src_ref=dst, dst_ref=dst, send_sem=ss.at[0], recv_sem=rs.at[r],
            device_id=other_core, device_id_type=MESH,
        ).wait_recv()

    def local(src, dst):
        cp = pltpu.make_async_copy(src, dst, ls.at[l_idx.take(1)])
        cp.start()
        return cp

    def window(cc):
        return pl.ds(pl.multiple_of(cc * SHIFT, 128), WIN)

    r_g0 = r_idx.take(2)
    r_g1 = r_idx.take(2)
    g_own = g_ref.at[:, window(c)]
    g_oth = g_ref.at[:, window(oc)]
    g_local = local(g_own, Gb.at[0, c, x, zh])
    post(g_oth, Gb.at[0, c, x, zh], r_g0 + c, other_core)
    post(g_own, Gb.at[0, c, x, zh], r_g1 + c, dev(hh=zn))
    post(g_oth, Gb.at[0, c, x, zh], r_g1 + c, dev(hh=zn, cc=oc))

    r_w = r_idx.take(4 * NC)

    def w_cols(cc, j):
        return pl.ds(pl.multiple_of(cc * SHIFT + j * CW, 128), CW)

    w_locals = []
    for j in range(NC):
        cols = pl.ds(j * CW, CW)
        w_locals.append(local(w_ref.at[:, w_cols(c, j)], Wb.at[c, :, cols]))
        post(w_ref.at[:, w_cols(oc, j)], Wb.at[c, :, cols], r_w + c * NC + j, other_core)

    def send_w(j):
        cols = pl.ds(j * CW, CW)
        for cc, yy in ((0, ya), (1, yb)):
            post(w_ref.at[:, w_cols(cc, j)], Wb.at[2 + c, :, cols],
                 r_w + (2 + c) * NC + j, dev(yy=yy, cc=cc))

    r_y = r_idx.take(4)
    r_xp = r_idx.take(4)
    r_xm = r_idx.take(4)
    r_f = r_idx.take(4)

    def unit(p, xx, h):
        return Gb.at[p, :, xx, h]

    def to_x(p, k, h):
        post(unit(p, x, h), unit(p, x, h), r_xp + 2 * p + k, dev(xx=xp))
        post(unit(p, x, h), unit(p, x, h), r_xm + 2 * p + k, dev(xx=xm))

    def forward_up(k, h):
        got(unit(0, xm, h), r_xp + k)
        post(unit(0, xm, h), unit(0, xm, h), r_f + k, dev(xx=xp))

    def forward_down(k, h):
        got(unit(1, xp, h), r_xm + 2 + k)
        post(unit(1, xp, h), unit(1, xp, h), r_f + 2 + k, dev(xx=xm))

    def to_partner(k, h):
        for core in range(2):
            post(Gb.at[0, core, x, h], Gb.at[1, core, x, h], r_y + 2 * k + core, dev(yy=tp))

    def from_partner(k, h):
        for core in range(2):
            got(Gb.at[1, core, x, h], r_y + 2 * k + core)

    g_local.wait()
    got(Gb.at[0, oc, x, zh], r_g0 + oc)
    to_partner(0, zh)
    to_x(0, 0, zh)

    r_c = r_idx.take(8)
    half = lax.rem(zl, 2)

    def x_block(q, blk):
        return XT.at[pl.ds(2 * q, 2), :, pl.ds(pl.multiple_of(blk * 256, 256), 256)]

    def x_group(q, yy, cc):
        chip = (1 - q) * yy + q * w_pair(yy, cc)
        return ctx_ref.at[pl.ds(2 * chip, 2)]

    def got_x(q, blk):
        got(x_block(q, blk), r_c + 2 * blk + q)

    def transpose_x(s, blk):
        t = XT[s, :, blk * 256:(blk + 1) * 256].T
        Xb[s, blk] = t.reshape(4, 64, ROWS)

    for y_to, cc in ((yb, 0), (ya, 1)):
        post(x_group(half, y_to, cc), x_block(half, 2 + c), r_c + 2 * (2 + c) + half, dev(yy=y_to, cc=cc))
    x_locals = []
    for q in range(2):
        x_locals.append(local(x_group(q, y, c), x_block(q, c)))
        post(x_group(q, y, oc), x_block(q, c), r_c + 2 * c + q, other_core)

    from_partner(0, zh)
    to_x(1, 0, zh)
    send_w(0)
    for cp in x_locals:
        cp.wait()
    for q in range(2):
        got_x(q, oc)
    for blk in range(2):
        for sl in range(4):
            transpose_x(sl, blk)
    for blk in (2, 3):
        got_x(half, blk)
        post(x_block(half, blk), x_block(half, blk), r_c + 2 * blk + half, dev(ll=flip(zl)))
    for blk in (2, 3):
        for sl in range(2):
            transpose_x(2 * half + sl, blk)
    forward_up(0, zh)
    forward_down(0, zh)

    for core in range(2):
        got(Gb.at[0, core, x, zn], r_g1 + core)
    to_partner(1, zn)
    to_x(0, 1, zn)
    send_w(1)
    from_partner(1, zn)
    to_x(1, 1, zn)
    send_w(2)

    for blk in (2, 3):
        got_x(1 - half, blk)
        for sl in range(2):
            transpose_x(2 * (1 - half) + sl, blk)
    for cp in w_locals:
        cp.wait()

    def project(j):
        total = None
        for sl in range(4):
            a = Xb[sl].reshape(1024, ROWS)
            part = jnp.dot(a, Wb[sl, :, j * CW:(j + 1) * CW], preferred_element_type=F32)
            total = part if total is None else total + part
        PF[j] = total.reshape(2, 2, 4, 64, CW)

    r_a = r_idx.take(2 * NC)
    r_b1 = r_idx.take(2 * NC)
    r_b2 = r_idx.take(2 * NC)
    to_xp, to_xm = dev(xx=xp), dev(xx=xm)

    def drain(src, s):
        pltpu.make_async_remote_copy(
            src_ref=src, dst_ref=src, send_sem=ss.at[s], recv_sem=rs.at[0],
            device_id=other_core, device_id_type=MESH,
        ).wait_send()

    def got_w(j):
        cols = pl.ds(j * CW, CW)
        got(Wb.at[oc, :, cols], r_w + oc * NC + j)
        for s in (2, 3):
            got(Wb.at[s, :, cols], r_w + s * NC + j)
        if j == 0:
            keep = (c == 0).astype(BF16)
            for s in range(4):
                Wb[s, :, 0:128] = Wb[s, :, 0:128] * keep

    def project_chunk(j):
        got_w(j)
        project(j)

    def post_a(j):
        bufA[j] = PF[j, :, :, x2].astype(BF16)
        post(bufA.at[j, 0], RA.at[j, 0], r_a + 2 * j, to_xp)
        post(bufA.at[j, 1], RA.at[j, 1], r_a + 2 * j + 1, to_xm)

    def post_b(j):
        bufB1[j, 1] = PF[j, 1, :, xp].astype(BF16)
        post(bufB1.at[j, 1], RB1.at[j, 1], r_b1 + 2 * j + 1, to_xp)
        bufB2[j, 0] = PF[j, 0, :, xm].astype(BF16)
        post(bufB2.at[j, 0], RB2.at[j, 0], r_b2 + 2 * j, to_xm)

    def pass_on(j):
        got(RA.at[j, 0], r_a + 2 * j)
        bufB1[j, 0] = (PF[j, 0, :, xp] + RA[j, 0].astype(F32)).astype(BF16)
        post(bufB1.at[j, 0], RB1.at[j, 0], r_b1 + 2 * j, to_xp)
        got(RA.at[j, 1], r_a + 2 * j + 1)
        bufB2[j, 1] = (PF[j, 1, :, xm] + RA[j, 1].astype(F32)).astype(BF16)
        post(bufB2.at[j, 1], RB2.at[j, 1], r_b2 + 2 * j + 1, to_xm)

    r_dy, r_dc, r_dz = r_idx.take(4), r_idx.take(16), r_idx.take(4)
    s_dz = s_idx.take(4)
    blocks = (x, xp, xm, x2)

    def back(k):
        d = blocks[k]

        @pl.loop(0, 4)
        def _(s):
            g = Gb[:, :, d].reshape(256, WIN)
            t = lax.dot_general(g, Wb[s], (((1,), (1,)), ((), ())),
                                preferred_element_type=F32).astype(BF16)
            t = jnp.concatenate([t, jnp.zeros((256, 256 - ROWS), BF16)], axis=1)
            t = t.reshape(2, 2, 64, 256)
            OWN[k, s] = t[0]
            DY[k, s] = t[1]

        post(DY.at[k], RDY.at[k], r_dy + k, dev(yy=tp))

    r_wg = r_idx.take(4 * NC)
    s_wg = s_idx.take(3 * NC)

    def grad(s, j):
        cols = pl.ds(pl.multiple_of(j * CW, 128), CW)
        b = Gb[:, :, :, :, :, cols].reshape(1024, CW)
        return jnp.dot(XT[s], b, preferred_element_type=F32).astype(BF16)

    own_groups = (y, wp)
    got_groups = (tp, w_pair(tp, c))

    def to_core(k):
        got(RDY.at[k], r_dy + k)
        for q in range(2):
            for part, group in ((OWN, own_groups[q]), (RDY, got_groups[q])):
                post(part.at[k, pl.ds(2 * q, 2), oc], RDC.at[k, group],
                     r_dc + 4 * k + group, other_core)

    def to_ao(k):
        d = blocks[k]
        for group in range(4):
            got(RDC.at[k, group], r_dc + 4 * k + group)
        for q in range(2):
            for part, group in ((OWN, own_groups[q]), (RDY, got_groups[q])):
                TZ[k, group] = (part[k, 2 * q:2 * q + 2, c].astype(F32)
                                + RDC[k, group].astype(F32)).astype(BF16)

        @pl.when(d != zl)
        def _():
            send(TZ.at[k], RDZ.at[zl], r_dz + zl, dev(ll=d), s_dz + k)

        @pl.when(d == zl)
        def _():
            RDZ[zl] = TZ[k]

    def grad_other(core):
        to = dev(yy=wp, cc=core)

        @pl.loop(0, NC)
        def _(j):
            DWs[core, j] = grad(2 + core, j)
            send(DWs.at[core, j], RW.at[c, 1, j], r_wg + (2 * c + 1) * NC + j, to, s_wg + core * NC + j)

    def grad_own():
        @pl.loop(0, NC)
        def _(j):
            DWs[2, j] = grad(oc, j)
            send(DWs.at[2, j], RW.at[c, 0, j], r_wg + 2 * c * NC + j, other_core, s_wg + 2 * NC + j)

        @pl.loop(0, NC)
        def _(j):
            RW[c, 0, j] = grad(c, j)

    project_chunk(0)
    forward_up(1, zn)
    forward_down(1, zn)
    post_a(0)
    got_w(1)
    got_w(2)
    back(0)
    project(1)
    for h, k in ((zh, 0), (zn, 1)):
        got(unit(1, xm, h), r_xp + 2 + k)
        got(unit(0, xp, h), r_xm + k)
    back(1)
    to_core(0)
    post_b(0)
    back(2)
    post_a(1)
    for k, h in ((0, zh), (1, zn)):
        got(unit(0, x2, h), r_f + k)
        got(unit(1, x2, h), r_f + 2 + k)
    back(3)
    to_ao(0)
    post_b(1)
    grad_other(0)
    to_core(1)
    grad_other(1)
    pass_on(0)
    to_ao(1)
    to_core(2)
    project(2)
    post_a(2)
    post_b(2)
    to_ao(2)
    to_core(3)
    pass_on(1)
    to_ao(3)
    grad_own()
    pass_on(2)

    r_py, r_pz, r_pc = r_idx.take(8 * NC), r_idx.take(4 * NC), r_idx.take(NC)

    def to_y(j):
        got(RB1.at[j, 1], r_b1 + 2 * j + 1)
        got(RB2.at[j, 1], r_b2 + 2 * j + 1)
        v = PF[j, 1, :, x] + RB1[j, 1].astype(F32) + RB2[j, 1].astype(F32)
        bufY[j] = v.astype(BF16).reshape(8, 16, CW)
        for h in range(8):
            post(bufY.at[j, h], RY.at[j, h], r_py + 8 * j + h, dev(yy=tp))

    def to_z(j):
        got(RB1.at[j, 0], r_b1 + 2 * j)
        got(RB2.at[j, 0], r_b2 + 2 * j)
        v = PF[j, 0, :, x] + RB1[j, 0].astype(F32) + RB2[j, 0].astype(F32)
        for h in range(8):
            got(RY.at[j, h], r_py + 8 * j + h)
        v = v.reshape(2, 2, TOK, CW) + RY[j].astype(F32).reshape(2, 2, TOK, CW)
        accP[j] = v
        bufZ[j] = accP[j, :, zn].astype(BF16).reshape(4, 16, CW)
        for h in range(4):
            post(bufZ.at[j, h], RZ.at[j, h], r_pz + 4 * j + h, dev(hh=zn))

    def to_c(j):
        for h in range(4):
            got(RZ.at[j, h], r_pz + 4 * j + h)
        own[j] = accP[j, c, zh] + RZ[j, pl.ds(2 * c, 2)].astype(F32).reshape(TOK, CW)
        bufC[j] = accP[j, oc, zh] + RZ[j, pl.ds(2 * oc, 2)].astype(F32).reshape(TOK, CW)
        post(bufC.at[j], RC.at[j], r_pc + j, other_core)

    def finish_context_grad():
        for m in (1, 2, 3):
            src = lax.rem(zl + m, 4)
            got(RDZ.at[src], r_dz + src)
        total = RDZ[0].astype(F32)
        for m in (1, 2, 3):
            total = total + RDZ[m].astype(F32)
        total = total.astype(BF16).reshape(8, 64, 256)
        cg_ref[...] = jnp.concatenate([total[g][:, :ROWS] for g in range(8)], axis=1)

    to_y(0)
    to_y(1)
    to_z(0)
    to_y(2)
    to_z(1)
    to_c(0)
    to_z(2)
    to_c(1)
    finish_context_grad()
    to_c(2)

    @pl.loop(0, NC)
    def _(j):
        got(RW.at[oc, 0, j], r_wg + 2 * oc * NC + j)
        for w in range(2):
            got(RW.at[w, 1, j], r_wg + (2 * w + 1) * NC + j)

    for w in range(2):
        @pl.loop(0, NC)
        def _(j):
            cols = pl.ds(pl.multiple_of(w * SHIFT + j * CW, 128), CW)
            wg_ref[:, cols] = (RW[w, 0, j].astype(F32) + RW[w, 1, j].astype(F32)).astype(BF16)

    for j in range(NC):
        got(RC.at[j], r_pc + j)
    for w in (1, 0):
        for j in range(NC):
            cols = slice(w * SHIFT + j * CW, w * SHIFT + (j + 1) * CW)
            v = jnp.where(c == w, own[j], RC[j])
            upd_ref[:, cols] = (res_ref[:, cols].astype(F32) + v).astype(BF16)

    for cp in sent:
        cp.wait_send()
    for j in range(NC):
        for s in range(3):
            drain(DWs.at[s, j], s_wg + s * NC + j)
    for k in range(4):
        @pl.when(blocks[k] != zl)
        def _():
            drain(TZ.at[k], s_dz + k)


def hand_over(a, b, d, a_out, b_out, d_out):
    a_out[...] = a[...]
    b_out[...] = b[...]
    d_out[...] = d[...]


def per_device(residual, context, proj_weight, out_grad):
    vmem = pl.BlockSpec(memory_space=pltpu.VMEM)
    anywhere = pl.BlockSpec(memory_space=pl.ANY)
    shape = jax.ShapeDtypeStruct
    updated, context_grad, weight_grad = pl.pallas_call(
        kernel,
        out_shape=(
            shape((TOK, D_ROW), BF16),
            shape((64, 8 * ROWS), BF16),
            shape((ROWS, D_ROW), BF16),
        ),
        in_specs=[vmem, anywhere, anywhere, anywhere],
        out_specs=(vmem, vmem, vmem),
        scratch_shapes=[
            pltpu.VMEM((4, ROWS, WIN), BF16),
            pltpu.VMEM((2, 2, 4, 2, TOK, WIN), BF16),
            pltpu.VMEM((4, 4, 4, 64, ROWS), BF16),
            pltpu.VMEM((4, ROWS, 1024), BF16),
            pltpu.VMEM((NC, 2, 2, 64, CW), BF16),
            pltpu.VMEM((NC, 2, 2, 64, CW), BF16),
            pltpu.VMEM((NC, 2, 2, 64, CW), BF16),
            pltpu.VMEM((NC, 2, 2, 64, CW), BF16),
            pltpu.VMEM((NC, 2, 2, 64, CW), BF16),
            pltpu.VMEM((NC, 2, 2, 64, CW), BF16),
            pltpu.VMEM((NC, 2, 2, 4, 64, CW), F32),
            pltpu.VMEM((NC, 2, 2, TOK, CW), F32),
            pltpu.VMEM((NC, 8, 16, CW), BF16),
            pltpu.VMEM((NC, 8, 16, CW), BF16),
            pltpu.VMEM((NC, 4, 16, CW), BF16),
            pltpu.VMEM((NC, 4, 16, CW), BF16),
            pltpu.VMEM((NC, TOK, CW), F32),
            pltpu.VMEM((NC, TOK, CW), F32),
            pltpu.VMEM((NC, TOK, CW), F32),
            pltpu.VMEM((4, 4, 2, 64, 256), BF16),
            pltpu.VMEM((4, 4, 2, 64, 256), BF16),
            pltpu.VMEM((4, 4, 2, 64, 256), BF16),
            pltpu.VMEM((4, 4, 2, 64, 256), BF16),
            pltpu.VMEM((4, 4, 2, 64, 256), BF16),
            pltpu.VMEM((4, 4, 2, 64, 256), BF16),
            pltpu.VMEM((3, NC, ROWS, CW), BF16),
            pltpu.VMEM((2, 2, NC, ROWS, CW), BF16),
            pltpu.SemaphoreType.DMA((N_SEMS,)),
            pltpu.SemaphoreType.DMA((N_SEMS,)),
            pltpu.SemaphoreType.DMA((16,)),
        ],
        compiler_params=pltpu.CompilerParams(
            collective_id=0, has_side_effects=True, vmem_limit_bytes=60 * 2**20
        ),
        cost_estimate=pl.CostEstimate(
            flops=6 * 1024 * 928 * WIN, bytes_accessed=8 * 2**20, transcendentals=0
        ),
    )(residual, context.T.reshape(8, ROWS, 256), proj_weight[0], out_grad)
    updated, context_grad, weight_grad = pl.pallas_call(
        hand_over,
        out_shape=(
            shape((TOK, D_ROW), BF16),
            shape((64, 8 * ROWS), BF16),
            shape((ROWS, D_ROW), BF16),
        ),
        in_specs=[vmem] * 3,
        out_specs=(vmem,) * 3,
    )(updated, context_grad, weight_grad)
    return updated, context_grad, weight_grad[None]


def solution(mesh):
    in_specs = (P(("ia", "wa"), "ao"), P("ia", "wa"), P("wa", "ia", "ao"), P(("ia", "wa"), "ao"))
    out_specs = (P(("ia", "wa"), "ao"), P(("ia", "ao"), "wa"), P("wa", "ia", "ao"))
    return jax.shard_map(
        per_device, mesh=mesh, in_specs=in_specs, out_specs=out_specs, check_vma=False
    )
```

```python
import jax
import jax.numpy as jnp
from jax import lax
from jax.experimental import pallas as pl
from jax.experimental.pallas import tpu as pltpu
from jax.sharding import PartitionSpec as P

MESH = pl.DeviceIdType.MESH
BF16 = jnp.bfloat16
F32 = jnp.float32

ROWS = 232
D_ROW = 3712
SHIFT = 1792
WIN = 1920
NC = 3
CW = WIN // NC
PW = (768, 768, 384)
PO = (0, 768, 1536)
TOK = 32


class Sems:
    def __init__(self):
        self.n = 0

    def take(self, count):
        base = self.n
        self.n += count
        return base


N_SEMS = 224


def kernel(
    res_ref, ctx_ref, w_ref, g_ref,
    upd_ref, cg_ref, wg_ref,
    Wb, Gb, Xb, XT,
    bufA, RA, bufB1, bufB2, RB1, RB2, PF, accP,
    bufY, RY, bufZ, RZ, bufC, RC, own,
    OWN, DY, RDY, RDC, TZ, RDZ, RL,
    DWs, RW, WG,
    ss, rs, ls,
):
    ia = lax.axis_index("ia")
    wa = lax.axis_index("wa")
    zl = lax.axis_index("ao")
    y, c = lax.div(ia, 2), lax.rem(ia, 2)
    x, zh = lax.div(wa, 2), lax.rem(wa, 2)
    oc, zn = 1 - c, 1 - zh

    def flip(v):
        return v + 1 - 2 * lax.rem(v, 2)

    ya, yb = flip(y), 3 - y

    def w_pair(yy, cc):
        return (1 - cc) * flip(yy) + cc * (3 - yy)

    def t_pair(yy, cc):
        return cc * flip(yy) + (1 - cc) * (3 - yy)

    wp, tp = w_pair(y, c), t_pair(y, c)
    xp, xm, x2 = lax.rem(x + 1, 4), lax.rem(x + 3, 4), lax.rem(x + 2, 4)

    def dev(yy=y, cc=c, xx=x, hh=zh, ll=zl):
        return (2 * yy + cc, 2 * xx + hh, ll)

    other_core = dev(cc=oc)
    partners = [
        other_core,
        dev(yy=ya, cc=0), dev(yy=ya, cc=1), dev(yy=yb, cc=0), dev(yy=yb, cc=1),
        dev(xx=xp), dev(xx=xm),
        dev(hh=zn), dev(hh=zn, cc=oc),
    ] + [dev(ll=lax.rem(zl + m, 4)) for m in (1, 2, 3)]

    middle = lax.rem(zl, 3) != 0
    far = 3 * (1 - lax.rem(zl + 1, 2))

    @pl.when(jnp.logical_not(middle))
    def _():
        RDZ[3 - zl] = jnp.zeros((4, 2, 64, 256), BF16)

    barrier = pltpu.get_barrier_semaphore()
    for p in partners:
        pl.semaphore_signal(barrier, inc=1, device_id=p, device_id_type=MESH)
    pl.semaphore_wait(barrier, len(partners))

    s_idx, r_idx, l_idx = Sems(), Sems(), Sems()
    sent = []

    def send(src, dst, r, to, s=None):
        if s is None:
            s = s_idx.take(1)
        cp = pltpu.make_async_remote_copy(
            src_ref=src, dst_ref=dst, send_sem=ss.at[s], recv_sem=rs.at[r],
            device_id=to, device_id_type=MESH,
        )
        cp.start()
        return cp

    def post(*args):
        sent.append(send(*args))

    def got(dst, r):
        pltpu.make_async_remote_copy(
            src_ref=dst, dst_ref=dst, send_sem=ss.at[0], recv_sem=rs.at[r],
            device_id=other_core, device_id_type=MESH,
        ).wait_recv()

    def local(src, dst):
        cp = pltpu.make_async_copy(src, dst, ls.at[l_idx.take(1)])
        cp.start()
        return cp

    def window(cc):
        return pl.ds(pl.multiple_of(cc * SHIFT, 128), WIN)

    r_g0 = r_idx.take(2)
    r_g1 = r_idx.take(2)
    g_own = g_ref.at[:, window(c)]
    g_oth = g_ref.at[:, window(oc)]
    g_local = local(g_own, Gb.at[0, c, x, zh])
    post(g_oth, Gb.at[0, c, x, zh], r_g0 + c, other_core)
    post(g_own, Gb.at[0, c, x, zh], r_g1 + c, dev(hh=zn))
    post(g_oth, Gb.at[0, c, x, zh], r_g1 + c, dev(hh=zn, cc=oc))

    r_w = r_idx.take(4 * NC)

    def w_cols(cc, j):
        return pl.ds(pl.multiple_of(cc * SHIFT + PO[j], 128), PW[j])

    def send_w(j):
        cols = pl.ds(PO[j], PW[j])
        for cc, yy in ((0, ya), (1, yb)):
            post(w_ref.at[:, w_cols(cc, j)], Wb.at[2 + c, :, cols],
                 r_w + (2 + c) * NC + j, dev(yy=yy, cc=cc))

    r_y = r_idx.take(2)
    r_xp = r_idx.take(4)
    r_xm = r_idx.take(4)
    r_f = r_idx.take(4)

    def unit(p, xx, h):
        return Gb.at[p, :, xx, h]

    def to_x(p, k, h):
        post(unit(p, x, h), unit(p, x, h), r_xp + 2 * p + k, dev(xx=xp))
        post(unit(p, x, h), unit(p, x, h), r_xm + 2 * p + k, dev(xx=xm))

    def forward_up(k, h):
        got(unit(0, xm, h), r_xp + k)
        post(unit(0, xm, h), unit(0, xm, h), r_f + k, dev(xx=xp))

    def forward_down(k, h):
        got(unit(1, xp, h), r_xm + 2 + k)
        post(unit(1, xp, h), unit(1, xp, h), r_f + 2 + k, dev(xx=xm))

    def to_partner(k, h):
        post(unit(0, x, h), unit(1, x, h), r_y + k, dev(yy=tp))

    def from_partner(k, h):
        got(unit(1, x, h), r_y + k)

    g_local.wait()
    got(Gb.at[0, oc, x, zh], r_g0 + oc)
    to_partner(0, zh)
    to_x(0, 0, zh)

    r_c = r_idx.take(8)
    half = lax.rem(zl, 2)

    def x_block(q, blk):
        return XT.at[pl.ds(2 * q, 2), :, pl.ds(pl.multiple_of(blk * 256, 256), 256)]

    def x_group(q, yy, cc):
        chip = (1 - q) * yy + q * w_pair(yy, cc)
        return ctx_ref.at[pl.ds(2 * chip, 2)]

    def got_x(q, blk):
        got(x_block(q, blk), r_c + 2 * blk + q)

    def transpose_x(s, blk):
        t = XT[s, :, blk * 256:(blk + 1) * 256].T
        Xb[s, blk] = t.reshape(4, 64, ROWS)

    for y_to, cc in ((yb, 0), (ya, 1)):
        post(x_group(half, y_to, cc), x_block(half, 2 + c), r_c + 2 * (2 + c) + half, dev(yy=y_to, cc=cc))
    x_locals = []
    for q in range(2):
        x_locals.append(local(x_group(q, y, c), x_block(q, c)))
        post(x_group(q, y, oc), x_block(q, c), r_c + 2 * c + q, other_core)

    w_locals = []
    for j in range(NC):
        cols = pl.ds(PO[j], PW[j])
        w_locals.append(local(w_ref.at[:, w_cols(c, j)], Wb.at[c, :, cols]))
        post(w_ref.at[:, w_cols(oc, j)], Wb.at[c, :, cols], r_w + c * NC + j, other_core)


    from_partner(0, zh)
    to_x(1, 0, zh)
    send_w(0)
    forward_up(0, zh)
    for cp in x_locals:
        cp.wait()
    for q in range(2):
        got_x(q, oc)
    for blk in range(2):
        for sl in range(4):
            transpose_x(sl, blk)
    for blk in (2, 3):
        got_x(half, blk)
        post(x_block(half, blk), x_block(half, blk), r_c + 2 * blk + half, dev(ll=flip(zl)))
    for blk in (2, 3):
        for sl in range(2):
            transpose_x(2 * half + sl, blk)
    forward_down(0, zh)

    for core in range(2):
        got(Gb.at[0, core, x, zn], r_g1 + core)
    to_partner(1, zn)
    to_x(0, 1, zn)
    send_w(1)
    send_w(2)
    from_partner(1, zn)
    to_x(1, 1, zn)

    for blk in (2, 3):
        got_x(1 - half, blk)
        for sl in range(2):
            transpose_x(2 * (1 - half) + sl, blk)
    for cp in w_locals:
        cp.wait()
    for j in range(NC):
        got(Wb.at[oc, :, pl.ds(PO[j], PW[j])], r_w + oc * NC + j)

    def project(j):
        @pl.loop(0, 4)
        def _(blk):
            total = None
            for sl in range(4):
                a = Xb[sl, blk].reshape(256, ROWS)
                part = jnp.dot(a, Wb[sl, :, PO[j]:PO[j] + PW[j]], preferred_element_type=F32)
                total = part if total is None else total + part
            PF[j][blk] = total.reshape(4, 64, PW[j])

    r_a = r_idx.take(2 * NC)
    r_b1 = r_idx.take(2 * NC)
    r_b2 = r_idx.take(2 * NC)
    to_xp, to_xm = dev(xx=xp), dev(xx=xm)

    def drain(src, s):
        pltpu.make_async_remote_copy(
            src_ref=src, dst_ref=src, send_sem=ss.at[s], recv_sem=rs.at[0],
            device_id=other_core, device_id_type=MESH,
        ).wait_send()

    def got_w(j):
        cols = pl.ds(PO[j], PW[j])
        for s in (2, 3):
            got(Wb.at[s, :, cols], r_w + s * NC + j)
        if j == 0:
            keep = (c == 0).astype(BF16)
            for s in range(4):
                Wb[s, :, 0:128] = Wb[s, :, 0:128] * keep

    def project_chunk(j):
        got_w(j)
        project(j)

    def post_a(j):
        bufA[j][...] = PF[j][:, x2].astype(BF16).reshape(2, 2, 64, PW[j])
        post(bufA[j].at[0], RA[j].at[0], r_a + 2 * j, to_xp)
        post(bufA[j].at[1], RA[j].at[1], r_a + 2 * j + 1, to_xm)

    def post_b(j):
        bufB1[j][1] = PF[j][2:4, xp].astype(BF16)
        post(bufB1[j].at[1], RB1[j].at[1], r_b1 + 2 * j + 1, to_xp)
        bufB2[j][0] = PF[j][0:2, xm].astype(BF16)
        post(bufB2[j].at[0], RB2[j].at[0], r_b2 + 2 * j, to_xm)

    def pass_on(j):
        got(RA[j].at[0], r_a + 2 * j)
        bufB1[j][0] = (PF[j][0:2, xp] + RA[j][0].astype(F32)).astype(BF16)
        post(bufB1[j].at[0], RB1[j].at[0], r_b1 + 2 * j, to_xp)
        got(RA[j].at[1], r_a + 2 * j + 1)
        bufB2[j][1] = (PF[j][2:4, xm] + RA[j][1].astype(F32)).astype(BF16)
        post(bufB2[j].at[1], RB2[j].at[1], r_b2 + 2 * j + 1, to_xm)

    r_dy, r_dc, r_dz = r_idx.take(4), r_idx.take(16), r_idx.take(4)
    r_rl = r_idx.take(1)
    s_dz = s_idx.take(5)
    blocks = (x, xp, xm, x2)

    def back(k, first=0, last=4):
        d = blocks[k]

        @pl.loop(first, last)
        def _(s):
            g = Gb[:, :, d].reshape(256, WIN)
            t = lax.dot_general(g, Wb[s], (((1,), (1,)), ((), ())),
                                preferred_element_type=F32).astype(BF16)
            t = jnp.concatenate([t, jnp.zeros((256, 256 - ROWS), BF16)], axis=1)
            t = t.reshape(2, 2, 64, 256)
            OWN[k, s] = t[0]
            DY[k, s] = t[1]

        if last == 4:
            post(DY.at[k], RDY.at[k], r_dy + k, dev(yy=tp))

    r_wg = r_idx.take(4 * NC)
    s_wg = s_idx.take(3 * NC)

    def grad(s, j):
        cols = pl.ds(pl.multiple_of(j * CW, 128), CW)
        b = Gb[:, :, :, :, :, cols].reshape(1024, CW)
        return jnp.dot(XT[s], b, preferred_element_type=F32).astype(BF16)

    own_groups = (y, wp)
    got_groups = (tp, w_pair(tp, c))

    def to_core(k):
        got(RDY.at[k], r_dy + k)
        for q in range(2):
            for part, group in ((OWN, own_groups[q]), (RDY, got_groups[q])):
                post(part.at[k, pl.ds(2 * q, 2), oc], RDC.at[k, group],
                     r_dc + 4 * k + group, other_core)

    def to_ao(k):
        d = blocks[k]
        for group in range(4):
            got(RDC.at[k, group], r_dc + 4 * k + group)
        for q in range(2):
            for part, group in ((OWN, own_groups[q]), (RDY, got_groups[q])):
                TZ[d, group] = (part[k, 2 * q:2 * q + 2, c].astype(F32)
                                + RDC[k, group].astype(F32)).astype(BF16)

        relay = jnp.logical_and(jnp.logical_not(middle), d == 3 - zl)
        held = jnp.logical_and(middle, d == far)

        @pl.when(relay)
        def _():
            send(TZ.at[d], RL, r_rl, dev(ll=1 + lax.div(zl, 3)), s_dz + k)

        @pl.when(jnp.logical_not(jnp.logical_or(relay, jnp.logical_or(held, d == zl))))
        def _():
            send(TZ.at[d], RDZ.at[zl], r_dz + zl, dev(ll=d), s_dz + k)

        @pl.when(d == zl)
        def _():
            RDZ[zl] = TZ[d]

    def relay_on():
        @pl.when(middle)
        def _():
            got(RL, r_rl)
            TZ[far] = (TZ[far].astype(F32) + RL[...].astype(F32)).astype(BF16)
            send(TZ.at[far], RDZ.at[zl], r_dz + zl, dev(ll=far), s_dz + 4)

    def grad_other(core):
        to = dev(yy=wp, cc=core)

        @pl.loop(0, NC)
        def _(j):
            DWs[core, j] = grad(2 + core, j)
            send(DWs.at[core, j], RW.at[c, 1, j], r_wg + (2 * c + 1) * NC + j, to, s_wg + core * NC + j)

    def grad_core():
        @pl.loop(0, NC)
        def _(j):
            DWs[2, j] = grad(oc, j)
            send(DWs.at[2, j], RW.at[c, 0, j], r_wg + 2 * c * NC + j, other_core, s_wg + 2 * NC + j)

    def grad_own():
        @pl.loop(0, NC)
        def _(j):
            RW[c, 0, j] = grad(c, j)

    project_chunk(0)
    forward_up(1, zn)
    post_a(0)
    back(0, 0, 2)
    forward_down(1, zn)
    post_b(0)
    project_chunk(1)
    post_a(1)
    got_w(2)
    back(0, 2, 4)
    for h, k in ((zh, 0), (zn, 1)):
        got(unit(1, xm, h), r_xp + 2 + k)
        got(unit(0, xp, h), r_xm + k)
    back(1)
    back(2)
    pass_on(0)
    post_b(1)
    to_core(0)
    for k, h in ((0, zh), (1, zn)):
        got(unit(0, x2, h), r_f + k)
        got(unit(1, x2, h), r_f + 2 + k)
    back(3)
    to_ao(0)
    to_core(1)
    grad_other(0)
    to_ao(1)
    to_core(2)
    project(2)
    post_a(2)
    pass_on(1)
    to_ao(2)
    to_core(3)
    grad_other(1)
    post_b(2)
    to_ao(3)

    r_py, r_pz, r_pc = r_idx.take(NC), r_idx.take(NC), r_idx.take(NC)

    def to_y(j):
        got(RB1[j].at[1], r_b1 + 2 * j + 1)
        got(RB2[j].at[1], r_b2 + 2 * j + 1)
        v = PF[j][2:4, x] + RB1[j][1].astype(F32) + RB2[j][1].astype(F32)
        bufY[j][...] = v.astype(BF16).reshape(2, 2, TOK, PW[j])
        post(bufY[j], RY[j], r_py + j, dev(yy=tp))

    def to_z(j):
        got(RB1[j].at[0], r_b1 + 2 * j)
        got(RB2[j].at[0], r_b2 + 2 * j)
        v = PF[j][0:2, x] + RB1[j][0].astype(F32) + RB2[j][0].astype(F32)
        got(RY[j], r_py + j)
        v = v.reshape(2, 2, TOK, PW[j]) + RY[j][...].astype(F32)
        accP[j][...] = v
        bufZ[j][...] = accP[j][:, zn].astype(BF16)
        post(bufZ[j], RZ[j], r_pz + j, dev(hh=zn))

    def to_c(j):
        got(RZ[j], r_pz + j)
        own[j][...] = accP[j][c, zh] + RZ[j][c].astype(F32)
        bufC[j][...] = accP[j][oc, zh] + RZ[j][oc].astype(F32)
        post(bufC[j], RC[j], r_pc + j, other_core)

    def finish_weight_grad():
        @pl.loop(0, NC)
        def _(j):
            got(RW.at[oc, 0, j], r_wg + 2 * oc * NC + j)
            for w in range(2):
                got(RW.at[w, 1, j], r_wg + (2 * w + 1) * NC + j)

        for w in range(2):
            @pl.loop(0, NC)
            def _(j):
                cols = pl.ds(pl.multiple_of(w * SHIFT + j * CW, 128), CW)
                WG[:, cols] = (RW[w, 0, j].astype(F32) + RW[w, 1, j].astype(F32)).astype(BF16)

        return local(WG, wg_ref)

    def finish_context_grad():
        for m in (1, 2, 3):
            src = lax.rem(zl + m, 4)

            @pl.when(jnp.logical_or(middle, src != 3 - zl))
            def _():
                got(RDZ.at[src], r_dz + src)

        total = RDZ[0].astype(F32)
        for m in (1, 2, 3):
            total = total + RDZ[m].astype(F32)
        total = total.astype(BF16).reshape(8, 64, 256)
        cg_ref[...] = jnp.concatenate([total[g][:, :ROWS] for g in range(8)], axis=1)

    to_y(0)
    grad_core()
    pass_on(2)
    relay_on()
    to_z(0)
    to_y(1)
    grad_own()
    to_y(2)
    to_z(1)
    to_z(2)
    wg_out = finish_weight_grad()
    to_c(0)
    to_c(1)
    finish_context_grad()
    to_c(2)

    for j in range(NC):
        got(RC[j], r_pc + j)
    for w in (1, 0):
        for j in range(NC):
            cols = slice(w * SHIFT + PO[j], w * SHIFT + PO[j] + PW[j])
            v = jnp.where(c == w, own[j][...], RC[j][...])
            upd_ref[:, cols] = (res_ref[:, cols].astype(F32) + v).astype(BF16)

    wg_out.wait()
    for cp in sent:
        cp.wait_send()
    for j in range(NC):
        for s in range(3):
            drain(DWs.at[s, j], s_wg + s * NC + j)
    for k in range(4):
        d = blocks[k]

        @pl.when(jnp.logical_not(jnp.logical_or(d == zl, jnp.logical_and(middle, d == far))))
        def _():
            drain(TZ.at[d], s_dz + k)

    @pl.when(middle)
    def _():
        drain(TZ.at[far], s_dz + 4)


def hand_over(a, b, d, a_out, b_out, d_out):
    a_out[...] = a[...]
    b_out[...] = b[...]
    d_out[...] = d[...]


def per_device(residual, context, proj_weight, out_grad):
    vmem = pl.BlockSpec(memory_space=pltpu.VMEM)
    anywhere = pl.BlockSpec(memory_space=pl.ANY)
    shape = jax.ShapeDtypeStruct
    updated, context_grad, weight_grad = pl.pallas_call(
        kernel,
        out_shape=(
            shape((TOK, D_ROW), BF16),
            shape((64, 8 * ROWS), BF16),
            shape((ROWS, D_ROW), BF16),
        ),
        in_specs=[vmem, anywhere, anywhere, anywhere],
        out_specs=(vmem, vmem, anywhere),
        scratch_shapes=[
            pltpu.VMEM((4, ROWS, WIN), BF16),
            pltpu.VMEM((2, 2, 4, 2, TOK, WIN), BF16),
            pltpu.VMEM((4, 4, 4, 64, ROWS), BF16),
            pltpu.VMEM((4, ROWS, 1024), BF16),
            [pltpu.VMEM((2, 2, 64, w), BF16) for w in PW],
            [pltpu.VMEM((2, 2, 64, w), BF16) for w in PW],
            [pltpu.VMEM((2, 2, 64, w), BF16) for w in PW],
            [pltpu.VMEM((2, 2, 64, w), BF16) for w in PW],
            [pltpu.VMEM((2, 2, 64, w), BF16) for w in PW],
            [pltpu.VMEM((2, 2, 64, w), BF16) for w in PW],
            [pltpu.VMEM((4, 4, 64, w), F32) for w in PW],
            [pltpu.VMEM((2, 2, TOK, w), F32) for w in PW],
            [pltpu.VMEM((2, 2, TOK, w), BF16) for w in PW],
            [pltpu.VMEM((2, 2, TOK, w), BF16) for w in PW],
            [pltpu.VMEM((2, TOK, w), BF16) for w in PW],
            [pltpu.VMEM((2, TOK, w), BF16) for w in PW],
            [pltpu.VMEM((TOK, w), F32) for w in PW],
            [pltpu.VMEM((TOK, w), F32) for w in PW],
            [pltpu.VMEM((TOK, w), F32) for w in PW],
            pltpu.VMEM((4, 4, 2, 64, 256), BF16),
            pltpu.VMEM((4, 4, 2, 64, 256), BF16),
            pltpu.VMEM((4, 4, 2, 64, 256), BF16),
            pltpu.VMEM((4, 4, 2, 64, 256), BF16),
            pltpu.VMEM((4, 4, 2, 64, 256), BF16),
            pltpu.VMEM((4, 4, 2, 64, 256), BF16),
            pltpu.VMEM((4, 2, 64, 256), BF16),
            pltpu.VMEM((3, NC, ROWS, CW), BF16),
            pltpu.VMEM((2, 2, NC, ROWS, CW), BF16),
            pltpu.VMEM((ROWS, D_ROW), BF16),
            pltpu.SemaphoreType.DMA((N_SEMS,)),
            pltpu.SemaphoreType.DMA((N_SEMS,)),
            pltpu.SemaphoreType.DMA((16,)),
        ],
        compiler_params=pltpu.CompilerParams(
            collective_id=0, has_side_effects=True, vmem_limit_bytes=60 * 2**20
        ),
        cost_estimate=pl.CostEstimate(
            flops=6 * 1024 * 928 * WIN, bytes_accessed=8 * 2**20, transcendentals=0
        ),
    )(residual, context.T.reshape(8, ROWS, 256), proj_weight[0], out_grad)
    updated, context_grad, weight_grad = pl.pallas_call(
        hand_over,
        out_shape=(
            shape((TOK, D_ROW), BF16),
            shape((64, 8 * ROWS), BF16),
            shape((ROWS, D_ROW), BF16),
        ),
        in_specs=[vmem] * 3,
        out_specs=(vmem,) * 3,
    )(updated, context_grad, weight_grad)
    return updated, context_grad, weight_grad[None]


def solution(mesh):
    in_specs = (P(("ia", "wa"), "ao"), P("ia", "wa"), P("wa", "ia", "ao"), P(("ia", "wa"), "ao"))
    out_specs = (P(("ia", "wa"), "ao"), P(("ia", "ao"), "wa"), P("wa", "ia", "ao"))
    return jax.shard_map(
        per_device, mesh=mesh, in_specs=in_specs, out_specs=out_specs, check_vma=False
    )
```

```python
import jax
import jax.numpy as jnp
from jax import lax
from jax.experimental import pallas as pl
from jax.experimental.pallas import tpu as pltpu
from jax.sharding import PartitionSpec as P

MESH = pl.DeviceIdType.MESH
BF16 = jnp.bfloat16
F32 = jnp.float32

ROWS = 232
D_ROW = 3712
SHIFT = 1792
WIN = 1920
NC = 3
CW = WIN // NC
PW = (768, 768, 384)
PO = (0, 768, 1536)
TOK = 32


class Sems:
    def __init__(self):
        self.n = 0

    def take(self, count):
        base = self.n
        self.n += count
        return base


S_SEMS, R_SEMS, L_SEMS = 69, 72, 8


def kernel(
    res_ref, ctx_ref, w_ref, g_ref,
    upd_ref, cg_ref, wg_ref,
    Wb, Gb, Xb, XT,
    bufA, RA, bufB1, bufB2, RB1, RB2, PF, accP,
    bufY, RY, bufZ, RZ, bufC, RC, own,
    OWN, DY, RDY, RDC, TZ, RDZ, RL,
    DWs, RW, WG, CG,
    ss, rs, ls,
):
    ia = lax.axis_index("ia")
    wa = lax.axis_index("wa")
    zl = lax.axis_index("ao")
    y, c = lax.div(ia, 2), lax.rem(ia, 2)
    x, zh = lax.div(wa, 2), lax.rem(wa, 2)
    oc, zn = 1 - c, 1 - zh

    def flip(v):
        return v + 1 - 2 * lax.rem(v, 2)

    ya, yb = flip(y), 3 - y

    def w_pair(yy, cc):
        return (1 - cc) * flip(yy) + cc * (3 - yy)

    def t_pair(yy, cc):
        return cc * flip(yy) + (1 - cc) * (3 - yy)

    wp, tp = w_pair(y, c), t_pair(y, c)
    xp, xm, x2 = lax.rem(x + 1, 4), lax.rem(x + 3, 4), lax.rem(x + 2, 4)

    def dev(yy=y, cc=c, xx=x, hh=zh, ll=zl):
        return (2 * yy + cc, 2 * xx + hh, ll)

    other_core = dev(cc=oc)
    partners = [
        other_core,
        dev(yy=ya, cc=0), dev(yy=ya, cc=1), dev(yy=yb, cc=0), dev(yy=yb, cc=1),
        dev(xx=xp), dev(xx=xm),
        dev(hh=zn), dev(hh=zn, cc=oc),
    ] + [dev(ll=lax.rem(zl + m, 4)) for m in (1, 2, 3)]

    middle = lax.rem(zl, 3) != 0
    far = 3 * (1 - lax.rem(zl + 1, 2))

    @pl.when(jnp.logical_not(middle))
    def _():
        RDZ[3 - zl] = jnp.zeros((4, 2, 64, 256), BF16)

    barrier = pltpu.get_barrier_semaphore()
    for p in partners:
        pl.semaphore_signal(barrier, inc=1, device_id=p, device_id_type=MESH)
    pl.semaphore_wait(barrier, len(partners))

    s_idx, r_idx, l_idx = Sems(), Sems(), Sems()
    sent = []

    def send(src, dst, r, to, s=None):
        if s is None:
            s = s_idx.take(1)
        cp = pltpu.make_async_remote_copy(
            src_ref=src, dst_ref=dst, send_sem=ss.at[s], recv_sem=rs.at[r],
            device_id=to, device_id_type=MESH,
        )
        cp.start()
        return cp

    def post(*args):
        sent.append(send(*args))

    def got(dst, r):
        pltpu.make_async_remote_copy(
            src_ref=dst, dst_ref=dst, send_sem=ss.at[0], recv_sem=rs.at[r],
            device_id=other_core, device_id_type=MESH,
        ).wait_recv()

    def local(src, dst):
        cp = pltpu.make_async_copy(src, dst, ls.at[l_idx.take(1)])
        cp.start()
        return cp

    def window(cc):
        return pl.ds(pl.multiple_of(cc * SHIFT, 128), WIN)

    r_g0 = r_idx.take(1)
    r_g1 = r_idx.take(1)
    g_own = g_ref.at[:, window(c)]
    g_oth = g_ref.at[:, window(oc)]
    g_local = local(g_own, Gb.at[0, c, x, zh])
    post(g_oth, Gb.at[0, c, x, zh], r_g0, other_core)
    post(g_own, Gb.at[0, c, x, zh], r_g1, dev(hh=zn))
    post(g_oth, Gb.at[0, c, x, zh], r_g1, dev(hh=zn, cc=oc))

    r_w = r_idx.take(1 + NC)
    s_w = s_idx.take(3)

    def w_cols(cc, j):
        return pl.ds(pl.multiple_of(cc * SHIFT + PO[j], 128), PW[j])

    def send_w(j):
        cols = pl.ds(PO[j], PW[j])
        for cc, yy in ((0, ya), (1, yb)):
            send(w_ref.at[:, w_cols(cc, j)], Wb.at[2 + c, :, cols],
                 r_w + 1 + j, dev(yy=yy, cc=cc), s_w + 1 + cc)

    r_y = r_idx.take(2)
    r_xp = r_idx.take(4)
    r_xm = r_idx.take(4)
    r_f = r_idx.take(4)

    def unit(p, xx, h):
        return Gb.at[p, :, xx, h]

    def to_x(p, k, h):
        post(unit(p, x, h), unit(p, x, h), r_xp + 2 * p + k, dev(xx=xp))
        post(unit(p, x, h), unit(p, x, h), r_xm + 2 * p + k, dev(xx=xm))

    def forward_up(k, h):
        got(unit(0, xm, h), r_xp + k)
        post(unit(0, xm, h), unit(0, xm, h), r_f + k, dev(xx=xp))

    def forward_down(k, h):
        got(unit(1, xp, h), r_xm + 2 + k)
        post(unit(1, xp, h), unit(1, xp, h), r_f + 2 + k, dev(xx=xm))

    def to_partner(k, h):
        post(unit(0, x, h), unit(1, x, h), r_y + k, dev(yy=tp))

    def from_partner(k, h):
        got(unit(1, x, h), r_y + k)

    g_local.wait()
    got(Gb.at[0, oc, x, zh], r_g0)
    to_partner(0, zh)
    to_x(0, 0, zh)

    r_c = r_idx.take(8)
    half = lax.rem(zl, 2)

    def x_block(q, blk):
        return XT.at[pl.ds(2 * q, 2), :, pl.ds(pl.multiple_of(blk * 256, 256), 256)]

    def x_group(q, yy, cc):
        chip = (1 - q) * yy + q * w_pair(yy, cc)
        return ctx_ref.at[pl.ds(2 * chip, 2)]

    def got_x(q, blk):
        got(x_block(q, blk), r_c + 2 * blk + q)

    def transpose_x(s, blk):
        t = XT[s, :, blk * 256:(blk + 1) * 256].T
        Xb[s, blk] = t.reshape(4, 64, ROWS)

    for y_to, cc in ((yb, 0), (ya, 1)):
        post(x_group(half, y_to, cc), x_block(half, 2 + c), r_c + 2 * (2 + c) + half, dev(yy=y_to, cc=cc))
    x_locals = []
    for q in range(2):
        x_locals.append(local(x_group(q, y, c), x_block(q, c)))
        post(x_group(q, y, oc), x_block(q, c), r_c + 2 * c + q, other_core)

    w_locals = []
    for j in range(NC):
        cols = pl.ds(PO[j], PW[j])
        w_locals.append(local(w_ref.at[:, w_cols(c, j)], Wb.at[c, :, cols]))
        send(w_ref.at[:, w_cols(oc, j)], Wb.at[c, :, cols], r_w, other_core, s_w)


    from_partner(0, zh)
    to_x(1, 0, zh)
    send_w(0)
    forward_up(0, zh)
    for cp in x_locals:
        cp.wait()
    for q in range(2):
        got_x(q, oc)
    for blk in range(2):
        for sl in range(4):
            transpose_x(sl, blk)
    for blk in (2, 3):
        got_x(half, blk)
        post(x_block(half, blk), x_block(half, blk), r_c + 2 * blk + half, dev(ll=flip(zl)))
    for blk in (2, 3):
        for sl in range(2):
            transpose_x(2 * half + sl, blk)
    forward_down(0, zh)

    got(unit(0, x, zn), r_g1)
    to_partner(1, zn)
    to_x(0, 1, zn)
    send_w(1)
    send_w(2)
    from_partner(1, zn)
    to_x(1, 1, zn)

    for blk in (2, 3):
        got_x(1 - half, blk)
        for sl in range(2):
            transpose_x(2 * (1 - half) + sl, blk)
    for cp in w_locals:
        cp.wait()
    got(Wb.at[oc], r_w)

    def project(j):
        @pl.loop(0, 4)
        def _(blk):
            total = None
            for sl in range(4):
                a = Xb[sl, blk].reshape(256, ROWS)
                part = jnp.dot(a, Wb[sl, :, PO[j]:PO[j] + PW[j]], preferred_element_type=F32)
                total = part if total is None else total + part
            PF[j][blk] = total.reshape(4, 64, PW[j])

    r_a = r_idx.take(2 * NC)
    r_b1 = r_idx.take(2 * NC)
    r_b2 = r_idx.take(2 * NC)
    to_xp, to_xm = dev(xx=xp), dev(xx=xm)

    def drain(src, s):
        pltpu.make_async_remote_copy(
            src_ref=src, dst_ref=src, send_sem=ss.at[s], recv_sem=rs.at[0],
            device_id=other_core, device_id_type=MESH,
        ).wait_send()

    def got_w(j):
        cols = pl.ds(PO[j], PW[j])
        got(Wb.at[2:4, :, cols], r_w + 1 + j)
        if j == 0:
            keep = (c == 0).astype(BF16)
            for s in range(4):
                Wb[s, :, 0:128] = Wb[s, :, 0:128] * keep

    def project_chunk(j):
        got_w(j)
        project(j)

    def post_a(j):
        bufA[j][...] = PF[j][:, x2].astype(BF16).reshape(2, 2, 64, PW[j])
        post(bufA[j].at[0], RA[j].at[0], r_a + 2 * j, to_xp)
        post(bufA[j].at[1], RA[j].at[1], r_a + 2 * j + 1, to_xm)

    def post_b(j):
        bufB1[j][1] = PF[j][2:4, xp].astype(BF16)
        post(bufB1[j].at[1], RB1[j].at[1], r_b1 + 2 * j + 1, to_xp)
        bufB2[j][0] = PF[j][0:2, xm].astype(BF16)
        post(bufB2[j].at[0], RB2[j].at[0], r_b2 + 2 * j, to_xm)

    def pass_on(j):
        got(RA[j].at[0], r_a + 2 * j)
        bufB1[j][0] = (PF[j][0:2, xp] + RA[j][0].astype(F32)).astype(BF16)
        post(bufB1[j].at[0], RB1[j].at[0], r_b1 + 2 * j, to_xp)
        got(RA[j].at[1], r_a + 2 * j + 1)
        bufB2[j][1] = (PF[j][2:4, xm] + RA[j][1].astype(F32)).astype(BF16)
        post(bufB2[j].at[1], RB2[j].at[1], r_b2 + 2 * j + 1, to_xm)

    r_dy, r_dc, r_dz = r_idx.take(4), r_idx.take(4), r_idx.take(4)
    s_dc = s_idx.take(4)
    r_rl = r_idx.take(1)
    s_dz = s_idx.take(5)
    blocks = (x, xp, xm, x2)

    def back(k, first=0, last=4):
        d = blocks[k]

        @pl.loop(first, last)
        def _(s):
            g = Gb[:, :, d].reshape(256, WIN)
            t = lax.dot_general(g, Wb[s], (((1,), (1,)), ((), ())),
                                preferred_element_type=F32).astype(BF16)
            t = jnp.concatenate([t, jnp.zeros((256, 256 - ROWS), BF16)], axis=1)
            t = t.reshape(2, 2, 64, 256)
            OWN[k, s] = t[0]
            DY[k, s] = t[1]

        if last == 4:
            post(DY.at[k], RDY.at[k], r_dy + k, dev(yy=tp))

    r_wg = r_idx.take(4)
    s_wg = s_idx.take(3)

    def grad(s, j):
        cols = pl.ds(pl.multiple_of(j * CW, 128), CW)
        b = Gb[:, :, :, :, :, cols].reshape(1024, CW)
        return jnp.dot(XT[s], b, preferred_element_type=F32).astype(BF16)

    own_groups = (y, wp)
    got_groups = (tp, w_pair(tp, c))

    def to_core(k):
        got(RDY.at[k], r_dy + k)
        for q in range(2):
            for part, group in ((OWN, own_groups[q]), (RDY, got_groups[q])):
                send(part.at[k, pl.ds(2 * q, 2), oc], RDC.at[k, group], r_dc + k, other_core, s_dc + k)

    def to_ao(k):
        d = blocks[k]
        got(RDC.at[k], r_dc + k)
        for q in range(2):
            for part, group in ((OWN, own_groups[q]), (RDY, got_groups[q])):
                TZ[d, group] = (part[k, 2 * q:2 * q + 2, c].astype(F32)
                                + RDC[k, group].astype(F32)).astype(BF16)

        relay = jnp.logical_and(jnp.logical_not(middle), d == 3 - zl)
        held = jnp.logical_and(middle, d == far)

        @pl.when(relay)
        def _():
            send(TZ.at[d], RL, r_rl, dev(ll=1 + lax.div(zl, 3)), s_dz + k)

        @pl.when(jnp.logical_not(jnp.logical_or(relay, jnp.logical_or(held, d == zl))))
        def _():
            send(TZ.at[d], RDZ.at[zl], r_dz + zl, dev(ll=d), s_dz + k)

        @pl.when(d == zl)
        def _():
            RDZ[zl] = TZ[d]

    def relay_on(when):
        @pl.when(jnp.logical_and(middle, when))
        def _():
            got(RL, r_rl)
            TZ[far] = (TZ[far].astype(F32) + RL[...].astype(F32)).astype(BF16)
            send(TZ.at[far], RDZ.at[zl], r_dz + zl, dev(ll=far), s_dz + 4)

    def grad_other(core):
        to = dev(yy=wp, cc=core)

        @pl.loop(0, NC)
        def _(j):
            DWs[core, j] = grad(2 + core, j)
            send(DWs.at[core, j], RW.at[c, 1, j], r_wg + 2 * c + 1, to, s_wg + core)

    def grad_core():
        @pl.loop(0, NC)
        def _(j):
            DWs[2, j] = grad(oc, j)
            send(DWs.at[2, j], RW.at[c, 0, j], r_wg + 2 * c, other_core, s_wg + 2)

    def grad_own():
        @pl.loop(0, NC)
        def _(j):
            RW[c, 0, j] = grad(c, j)

    project_chunk(0)
    forward_up(1, zn)
    post_a(0)
    back(0, 0, 2)
    forward_down(1, zn)
    post_b(0)
    project_chunk(1)
    post_a(1)
    got_w(2)
    back(0, 2, 4)
    for h, k in ((zh, 0), (zn, 1)):
        got(unit(1, xm, h), r_xp + 2 + k)
        got(unit(0, xp, h), r_xm + k)
    back(1)
    back(2)
    pass_on(0)
    post_b(1)
    to_core(0)
    for k, h in ((0, zh), (1, zn)):
        got(unit(0, x2, h), r_f + k)
        got(unit(1, x2, h), r_f + 2 + k)
    back(3)
    to_ao(0)
    to_core(1)
    grad_other(0)
    to_ao(1)
    to_core(2)
    project(2)
    post_a(2)
    pass_on(1)
    to_ao(2)
    to_core(3)
    relay_on(jnp.logical_or(far == x, far == xp))
    grad_other(1)
    post_b(2)
    to_ao(3)

    r_py, r_pz, r_pc = r_idx.take(NC), r_idx.take(NC), r_idx.take(NC)

    def to_y(j):
        got(RB1[j].at[1], r_b1 + 2 * j + 1)
        got(RB2[j].at[1], r_b2 + 2 * j + 1)
        v = PF[j][2:4, x] + RB1[j][1].astype(F32) + RB2[j][1].astype(F32)
        bufY[j][...] = v.astype(BF16).reshape(2, 2, TOK, PW[j])
        post(bufY[j], RY[j], r_py + j, dev(yy=tp))

    def to_z(j):
        got(RB1[j].at[0], r_b1 + 2 * j)
        got(RB2[j].at[0], r_b2 + 2 * j)
        v = PF[j][0:2, x] + RB1[j][0].astype(F32) + RB2[j][0].astype(F32)
        got(RY[j], r_py + j)
        v = v.reshape(2, 2, TOK, PW[j]) + RY[j][...].astype(F32)
        accP[j][...] = v
        bufZ[j][...] = accP[j][:, zn].astype(BF16)
        post(bufZ[j], RZ[j], r_pz + j, dev(hh=zn))

    def to_c(j):
        got(RZ[j], r_pz + j)
        own[j][...] = accP[j][c, zh] + RZ[j][c].astype(F32)
        bufC[j][...] = accP[j][oc, zh] + RZ[j][oc].astype(F32)
        post(bufC[j], RC[j], r_pc + j, other_core)

    def finish_weight_grad():
        got(RW.at[oc, 0], r_wg + 2 * oc)
        for w in range(2):
            got(RW.at[w, 1], r_wg + 2 * w + 1)

        for w in range(2):
            @pl.loop(0, NC)
            def _(j):
                cols = pl.ds(pl.multiple_of(w * SHIFT + j * CW, 128), CW)
                WG[:, cols] = (RW[w, 0, j].astype(F32) + RW[w, 1, j].astype(F32)).astype(BF16)

        return local(WG, wg_ref)

    def finish_context_grad():
        for m in (1, 2, 3):
            src = lax.rem(zl + m, 4)

            @pl.when(jnp.logical_or(middle, src != 3 - zl))
            def _():
                got(RDZ.at[src], r_dz + src)

        total = RDZ[0].astype(F32)
        for m in (1, 2, 3):
            total = total + RDZ[m].astype(F32)
        total = total.astype(BF16).reshape(8, 64, 256)
        CG[...] = jnp.concatenate([total[g][:, :ROWS] for g in range(8)], axis=1)
        return local(CG, cg_ref)

    to_y(0)
    grad_core()
    relay_on(far == xm)
    pass_on(2)
    relay_on(far == x2)
    to_z(0)
    to_y(1)
    grad_own()
    to_y(2)
    to_z(1)
    to_z(2)
    wg_out = finish_weight_grad()
    to_c(0)
    to_c(1)
    cg_out = finish_context_grad()
    to_c(2)

    for j in range(NC):
        got(RC[j], r_pc + j)
    for w in (1, 0):
        for j in range(NC):
            cols = slice(w * SHIFT + PO[j], w * SHIFT + PO[j] + PW[j])
            v = jnp.where(c == w, own[j][...], RC[j][...])
            upd_ref[:, cols] = (res_ref[:, cols].astype(F32) + v).astype(BF16)

    wg_out.wait()
    cg_out.wait()
    for cp in sent:
        cp.wait_send()
    for s in range(3):
        drain(DWs.at[s], s_wg + s)
    for k in range(4):
        drain(RDC.at[k], s_dc + k)
    for to in range(3):
        drain(Wb.at[0], s_w + to)
    for k in range(4):
        d = blocks[k]

        @pl.when(jnp.logical_not(jnp.logical_or(d == zl, jnp.logical_and(middle, d == far))))
        def _():
            drain(TZ.at[d], s_dz + k)

    @pl.when(middle)
    def _():
        drain(TZ.at[far], s_dz + 4)


def hand_over(a, b, d, a_out, b_out, d_out, va, vb, vd, sems):
    moves = [(d.at[:, pl.ds(o, n)], vd.at[:, pl.ds(o, n)], d_out.at[:, pl.ds(o, n)])
             for o, n in ((0, 1024), (1024, 1024), (2048, 1024), (3072, 640))]
    moves += [(a, va, a_out), (b, vb, b_out)]
    arrive = [pltpu.make_async_copy(src, mid, sems.at[0, i]) for i, (src, mid, _) in enumerate(moves)]
    leave = [pltpu.make_async_copy(mid, dst, sems.at[1, i]) for i, (_, mid, dst) in enumerate(moves)]
    for cp in arrive:
        cp.start()
    for first, second in zip(arrive, leave):
        first.wait()
        second.start()
    for cp in leave:
        cp.wait()


def per_device(residual, context, proj_weight, out_grad):
    vmem = pl.BlockSpec(memory_space=pltpu.VMEM)
    anywhere = pl.BlockSpec(memory_space=pl.ANY)
    shape = jax.ShapeDtypeStruct
    updated, context_grad, weight_grad = pl.pallas_call(
        kernel,
        out_shape=(
            shape((TOK, D_ROW), BF16),
            shape((64, 8 * ROWS), BF16),
            shape((ROWS, D_ROW), BF16),
        ),
        in_specs=[vmem, anywhere, anywhere, anywhere],
        out_specs=(vmem, anywhere, anywhere),
        scratch_shapes=[
            pltpu.VMEM((4, ROWS, WIN), BF16),
            pltpu.VMEM((2, 2, 4, 2, TOK, WIN), BF16),
            pltpu.VMEM((4, 4, 4, 64, ROWS), BF16),
            pltpu.VMEM((4, ROWS, 1024), BF16),
            [pltpu.VMEM((2, 2, 64, w), BF16) for w in PW],
            [pltpu.VMEM((2, 2, 64, w), BF16) for w in PW],
            [pltpu.VMEM((2, 2, 64, w), BF16) for w in PW],
            [pltpu.VMEM((2, 2, 64, w), BF16) for w in PW],
            [pltpu.VMEM((2, 2, 64, w), BF16) for w in PW],
            [pltpu.VMEM((2, 2, 64, w), BF16) for w in PW],
            [pltpu.VMEM((4, 4, 64, w), F32) for w in PW],
            [pltpu.VMEM((2, 2, TOK, w), F32) for w in PW],
            [pltpu.VMEM((2, 2, TOK, w), BF16) for w in PW],
            [pltpu.VMEM((2, 2, TOK, w), BF16) for w in PW],
            [pltpu.VMEM((2, TOK, w), BF16) for w in PW],
            [pltpu.VMEM((2, TOK, w), BF16) for w in PW],
            [pltpu.VMEM((TOK, w), F32) for w in PW],
            [pltpu.VMEM((TOK, w), F32) for w in PW],
            [pltpu.VMEM((TOK, w), F32) for w in PW],
            pltpu.VMEM((4, 4, 2, 64, 256), BF16),
            pltpu.VMEM((4, 4, 2, 64, 256), BF16),
            pltpu.VMEM((4, 4, 2, 64, 256), BF16),
            pltpu.VMEM((4, 4, 2, 64, 256), BF16),
            pltpu.VMEM((4, 4, 2, 64, 256), BF16),
            pltpu.VMEM((4, 4, 2, 64, 256), BF16),
            pltpu.VMEM((4, 2, 64, 256), BF16),
            pltpu.VMEM((3, NC, ROWS, CW), BF16),
            pltpu.VMEM((2, 2, NC, ROWS, CW), BF16),
            pltpu.VMEM((ROWS, D_ROW), BF16),
            pltpu.VMEM((64, 8 * ROWS), BF16),
            pltpu.SemaphoreType.DMA((S_SEMS,)),
            pltpu.SemaphoreType.DMA((R_SEMS,)),
            pltpu.SemaphoreType.DMA((L_SEMS,)),
        ],
        compiler_params=pltpu.CompilerParams(
            collective_id=0, has_side_effects=True, vmem_limit_bytes=60 * 2**20
        ),
        cost_estimate=pl.CostEstimate(
            flops=6 * 1024 * 928 * WIN, bytes_accessed=8 * 2**20, transcendentals=0
        ),
    )(residual, context.T.reshape(8, ROWS, 256), proj_weight[0], out_grad)
    updated, context_grad, weight_grad = pl.pallas_call(
        hand_over,
        out_shape=(
            shape((TOK, D_ROW), BF16),
            shape((64, 8 * ROWS), BF16),
            shape((ROWS, D_ROW), BF16),
        ),
        in_specs=[anywhere] * 3,
        out_specs=(anywhere,) * 3,
        scratch_shapes=[
            pltpu.VMEM((TOK, D_ROW), BF16),
            pltpu.VMEM((64, 8 * ROWS), BF16),
            pltpu.VMEM((ROWS, D_ROW), BF16),
            pltpu.SemaphoreType.DMA((2, 6)),
        ],
    )(updated, context_grad, weight_grad)
    return updated, context_grad, weight_grad[None]


def solution(mesh):
    in_specs = (P(("ia", "wa"), "ao"), P("ia", "wa"), P("wa", "ia", "ao"), P(("ia", "wa"), "ao"))
    out_specs = (P(("ia", "wa"), "ao"), P(("ia", "ao"), "wa"), P("wa", "ia", "ao"))
    return jax.shard_map(
        per_device, mesh=mesh, in_specs=in_specs, out_specs=out_specs, check_vma=False
    )
```

```python
import jax
import jax.numpy as jnp
from jax import lax
from jax.experimental import pallas as pl
from jax.experimental.pallas import tpu as pltpu
from jax.sharding import PartitionSpec as P

MESH = pl.DeviceIdType.MESH
BF16 = jnp.bfloat16
F32 = jnp.float32

ROWS = 232
D_ROW = 3712
SHIFT = 1792
WIN = 1920
NC = 3
CW = WIN // NC
PW = (768, 768, 384)
PO = (0, 768, 1536)
TOK = 32


class Sems:
    def __init__(self):
        self.n = 0

    def take(self, count):
        base = self.n
        self.n += count
        return base


S_SEMS, R_SEMS, L_SEMS = 69, 72, 8


def kernel(
    res_ref, ctx_ref, w_ref, g_ref,
    upd_ref, cg_ref, wg_ref,
    Wb, Gb, Xb, XT,
    bufA, RA, bufB1, bufB2, RB1, RB2, PF, accP,
    bufY, RY, bufZ, RZ, bufC, RC, own,
    OWN, DY, RDY, RDC, TZ, RDZ, RL,
    DWs, RW, WG, CG,
    ss, rs, ls,
):
    ia = lax.axis_index("ia")
    wa = lax.axis_index("wa")
    zl = lax.axis_index("ao")
    y, c = lax.div(ia, 2), lax.rem(ia, 2)
    x, zh = lax.div(wa, 2), lax.rem(wa, 2)
    oc, zn = 1 - c, 1 - zh

    def flip(v):
        return v + 1 - 2 * lax.rem(v, 2)

    ya, yb = flip(y), 3 - y

    def w_pair(yy, cc):
        return (1 - cc) * flip(yy) + cc * (3 - yy)

    def t_pair(yy, cc):
        return cc * flip(yy) + (1 - cc) * (3 - yy)

    wp, tp = w_pair(y, c), t_pair(y, c)
    xp, xm, x2 = lax.rem(x + 1, 4), lax.rem(x + 3, 4), lax.rem(x + 2, 4)

    def dev(yy=y, cc=c, xx=x, hh=zh, ll=zl):
        return (2 * yy + cc, 2 * xx + hh, ll)

    other_core = dev(cc=oc)
    partners = [
        other_core,
        dev(yy=ya, cc=0), dev(yy=ya, cc=1), dev(yy=yb, cc=0), dev(yy=yb, cc=1),
        dev(xx=xp), dev(xx=xm),
        dev(hh=zn), dev(hh=zn, cc=oc),
    ] + [dev(ll=lax.rem(zl + m, 4)) for m in (1, 2, 3)]

    middle = lax.rem(zl, 3) != 0
    far = 3 * (1 - lax.rem(zl + 1, 2))

    @pl.when(jnp.logical_not(middle))
    def _():
        RDZ[3 - zl] = jnp.zeros((4, 2, 64, 256), BF16)

    barrier = pltpu.get_barrier_semaphore()
    for p in partners:
        pl.semaphore_signal(barrier, inc=1, device_id=p, device_id_type=MESH)
    pl.semaphore_wait(barrier, len(partners))

    s_idx, r_idx, l_idx = Sems(), Sems(), Sems()
    sent = []

    def send(src, dst, r, to, s=None):
        if s is None:
            s = s_idx.take(1)
        cp = pltpu.make_async_remote_copy(
            src_ref=src, dst_ref=dst, send_sem=ss.at[s], recv_sem=rs.at[r],
            device_id=to, device_id_type=MESH,
        )
        cp.start()
        return cp

    def post(*args):
        sent.append(send(*args))

    def got(dst, r):
        pltpu.make_async_remote_copy(
            src_ref=dst, dst_ref=dst, send_sem=ss.at[0], recv_sem=rs.at[r],
            device_id=other_core, device_id_type=MESH,
        ).wait_recv()

    def local(src, dst):
        cp = pltpu.make_async_copy(src, dst, ls.at[l_idx.take(1)])
        cp.start()
        return cp

    def window(cc):
        return pl.ds(pl.multiple_of(cc * SHIFT, 128), WIN)

    r_g0 = r_idx.take(1)
    r_g1 = r_idx.take(1)
    g_own = g_ref.at[:, window(c)]
    g_oth = g_ref.at[:, window(oc)]
    g_local = local(g_own, Gb.at[0, c, x, zh])
    post(g_oth, Gb.at[0, c, x, zh], r_g0, other_core)
    post(g_own, Gb.at[0, c, x, zh], r_g1, dev(hh=zn))
    post(g_oth, Gb.at[0, c, x, zh], r_g1, dev(hh=zn, cc=oc))

    r_w = r_idx.take(1 + NC)
    s_w = s_idx.take(3)

    def w_cols(cc, j):
        return pl.ds(pl.multiple_of(cc * SHIFT + PO[j], 128), PW[j])

    def send_w(j):
        cols = pl.ds(PO[j], PW[j])
        for cc, yy in ((0, ya), (1, yb)):
            send(w_ref.at[:, w_cols(cc, j)], Wb.at[2 + c, :, cols],
                 r_w + 1 + j, dev(yy=yy, cc=cc), s_w + 1 + cc)

    r_y = r_idx.take(2)
    r_xp = r_idx.take(4)
    r_xm = r_idx.take(4)
    r_f = r_idx.take(4)

    def unit(p, xx, h):
        return Gb.at[p, :, xx, h]

    def to_x(p, k, h):
        post(unit(p, x, h), unit(p, x, h), r_xp + 2 * p + k, dev(xx=xp))
        post(unit(p, x, h), unit(p, x, h), r_xm + 2 * p + k, dev(xx=xm))

    def forward_up(k, h):
        got(unit(0, xm, h), r_xp + k)
        post(unit(0, xm, h), unit(0, xm, h), r_f + k, dev(xx=xp))

    def forward_down(k, h):
        got(unit(1, xp, h), r_xm + 2 + k)
        post(unit(1, xp, h), unit(1, xp, h), r_f + 2 + k, dev(xx=xm))

    def to_partner(k, h):
        post(unit(0, x, h), unit(1, x, h), r_y + k, dev(yy=tp))

    def from_partner(k, h):
        got(unit(1, x, h), r_y + k)

    g_local.wait()
    got(Gb.at[0, oc, x, zh], r_g0)
    to_partner(0, zh)
    to_x(0, 0, zh)

    r_c = r_idx.take(8)
    half = lax.rem(zl, 2)

    def x_block(q, blk):
        return XT.at[pl.ds(2 * q, 2), :, pl.ds(pl.multiple_of(blk * 256, 256), 256)]

    def x_group(q, yy, cc):
        chip = (1 - q) * yy + q * w_pair(yy, cc)
        return ctx_ref.at[pl.ds(2 * chip, 2)]

    def got_x(q, blk):
        got(x_block(q, blk), r_c + 2 * blk + q)

    def transpose_x(s, blk):
        t = XT[s, :, blk * 256:(blk + 1) * 256].T
        Xb[s, blk] = t.reshape(4, 64, ROWS)

    def send_context(y_to, cc):
        post(x_group(half, y_to, cc), x_block(half, 2 + c), r_c + 2 * (2 + c) + half, dev(yy=y_to, cc=cc))

    send_context(tp, c)
    x_locals = []
    for q in range(2):
        x_locals.append(local(x_group(q, y, c), x_block(q, c)))
        post(x_group(q, y, oc), x_block(q, c), r_c + 2 * c + q, other_core)

    w_locals = []
    for j in range(NC):
        cols = pl.ds(PO[j], PW[j])
        w_locals.append(local(w_ref.at[:, w_cols(c, j)], Wb.at[c, :, cols]))
        send(w_ref.at[:, w_cols(oc, j)], Wb.at[c, :, cols], r_w, other_core, s_w)


    from_partner(0, zh)
    to_x(1, 0, zh)
    send_context(wp, oc)
    send_w(0)
    forward_up(0, zh)
    for cp in x_locals:
        cp.wait()
    for q in range(2):
        got_x(q, oc)
    for blk in range(2):
        for sl in range(4):
            transpose_x(sl, blk)
    for blk in (2, 3):
        got_x(half, blk)
        post(x_block(half, blk), x_block(half, blk), r_c + 2 * blk + half, dev(ll=flip(zl)))
    for blk in (2, 3):
        for sl in range(2):
            transpose_x(2 * half + sl, blk)
    forward_down(0, zh)

    got(unit(0, x, zn), r_g1)
    to_partner(1, zn)
    to_x(0, 1, zn)
    send_w(1)
    send_w(2)
    from_partner(1, zn)
    to_x(1, 1, zn)

    for blk in (2, 3):
        got_x(1 - half, blk)
        for sl in range(2):
            transpose_x(2 * (1 - half) + sl, blk)
    for cp in w_locals:
        cp.wait()
    got(Wb.at[oc], r_w)

    def project(j):
        @pl.loop(0, 4)
        def _(blk):
            total = None
            for sl in range(4):
                a = Xb[sl, blk].reshape(256, ROWS)
                part = jnp.dot(a, Wb[sl, :, PO[j]:PO[j] + PW[j]], preferred_element_type=F32)
                total = part if total is None else total + part
            PF[j][blk] = total.reshape(4, 64, PW[j])

    r_a = r_idx.take(2 * NC)
    r_b1 = r_idx.take(2 * NC)
    r_b2 = r_idx.take(2 * NC)
    to_xp, to_xm = dev(xx=xp), dev(xx=xm)

    def drain(src, s):
        pltpu.make_async_remote_copy(
            src_ref=src, dst_ref=src, send_sem=ss.at[s], recv_sem=rs.at[0],
            device_id=other_core, device_id_type=MESH,
        ).wait_send()

    def got_w(j):
        cols = pl.ds(PO[j], PW[j])
        got(Wb.at[2:4, :, cols], r_w + 1 + j)
        if j == 0:
            keep = (c == 0).astype(BF16)
            for s in range(4):
                Wb[s, :, 0:128] = Wb[s, :, 0:128] * keep

    def project_chunk(j):
        got_w(j)
        project(j)

    def post_a(j):
        bufA[j][...] = PF[j][:, x2].astype(BF16).reshape(2, 2, 64, PW[j])
        post(bufA[j].at[0], RA[j].at[0], r_a + 2 * j, to_xp)
        post(bufA[j].at[1], RA[j].at[1], r_a + 2 * j + 1, to_xm)

    def post_b(j):
        bufB1[j][1] = PF[j][2:4, xp].astype(BF16)
        post(bufB1[j].at[1], RB1[j].at[1], r_b1 + 2 * j + 1, to_xp)
        bufB2[j][0] = PF[j][0:2, xm].astype(BF16)
        post(bufB2[j].at[0], RB2[j].at[0], r_b2 + 2 * j, to_xm)

    def pass_on(j):
        got(RA[j].at[0], r_a + 2 * j)
        bufB1[j][0] = (PF[j][0:2, xp] + RA[j][0].astype(F32)).astype(BF16)
        post(bufB1[j].at[0], RB1[j].at[0], r_b1 + 2 * j, to_xp)
        got(RA[j].at[1], r_a + 2 * j + 1)
        bufB2[j][1] = (PF[j][2:4, xm] + RA[j][1].astype(F32)).astype(BF16)
        post(bufB2[j].at[1], RB2[j].at[1], r_b2 + 2 * j + 1, to_xm)

    r_dy, r_dc, r_dz = r_idx.take(4), r_idx.take(4), r_idx.take(4)
    s_dc = s_idx.take(4)
    r_rl = r_idx.take(1)
    s_dz = s_idx.take(5)
    edge = 2 * (1 - lax.min(x, 1))
    n1, n2 = lax.rem(x + 1 + edge, 4), lax.rem(x + 3 + edge, 4)
    blocks = (x, n1, n2, x2)

    def back(k, first=0, last=4):
        d = blocks[k]

        @pl.loop(first, last)
        def _(s):
            g = Gb[:, :, d].reshape(256, WIN)
            t = lax.dot_general(g, Wb[s], (((1,), (1,)), ((), ())),
                                preferred_element_type=F32).astype(BF16)
            t = jnp.concatenate([t, jnp.zeros((256, 256 - ROWS), BF16)], axis=1)
            t = t.reshape(2, 2, 64, 256)
            OWN[k, s] = t[0]
            DY[k, s] = t[1]

        if last == 4:
            post(DY.at[k], RDY.at[k], r_dy + k, dev(yy=tp))

    r_wg = r_idx.take(4)
    s_wg = s_idx.take(3)

    def grad(s, j):
        cols = pl.ds(pl.multiple_of(j * CW, 128), CW)
        b = Gb[:, :, :, :, :, cols].reshape(1024, CW)
        return jnp.dot(XT[s], b, preferred_element_type=F32).astype(BF16)

    own_groups = (y, wp)
    got_groups = (tp, w_pair(tp, c))

    def to_core(k):
        got(RDY.at[k], r_dy + k)
        for q in range(2):
            for part, group in ((OWN, own_groups[q]), (RDY, got_groups[q])):
                send(part.at[k, pl.ds(2 * q, 2), oc], RDC.at[k, group], r_dc + k, other_core, s_dc + k)

    def to_ao(k):
        d = blocks[k]
        got(RDC.at[k], r_dc + k)
        for q in range(2):
            for part, group in ((OWN, own_groups[q]), (RDY, got_groups[q])):
                TZ[d, group] = (part[k, 2 * q:2 * q + 2, c].astype(F32)
                                + RDC[k, group].astype(F32)).astype(BF16)

        relay = jnp.logical_and(jnp.logical_not(middle), d == 3 - zl)
        held = jnp.logical_and(middle, d == far)

        @pl.when(relay)
        def _():
            send(TZ.at[d], RL, r_rl, dev(ll=1 + lax.div(zl, 3)), s_dz + k)

        @pl.when(jnp.logical_not(jnp.logical_or(relay, jnp.logical_or(held, d == zl))))
        def _():
            send(TZ.at[d], RDZ.at[zl], r_dz + zl, dev(ll=d), s_dz + k)

        @pl.when(d == zl)
        def _():
            RDZ[zl] = TZ[d]

    def relay_on(when):
        @pl.when(jnp.logical_and(middle, when))
        def _():
            got(RL, r_rl)
            TZ[far] = (TZ[far].astype(F32) + RL[...].astype(F32)).astype(BF16)
            send(TZ.at[far], RDZ.at[zl], r_dz + zl, dev(ll=far), s_dz + 4)

    def grad_other(core):
        to = dev(yy=wp, cc=core)

        @pl.loop(0, NC)
        def _(j):
            DWs[core, j] = grad(2 + core, j)
            send(DWs.at[core, j], RW.at[c, 1, j], r_wg + 2 * c + 1, to, s_wg + core)

    def grad_core():
        @pl.loop(0, NC)
        def _(j):
            DWs[2, j] = grad(oc, j)
            send(DWs.at[2, j], RW.at[c, 0, j], r_wg + 2 * c, other_core, s_wg + 2)

    def grad_own():
        @pl.loop(0, NC)
        def _(j):
            RW[c, 0, j] = grad(c, j)

    project_chunk(0)
    forward_up(1, zn)
    post_a(0)
    back(0, 0, 2)
    forward_down(1, zn)
    post_b(0)
    got_w(1)
    got_w(2)
    back(0, 2, 4)
    for h, k in ((zh, 0), (zn, 1)):
        got(unit(1, xm, h), r_xp + 2 + k)
        got(unit(0, xp, h), r_xm + k)
    back(1)
    project(1)
    post_a(1)
    back(2)
    pass_on(0)
    post_b(1)
    to_core(0)
    for k, h in ((0, zh), (1, zn)):
        got(unit(0, x2, h), r_f + k)
        got(unit(1, x2, h), r_f + 2 + k)
    back(3)
    to_ao(0)
    to_core(1)
    grad_other(0)
    to_ao(1)
    to_core(2)
    grad_other(1)
    to_ao(2)
    pass_on(1)
    to_core(3)
    relay_on(jnp.logical_or(far == x, far == n1))
    project(2)
    post_a(2)
    post_b(2)
    to_ao(3)

    r_py, r_pz, r_pc = r_idx.take(NC), r_idx.take(NC), r_idx.take(NC)

    def to_y(j):
        got(RB1[j].at[1], r_b1 + 2 * j + 1)
        got(RB2[j].at[1], r_b2 + 2 * j + 1)
        v = PF[j][2:4, x] + RB1[j][1].astype(F32) + RB2[j][1].astype(F32)
        bufY[j][...] = v.astype(BF16).reshape(2, 2, TOK, PW[j])
        post(bufY[j], RY[j], r_py + j, dev(yy=tp))

    def to_z(j):
        got(RB1[j].at[0], r_b1 + 2 * j)
        got(RB2[j].at[0], r_b2 + 2 * j)
        v = PF[j][0:2, x] + RB1[j][0].astype(F32) + RB2[j][0].astype(F32)
        got(RY[j], r_py + j)
        v = v.reshape(2, 2, TOK, PW[j]) + RY[j][...].astype(F32)
        accP[j][...] = v
        bufZ[j][...] = accP[j][:, zn].astype(BF16)
        post(bufZ[j], RZ[j], r_pz + j, dev(hh=zn))

    def to_c(j):
        got(RZ[j], r_pz + j)
        own[j][...] = accP[j][c, zh] + RZ[j][c].astype(F32)
        bufC[j][...] = accP[j][oc, zh] + RZ[j][oc].astype(F32)
        post(bufC[j], RC[j], r_pc + j, other_core)

    def finish_weight_grad():
        got(RW.at[oc, 0], r_wg + 2 * oc)
        for w in range(2):
            got(RW.at[w, 1], r_wg + 2 * w + 1)

        for w in range(2):
            @pl.loop(0, NC)
            def _(j):
                cols = pl.ds(pl.multiple_of(w * SHIFT + j * CW, 128), CW)
                WG[:, cols] = (RW[w, 0, j].astype(F32) + RW[w, 1, j].astype(F32)).astype(BF16)

        return local(WG, wg_ref)

    def finish_context_grad():
        for m in (1, 2, 3):
            src = lax.rem(zl + m, 4)

            @pl.when(jnp.logical_or(middle, src != 3 - zl))
            def _():
                got(RDZ.at[src], r_dz + src)

        total = RDZ[0].astype(F32)
        for m in (1, 2, 3):
            total = total + RDZ[m].astype(F32)
        total = total.astype(BF16).reshape(8, 64, 256)
        CG[...] = jnp.concatenate([total[g][:, :ROWS] for g in range(8)], axis=1)
        return local(CG, cg_ref)

    to_y(0)
    grad_core()
    relay_on(far == n2)
    grad_own()
    to_z(0)
    relay_on(far == x2)
    to_y(1)
    pass_on(2)
    to_z(1)
    to_y(2)
    wg_out = finish_weight_grad()
    to_z(2)
    to_c(0)
    to_c(1)
    cg_out = finish_context_grad()
    to_c(2)

    for j in range(NC):
        got(RC[j], r_pc + j)
    for w in (1, 0):
        for j in range(NC):
            cols = slice(w * SHIFT + PO[j], w * SHIFT + PO[j] + PW[j])
            v = jnp.where(c == w, own[j][...], RC[j][...])
            upd_ref[:, cols] = (res_ref[:, cols].astype(F32) + v).astype(BF16)

    wg_out.wait()
    cg_out.wait()
    for cp in sent:
        cp.wait_send()
    for s in range(3):
        drain(DWs.at[s], s_wg + s)
    for k in range(4):
        drain(RDC.at[k], s_dc + k)
    for to in range(3):
        drain(Wb.at[0], s_w + to)
    for k in range(4):
        d = blocks[k]

        @pl.when(jnp.logical_not(jnp.logical_or(d == zl, jnp.logical_and(middle, d == far))))
        def _():
            drain(TZ.at[d], s_dz + k)

    @pl.when(middle)
    def _():
        drain(TZ.at[far], s_dz + 4)


def hand_over(a, b, d, a_out, b_out, d_out, va, vb, vd, sems):
    moves = [(d.at[:, pl.ds(o, n)], vd.at[:, pl.ds(o, n)], d_out.at[:, pl.ds(o, n)])
             for o, n in ((0, 1024), (1024, 1024), (2048, 1024), (3072, 640))]
    moves += [(a, va, a_out), (b, vb, b_out)]
    arrive = [pltpu.make_async_copy(src, mid, sems.at[0, i]) for i, (src, mid, _) in enumerate(moves)]
    leave = [pltpu.make_async_copy(mid, dst, sems.at[1, i]) for i, (_, mid, dst) in enumerate(moves)]
    for cp in arrive:
        cp.start()
    for first, second in zip(arrive, leave):
        first.wait()
        second.start()
    for cp in leave:
        cp.wait()


def per_device(residual, context, proj_weight, out_grad):
    vmem = pl.BlockSpec(memory_space=pltpu.VMEM)
    anywhere = pl.BlockSpec(memory_space=pl.ANY)
    shape = jax.ShapeDtypeStruct
    updated, context_grad, weight_grad = pl.pallas_call(
        kernel,
        out_shape=(
            shape((TOK, D_ROW), BF16),
            shape((64, 8 * ROWS), BF16),
            shape((ROWS, D_ROW), BF16),
        ),
        in_specs=[vmem, anywhere, anywhere, anywhere],
        out_specs=(vmem, anywhere, anywhere),
        scratch_shapes=[
            pltpu.VMEM((4, ROWS, WIN), BF16),
            pltpu.VMEM((2, 2, 4, 2, TOK, WIN), BF16),
            pltpu.VMEM((4, 4, 4, 64, ROWS), BF16),
            pltpu.VMEM((4, ROWS, 1024), BF16),
            [pltpu.VMEM((2, 2, 64, w), BF16) for w in PW],
            [pltpu.VMEM((2, 2, 64, w), BF16) for w in PW],
            [pltpu.VMEM((2, 2, 64, w), BF16) for w in PW],
            [pltpu.VMEM((2, 2, 64, w), BF16) for w in PW],
            [pltpu.VMEM((2, 2, 64, w), BF16) for w in PW],
            [pltpu.VMEM((2, 2, 64, w), BF16) for w in PW],
            [pltpu.VMEM((4, 4, 64, w), F32) for w in PW],
            [pltpu.VMEM((2, 2, TOK, w), F32) for w in PW],
            [pltpu.VMEM((2, 2, TOK, w), BF16) for w in PW],
            [pltpu.VMEM((2, 2, TOK, w), BF16) for w in PW],
            [pltpu.VMEM((2, TOK, w), BF16) for w in PW],
            [pltpu.VMEM((2, TOK, w), BF16) for w in PW],
            [pltpu.VMEM((TOK, w), F32) for w in PW],
            [pltpu.VMEM((TOK, w), F32) for w in PW],
            [pltpu.VMEM((TOK, w), F32) for w in PW],
            pltpu.VMEM((4, 4, 2, 64, 256), BF16),
            pltpu.VMEM((4, 4, 2, 64, 256), BF16),
            pltpu.VMEM((4, 4, 2, 64, 256), BF16),
            pltpu.VMEM((4, 4, 2, 64, 256), BF16),
            pltpu.VMEM((4, 4, 2, 64, 256), BF16),
            pltpu.VMEM((4, 4, 2, 64, 256), BF16),
            pltpu.VMEM((4, 2, 64, 256), BF16),
            pltpu.VMEM((3, NC, ROWS, CW), BF16),
            pltpu.VMEM((2, 2, NC, ROWS, CW), BF16),
            pltpu.VMEM((ROWS, D_ROW), BF16),
            pltpu.VMEM((64, 8 * ROWS), BF16),
            pltpu.SemaphoreType.DMA((S_SEMS,)),
            pltpu.SemaphoreType.DMA((R_SEMS,)),
            pltpu.SemaphoreType.DMA((L_SEMS,)),
        ],
        compiler_params=pltpu.CompilerParams(
            collective_id=0, has_side_effects=True, vmem_limit_bytes=60 * 2**20
        ),
        cost_estimate=pl.CostEstimate(
            flops=6 * 1024 * 928 * WIN, bytes_accessed=8 * 2**20, transcendentals=0
        ),
    )(residual, context.T.reshape(8, ROWS, 256), proj_weight[0], out_grad)
    updated, context_grad, weight_grad = pl.pallas_call(
        hand_over,
        out_shape=(
            shape((TOK, D_ROW), BF16),
            shape((64, 8 * ROWS), BF16),
            shape((ROWS, D_ROW), BF16),
        ),
        in_specs=[anywhere] * 3,
        out_specs=(anywhere,) * 3,
        scratch_shapes=[
            pltpu.VMEM((TOK, D_ROW), BF16),
            pltpu.VMEM((64, 8 * ROWS), BF16),
            pltpu.VMEM((ROWS, D_ROW), BF16),
            pltpu.SemaphoreType.DMA((2, 6)),
        ],
    )(updated, context_grad, weight_grad)
    return updated, context_grad, weight_grad[None]


def solution(mesh):
    in_specs = (P(("ia", "wa"), "ao"), P("ia", "wa"), P("wa", "ia", "ao"), P(("ia", "wa"), "ao"))
    out_specs = (P(("ia", "wa"), "ao"), P(("ia", "ao"), "wa"), P("wa", "ia", "ao"))
    return jax.shard_map(
        per_device, mesh=mesh, in_specs=in_specs, out_specs=out_specs, check_vma=False
    )
```

```python
import jax
import jax.numpy as jnp
from jax import lax
from jax.experimental import pallas as pl
from jax.experimental.pallas import tpu as pltpu
from jax.sharding import PartitionSpec as P

MESH = pl.DeviceIdType.MESH
BF16 = jnp.bfloat16
F32 = jnp.float32

ROWS = 232
D_ROW = 3712
SHIFT = 1792
WIN = 1920
NC = 3
CW = WIN // NC
PW = (768, 512, 384, 256)
PO = (0, 768, 1280, 1664)
NP = len(PW)
TOK = 32


class Sems:
    def __init__(self):
        self.n = 0

    def take(self, count):
        base = self.n
        self.n += count
        return base


S_SEMS, R_SEMS, L_SEMS = 83, 83, 9


def kernel(
    res_ref, ctx_ref, w_ref, g_ref,
    upd_ref, cg_ref, wg_ref,
    Wb, Gb, Xb, XT,
    bufA, RA, bufB1, bufB2, RB1, RB2, PF, accP,
    bufY, RY, bufZ, RZ, bufC, RC,
    OWN, DY, RDY, RDC, TZ, RDZ, RL,
    DWs, RW, WG, CG,
    ss, rs, ls,
):
    ia = lax.axis_index("ia")
    wa = lax.axis_index("wa")
    zl = lax.axis_index("ao")
    y, c = lax.div(ia, 2), lax.rem(ia, 2)
    x, zh = lax.div(wa, 2), lax.rem(wa, 2)
    oc, zn = 1 - c, 1 - zh

    def flip(v):
        return v + 1 - 2 * lax.rem(v, 2)

    ya, yb = flip(y), 3 - y

    def w_pair(yy, cc):
        return (1 - cc) * flip(yy) + cc * (3 - yy)

    def t_pair(yy, cc):
        return cc * flip(yy) + (1 - cc) * (3 - yy)

    wp, tp = w_pair(y, c), t_pair(y, c)
    xp, xm, x2 = lax.rem(x + 1, 4), lax.rem(x + 3, 4), lax.rem(x + 2, 4)

    def dev(yy=y, cc=c, xx=x, hh=zh, ll=zl):
        return (2 * yy + cc, 2 * xx + hh, ll)

    other_core = dev(cc=oc)
    partners = [
        other_core,
        dev(yy=ya, cc=0), dev(yy=ya, cc=1), dev(yy=yb, cc=0), dev(yy=yb, cc=1),
        dev(xx=xp), dev(xx=xm),
        dev(hh=zn), dev(hh=zn, cc=oc),
    ] + [dev(ll=lax.rem(zl + m, 4)) for m in (1, 2, 3)]

    middle = lax.rem(zl, 3) != 0
    far = 3 * (1 - lax.rem(zl + 1, 2))

    mate = 3 - zl
    absent = 3 * (1 - lax.div(zl, 2))
    RDZ[absent] = jnp.zeros((4, 2, 64, 256), BF16)

    barrier = pltpu.get_barrier_semaphore()
    for p in partners:
        pl.semaphore_signal(barrier, inc=1, device_id=p, device_id_type=MESH)
    pl.semaphore_wait(barrier, len(partners))

    s_idx, r_idx, l_idx = Sems(), Sems(), Sems()
    sent = []

    def send(src, dst, r, to, s=None):
        if s is None:
            s = s_idx.take(1)
        cp = pltpu.make_async_remote_copy(
            src_ref=src, dst_ref=dst, send_sem=ss.at[s], recv_sem=rs.at[r],
            device_id=to, device_id_type=MESH,
        )
        cp.start()
        return cp

    def post(*args):
        sent.append(send(*args))

    def got(dst, r):
        pltpu.make_async_remote_copy(
            src_ref=dst, dst_ref=dst, send_sem=ss.at[0], recv_sem=rs.at[r],
            device_id=other_core, device_id_type=MESH,
        ).wait_recv()

    def local(src, dst):
        cp = pltpu.make_async_copy(src, dst, ls.at[l_idx.take(1)])
        cp.start()
        return cp

    def window(cc):
        return pl.ds(pl.multiple_of(cc * SHIFT, 128), WIN)

    r_g0 = r_idx.take(1)
    r_g1 = r_idx.take(1)
    g_own = g_ref.at[:, window(c)]
    g_oth = g_ref.at[:, window(oc)]
    g_local = local(g_own, Gb.at[0, c, x, zh])
    post(g_oth, Gb.at[0, c, x, zh], r_g0, other_core)
    post(g_own, Gb.at[0, c, x, zh], r_g1, dev(hh=zn))
    post(g_oth, Gb.at[0, c, x, zh], r_g1, dev(hh=zn, cc=oc))

    r_w = r_idx.take(1 + NP)
    s_w = s_idx.take(3)

    def w_cols(cc, j):
        return pl.ds(pl.multiple_of(cc * SHIFT + PO[j], 128), PW[j])

    def send_w(j):
        cols = pl.ds(PO[j], PW[j])
        for cc, yy in ((0, ya), (1, yb)):
            send(w_ref.at[:, w_cols(cc, j)], Wb.at[2 + c, :, cols],
                 r_w + 1 + j, dev(yy=yy, cc=cc), s_w + 1 + cc)

    r_y = r_idx.take(2)
    r_xp = r_idx.take(4)
    r_xm = r_idx.take(4)
    r_f = r_idx.take(4)

    def unit(p, xx, h):
        return Gb.at[p, :, xx, h]

    def to_x(p, k, h):
        post(unit(p, x, h), unit(p, x, h), r_xp + 2 * p + k, dev(xx=xp))
        post(unit(p, x, h), unit(p, x, h), r_xm + 2 * p + k, dev(xx=xm))

    def forward_up(k, h):
        got(unit(0, xm, h), r_xp + k)
        post(unit(0, xm, h), unit(0, xm, h), r_f + k, dev(xx=xp))

    def forward_down(k, h):
        got(unit(1, xp, h), r_xm + 2 + k)
        post(unit(1, xp, h), unit(1, xp, h), r_f + 2 + k, dev(xx=xm))

    def to_partner(k, h):
        post(unit(0, x, h), unit(1, x, h), r_y + k, dev(yy=tp))

    def from_partner(k, h):
        got(unit(1, x, h), r_y + k)

    g_local.wait()
    got(Gb.at[0, oc, x, zh], r_g0)
    to_partner(0, zh)
    to_x(0, 0, zh)

    r_c = r_idx.take(8)
    half = lax.rem(zl, 2)

    def x_block(q, blk):
        return XT.at[pl.ds(2 * q, 2), :, pl.ds(pl.multiple_of(blk * 256, 256), 256)]

    def x_group(q, yy, cc):
        chip = (1 - q) * yy + q * w_pair(yy, cc)
        return ctx_ref.at[pl.ds(2 * chip, 2)]

    def got_x(q, blk):
        got(x_block(q, blk), r_c + 2 * blk + q)

    def transpose_x(s, blk):
        t = XT[s, :, blk * 256:(blk + 1) * 256].T
        Xb[s, blk] = t.reshape(4, 64, ROWS)

    def send_context(y_to, cc):
        post(x_group(half, y_to, cc), x_block(half, 2 + c), r_c + 2 * (2 + c) + half, dev(yy=y_to, cc=cc))

    send_context(tp, c)
    x_locals = []
    for q in range(2):
        x_locals.append(local(x_group(q, y, c), x_block(q, c)))
        post(x_group(q, y, oc), x_block(q, c), r_c + 2 * c + q, other_core)

    w_locals = []
    for j in range(NP):
        cols = pl.ds(PO[j], PW[j])
        w_locals.append(local(w_ref.at[:, w_cols(c, j)], Wb.at[c, :, cols]))
        send(w_ref.at[:, w_cols(oc, j)], Wb.at[c, :, cols], r_w, other_core, s_w)


    from_partner(0, zh)
    to_x(1, 0, zh)
    send_context(wp, oc)
    send_w(0)
    forward_up(0, zh)
    for cp in x_locals:
        cp.wait()
    for q in range(2):
        got_x(q, oc)
    for blk in range(2):
        for sl in range(4):
            transpose_x(sl, blk)
    for blk in (2, 3):
        got_x(half, blk)
        post(x_block(half, blk), x_block(half, blk), r_c + 2 * blk + half, dev(ll=flip(zl)))
    for blk in (2, 3):
        for sl in range(2):
            transpose_x(2 * half + sl, blk)
    forward_down(0, zh)

    got(unit(0, x, zn), r_g1)
    to_partner(1, zn)
    to_x(0, 1, zn)
    for j in range(1, NP):
        send_w(j)
    from_partner(1, zn)
    to_x(1, 1, zn)

    for blk in (2, 3):
        got_x(1 - half, blk)
        for sl in range(2):
            transpose_x(2 * (1 - half) + sl, blk)
    for cp in w_locals:
        cp.wait()
    got(Wb.at[oc], r_w)

    def project(j):
        @pl.loop(0, 4)
        def _(blk):
            total = None
            for sl in range(4):
                a = Xb[sl, blk].reshape(256, ROWS)
                part = jnp.dot(a, Wb[sl, :, PO[j]:PO[j] + PW[j]], preferred_element_type=F32)
                total = part if total is None else total + part
            PF[j][blk] = total.reshape(4, 64, PW[j])

    r_a = r_idx.take(2 * NP)
    r_b1 = r_idx.take(2 * NP)
    r_b2 = r_idx.take(2 * NP)
    to_xp, to_xm = dev(xx=xp), dev(xx=xm)

    def drain(src, s):
        pltpu.make_async_remote_copy(
            src_ref=src, dst_ref=src, send_sem=ss.at[s], recv_sem=rs.at[0],
            device_id=other_core, device_id_type=MESH,
        ).wait_send()

    def got_w(j):
        cols = pl.ds(PO[j], PW[j])
        got(Wb.at[2:4, :, cols], r_w + 1 + j)
        if j == 0:
            keep = (c == 0).astype(BF16)
            for s in range(4):
                Wb[s, :, 0:128] = Wb[s, :, 0:128] * keep

    def project_chunk(j):
        got_w(j)
        project(j)

    def post_a(j):
        bufA[j][...] = PF[j][:, x2].astype(BF16).reshape(2, 2, 64, PW[j])
        post(bufA[j].at[0], RA[j].at[0], r_a + 2 * j, to_xp)
        post(bufA[j].at[1], RA[j].at[1], r_a + 2 * j + 1, to_xm)

    def post_b(j):
        bufB1[j][1] = PF[j][2:4, xp].astype(BF16)
        post(bufB1[j].at[1], RB1[j].at[1], r_b1 + 2 * j + 1, to_xp)
        bufB2[j][0] = PF[j][0:2, xm].astype(BF16)
        post(bufB2[j].at[0], RB2[j].at[0], r_b2 + 2 * j, to_xm)

    def pass_on(j):
        got(RA[j].at[0], r_a + 2 * j)
        bufB1[j][0] = (PF[j][0:2, xp] + RA[j][0].astype(F32)).astype(BF16)
        post(bufB1[j].at[0], RB1[j].at[0], r_b1 + 2 * j, to_xp)
        got(RA[j].at[1], r_a + 2 * j + 1)
        bufB2[j][1] = (PF[j][2:4, xm] + RA[j][1].astype(F32)).astype(BF16)
        post(bufB2[j].at[1], RB2[j].at[1], r_b2 + 2 * j + 1, to_xm)

    r_dy, r_dc, r_dz = r_idx.take(4), r_idx.take(4), r_idx.take(4)
    s_dc = s_idx.take(4)
    r_rl = r_idx.take(2)
    s_dz = s_idx.take(6)
    n1, n2 = 3 - x, flip(x)
    blocks = (x, n1, n2, x2)

    def back(k, first=0, last=4):
        d = blocks[k]

        @pl.loop(first, last)
        def _(s):
            g = Gb[:, :, d].reshape(256, WIN)
            t = lax.dot_general(g, Wb[s], (((1,), (1,)), ((), ())),
                                preferred_element_type=F32).astype(BF16)
            t = jnp.concatenate([t, jnp.zeros((256, 256 - ROWS), BF16)], axis=1)
            t = t.reshape(2, 2, 64, 256)
            OWN[k, s] = t[0]
            DY[k, s] = t[1]

        if last == 4:
            post(DY.at[k], RDY.at[k], r_dy + k, dev(yy=tp))

    r_wg = r_idx.take(4)
    s_wg = s_idx.take(3)

    def grad(s, j):
        cols = pl.ds(pl.multiple_of(j * CW, 128), CW)
        b = Gb[:, :, :, :, :, cols].reshape(1024, CW)
        return jnp.dot(XT[s], b, preferred_element_type=F32).astype(BF16)

    own_groups = (y, wp)
    got_groups = (tp, w_pair(tp, c))

    def to_core(k):
        got(RDY.at[k], r_dy + k)
        for q in range(2):
            for part, group in ((OWN, own_groups[q]), (RDY, got_groups[q])):
                send(part.at[k, pl.ds(2 * q, 2), oc], RDC.at[k, group], r_dc + k, other_core, s_dc + k)

    def to_ao(k):
        d = blocks[k]
        got(RDC.at[k], r_dc + k)
        for q in range(2):
            for part, group in ((OWN, own_groups[q]), (RDY, got_groups[q])):
                TZ[d, group] = (part[k, 2 * q:2 * q + 2, c].astype(F32)
                                + RDC[k, group].astype(F32)).astype(BF16)

        neighbour = 1 + lax.div(zl, 3)
        relay = jnp.logical_and(jnp.logical_not(middle), jnp.logical_and(d != zl, d != neighbour))
        held = jnp.logical_and(middle, jnp.logical_or(d == far, d == mate))

        @pl.when(relay)
        def _():
            r = lax.min(lax.rem(d, 3), 1)
            send(TZ.at[d], RL.at[r], r_rl + r, dev(ll=neighbour), s_dz + k)

        @pl.when(jnp.logical_not(jnp.logical_or(relay, jnp.logical_or(held, d == zl))))
        def _():
            send(TZ.at[d], RDZ.at[zl], r_dz + zl, dev(ll=d), s_dz + k)

        @pl.when(d == zl)
        def _():
            RDZ[zl] = TZ[d]

    def relay_on(*ks):
        for r, d in ((0, far), (1, mate)):
            due = d == blocks[ks[0]]
            for k in ks[1:]:
                due = jnp.logical_or(due, d == blocks[k])

            @pl.when(jnp.logical_and(middle, due))
            def _():
                got(RL.at[r], r_rl + r)
                TZ[d] = (TZ[d].astype(F32) + RL[r].astype(F32)).astype(BF16)
                send(TZ.at[d], RDZ.at[zl], r_dz + zl, dev(ll=d), s_dz + 4 + r)

    def grad_other(core):
        to = dev(yy=wp, cc=core)

        @pl.loop(0, NC)
        def _(j):
            DWs[core, j] = grad(2 + core, j)
            send(DWs.at[core, j], RW.at[c, 1, j], r_wg + 2 * c + 1, to, s_wg + core)

    def grad_core():
        @pl.loop(0, NC)
        def _(j):
            DWs[2, j] = grad(oc, j)
            send(DWs.at[2, j], RW.at[c, 0, j], r_wg + 2 * c, other_core, s_wg + 2)

    def grad_own():
        @pl.loop(0, NC)
        def _(j):
            RW[c, 0, j] = grad(c, j)

    r_py, r_pz, r_pc = r_idx.take(NP), r_idx.take(NP), r_idx.take(NP)

    def to_y(j):
        got(RB1[j].at[1], r_b1 + 2 * j + 1)
        got(RB2[j].at[1], r_b2 + 2 * j + 1)
        v = PF[j][2:4, x] + RB1[j][1].astype(F32) + RB2[j][1].astype(F32)
        bufY[j][...] = v.astype(BF16).reshape(2, 2, TOK, PW[j])
        post(bufY[j], RY[j], r_py + j, dev(yy=tp))

    def to_z(j):
        got(RB1[j].at[0], r_b1 + 2 * j)
        got(RB2[j].at[0], r_b2 + 2 * j)
        v = PF[j][0:2, x] + RB1[j][0].astype(F32) + RB2[j][0].astype(F32)
        got(RY[j], r_py + j)
        v = v.reshape(2, 2, TOK, PW[j]) + RY[j][...].astype(F32)
        accP[j][...] = v
        bufZ[j][...] = accP[j][:, zn].astype(BF16)
        post(bufZ[j].at[c], RZ[j].at[c], r_pz + j, dev(hh=zn))
        post(bufZ[j].at[oc], RZ[j].at[c], r_pz + j, dev(hh=zn, cc=oc))
        bufC[j][...] = accP[j][oc, zh]
        post(bufC[j], RC[j], r_pc + j, other_core)

    def finish_update(j):
        got(RC[j], r_pc + j)
        got(RZ[j], r_pz + j)
        for w in (1, 0):
            cols = slice(w * SHIFT + PO[j], w * SHIFT + PO[j] + PW[j])
            v = jnp.where(c == w, accP[j][c, zh], RC[j][...]) + RZ[j][w].astype(F32)
            upd_ref[:, cols] = (res_ref[:, cols].astype(F32) + v).astype(BF16)

    def finish_weight_grad():
        got(RW.at[oc, 0], r_wg + 2 * oc)
        for w in range(2):
            got(RW.at[w, 1], r_wg + 2 * w + 1)

        for w in range(2):
            @pl.loop(0, NC)
            def _(j):
                cols = pl.ds(pl.multiple_of(w * SHIFT + j * CW, 128), CW)
                WG[:, cols] = (RW[w, 0, j].astype(F32) + RW[w, 1, j].astype(F32)).astype(BF16)

        return local(WG, wg_ref)

    def finish_context_grad():
        for m in (1, 2, 3):
            src = lax.rem(zl + m, 4)

            @pl.when(src != absent)
            def _():
                got(RDZ.at[src], r_dz + src)

        total = RDZ[0].astype(F32)
        for m in (1, 2, 3):
            total = total + RDZ[m].astype(F32)
        total = total.astype(BF16).reshape(8, 64, 256)
        CG[...] = jnp.concatenate([total[g][:, :ROWS] for g in range(8)], axis=1)
        return local(CG, cg_ref)

    project_chunk(0)
    forward_up(1, zn)
    post_a(0)
    back(0, 0, 2)
    forward_down(1, zn)
    post_b(0)
    for j in range(1, NP):
        got_w(j)
    back(0, 2, 4)
    for h, k in ((zh, 0), (zn, 1)):
        got(unit(1, xm, h), r_xp + 2 + k)
        got(unit(0, xp, h), r_xm + k)
    back(1)
    project(1)
    post_a(1)
    back(2)
    pass_on(0)
    post_b(1)
    to_core(0)
    for k, h in ((0, zh), (1, zn)):
        got(unit(0, x2, h), r_f + k)
        got(unit(1, x2, h), r_f + 2 + k)
    back(3)
    to_ao(0)
    to_core(1)
    grad_other(0)
    to_ao(1)
    to_core(2)
    grad_other(1)
    to_ao(2)
    pass_on(1)
    to_core(3)
    relay_on(0, 1)
    project(2)
    project(3)
    post_a(2)
    post_a(3)
    post_b(2)
    post_b(3)
    to_y(0)
    to_ao(3)

    grad_core()
    relay_on(2)
    grad_own()
    to_z(0)
    relay_on(3)
    to_y(1)
    pass_on(2)
    pass_on(3)
    to_z(1)
    to_y(2)
    to_y(3)
    wg_out = finish_weight_grad()
    to_z(2)
    to_z(3)
    finish_update(0)
    finish_update(1)
    cg_out = finish_context_grad()
    finish_update(2)
    finish_update(3)

    wg_out.wait()
    cg_out.wait()
    for cp in sent:
        cp.wait_send()
    for s in range(3):
        drain(DWs.at[s], s_wg + s)
    for k in range(4):
        drain(RDC.at[k], s_dc + k)
    for to in range(3):
        drain(Wb.at[0], s_w + to)
    for k in range(4):
        d = blocks[k]

        @pl.when(jnp.logical_not(jnp.logical_or(d == zl, jnp.logical_and(middle, jnp.logical_or(d == far, d == mate)))))
        def _():
            drain(TZ.at[d], s_dz + k)

    @pl.when(middle)
    def _():
        drain(TZ.at[far], s_dz + 4)
        drain(TZ.at[mate], s_dz + 5)


def hand_over(a, b, d, a_out, b_out, d_out, va, vb, vd, sems):
    moves = [(d.at[:, pl.ds(o, n)], vd.at[:, pl.ds(o, n)], d_out.at[:, pl.ds(o, n)])
             for o, n in ((0, 1024), (1024, 1024), (2048, 1024), (3072, 640))]
    moves += [(a, va, a_out), (b, vb, b_out)]
    arrive = [pltpu.make_async_copy(src, mid, sems.at[0, i]) for i, (src, mid, _) in enumerate(moves)]
    leave = [pltpu.make_async_copy(mid, dst, sems.at[1, i]) for i, (_, mid, dst) in enumerate(moves)]
    for cp in arrive:
        cp.start()
    for first, second in zip(arrive, leave):
        first.wait()
        second.start()
    for cp in leave:
        cp.wait()


def per_device(residual, context, proj_weight, out_grad):
    vmem = pl.BlockSpec(memory_space=pltpu.VMEM)
    anywhere = pl.BlockSpec(memory_space=pl.ANY)
    shape = jax.ShapeDtypeStruct
    updated, context_grad, weight_grad = pl.pallas_call(
        kernel,
        out_shape=(
            shape((TOK, D_ROW), BF16),
            shape((64, 8 * ROWS), BF16),
            shape((ROWS, D_ROW), BF16),
        ),
        in_specs=[vmem, anywhere, anywhere, anywhere],
        out_specs=(vmem, anywhere, anywhere),
        scratch_shapes=[
            pltpu.VMEM((4, ROWS, WIN), BF16),
            pltpu.VMEM((2, 2, 4, 2, TOK, WIN), BF16),
            pltpu.VMEM((4, 4, 4, 64, ROWS), BF16),
            pltpu.VMEM((4, ROWS, 1024), BF16),
            [pltpu.VMEM((2, 2, 64, w), BF16) for w in PW],
            [pltpu.VMEM((2, 2, 64, w), BF16) for w in PW],
            [pltpu.VMEM((2, 2, 64, w), BF16) for w in PW],
            [pltpu.VMEM((2, 2, 64, w), BF16) for w in PW],
            [pltpu.VMEM((2, 2, 64, w), BF16) for w in PW],
            [pltpu.VMEM((2, 2, 64, w), BF16) for w in PW],
            [pltpu.VMEM((4, 4, 64, w), F32) for w in PW],
            [pltpu.VMEM((2, 2, TOK, w), F32) for w in PW],
            [pltpu.VMEM((2, 2, TOK, w), BF16) for w in PW],
            [pltpu.VMEM((2, 2, TOK, w), BF16) for w in PW],
            [pltpu.VMEM((2, TOK, w), BF16) for w in PW],
            [pltpu.VMEM((2, TOK, w), BF16) for w in PW],
            [pltpu.VMEM((TOK, w), F32) for w in PW],
            [pltpu.VMEM((TOK, w), F32) for w in PW],
            pltpu.VMEM((4, 4, 2, 64, 256), BF16),
            pltpu.VMEM((4, 4, 2, 64, 256), BF16),
            pltpu.VMEM((4, 4, 2, 64, 256), BF16),
            pltpu.VMEM((4, 4, 2, 64, 256), BF16),
            pltpu.VMEM((4, 4, 2, 64, 256), BF16),
            pltpu.VMEM((4, 4, 2, 64, 256), BF16),
            pltpu.VMEM((2, 4, 2, 64, 256), BF16),
            pltpu.VMEM((3, NC, ROWS, CW), BF16),
            pltpu.VMEM((2, 2, NC, ROWS, CW), BF16),
            pltpu.VMEM((ROWS, D_ROW), BF16),
            pltpu.VMEM((64, 8 * ROWS), BF16),
            pltpu.SemaphoreType.DMA((S_SEMS,)),
            pltpu.SemaphoreType.DMA((R_SEMS,)),
            pltpu.SemaphoreType.DMA((L_SEMS,)),
        ],
        compiler_params=pltpu.CompilerParams(
            collective_id=0, has_side_effects=True, vmem_limit_bytes=60 * 2**20
        ),
        cost_estimate=pl.CostEstimate(
            flops=6 * 1024 * 928 * WIN, bytes_accessed=8 * 2**20, transcendentals=0
        ),
    )(residual, context.T.reshape(8, ROWS, 256), proj_weight[0], out_grad)
    updated, context_grad, weight_grad = pl.pallas_call(
        hand_over,
        out_shape=(
            shape((TOK, D_ROW), BF16),
            shape((64, 8 * ROWS), BF16),
            shape((ROWS, D_ROW), BF16),
        ),
        in_specs=[anywhere] * 3,
        out_specs=(anywhere,) * 3,
        scratch_shapes=[
            pltpu.VMEM((TOK, D_ROW), BF16),
            pltpu.VMEM((64, 8 * ROWS), BF16),
            pltpu.VMEM((ROWS, D_ROW), BF16),
            pltpu.SemaphoreType.DMA((2, 6)),
        ],
    )(updated, context_grad, weight_grad)
    return updated, context_grad, weight_grad[None]


def solution(mesh):
    in_specs = (P(("ia", "wa"), "ao"), P("ia", "wa"), P("wa", "ia", "ao"), P(("ia", "wa"), "ao"))
    out_specs = (P(("ia", "wa"), "ao"), P(("ia", "ao"), "wa"), P("wa", "ia", "ao"))
    return jax.shard_map(
        per_device, mesh=mesh, in_specs=in_specs, out_specs=out_specs, check_vma=False
    )
```

```python
import jax
import jax.numpy as jnp
from jax import lax
from jax.experimental import pallas as pl
from jax.experimental.pallas import tpu as pltpu
from jax.sharding import PartitionSpec as P

MESH = pl.DeviceIdType.MESH
BF16 = jnp.bfloat16
F32 = jnp.float32

ROWS = 232
D_ROW = 3712
SHIFT = 1792
WIN = 1920
SHARED = 128
NC = 3
CW = WIN // NC
PW = (768, 512, 384, 256)
PO = (0, 768, 1280, 1664)
NP = len(PW)
TOK = 32


class Sems:
    def __init__(self):
        self.n = 0

    def take(self, count):
        base = self.n
        self.n += count
        return base


S_SEMS, R_SEMS, L_SEMS = 83, 84, 9


def kernel(
    res_ref, ctx_ref, w_ref, g_ref,
    upd_ref, cg_ref, wg_ref,
    Wb, Gb, Xb, XT,
    bufA, RA, bufB1, bufB2, RB1, RB2, PF, accP,
    bufY, RY, bufZ, RZ, bufC, RC,
    OWN, DY, RDY, RDC, TZ, RDZ, RL,
    DWs, RW, WG, CG,
    ss, rs, ls,
):
    ia = lax.axis_index("ia")
    wa = lax.axis_index("wa")
    zl = lax.axis_index("ao")
    y, c = lax.div(ia, 2), lax.rem(ia, 2)
    x, zh = lax.div(wa, 2), lax.rem(wa, 2)
    oc, zn = 1 - c, 1 - zh

    def flip(v):
        return v + 1 - 2 * lax.rem(v, 2)

    ya, yb = flip(y), 3 - y

    def w_pair(yy, cc):
        return (1 - cc) * flip(yy) + cc * (3 - yy)

    def t_pair(yy, cc):
        return cc * flip(yy) + (1 - cc) * (3 - yy)

    wp, tp = w_pair(y, c), t_pair(y, c)
    xp, xm, x2 = lax.rem(x + 1, 4), lax.rem(x + 3, 4), lax.rem(x + 2, 4)

    def dev(yy=y, cc=c, xx=x, hh=zh, ll=zl):
        return (2 * yy + cc, 2 * xx + hh, ll)

    other_core = dev(cc=oc)
    partners = [
        other_core,
        dev(yy=ya, cc=0), dev(yy=ya, cc=1), dev(yy=yb, cc=0), dev(yy=yb, cc=1),
        dev(xx=xp), dev(xx=xm),
        dev(hh=zn), dev(hh=zn, cc=oc),
    ] + [dev(ll=lax.rem(zl + m, 4)) for m in (1, 2, 3)]

    middle = lax.rem(zl, 3) != 0
    far = 3 * (1 - lax.rem(zl + 1, 2))

    mate = 3 - zl
    absent = 3 * (1 - lax.div(zl, 2))
    RDZ[absent] = jnp.zeros((4, 2, 64, 256), BF16)

    @pl.when(c == 1)
    def _():
        Gb[:, :, :, :, :, 0:SHARED] = jnp.zeros((2, 2, 4, 2, TOK, SHARED), BF16)
        Wb[2:4, :, 0:SHARED] = jnp.zeros((2, ROWS, SHARED), BF16)


    barrier = pltpu.get_barrier_semaphore()
    for p in partners:
        pl.semaphore_signal(barrier, inc=1, device_id=p, device_id_type=MESH)
    pl.semaphore_wait(barrier, len(partners))

    s_idx, r_idx, l_idx = Sems(), Sems(), Sems()
    sent = []
    sent_cut = []

    def send(src, dst, r, to, s=None):
        if s is None:
            s = s_idx.take(1)
        cp = pltpu.make_async_remote_copy(
            src_ref=src, dst_ref=dst, send_sem=ss.at[s], recv_sem=rs.at[r],
            device_id=to, device_id_type=MESH,
        )
        cp.start()
        return cp

    def post(*args):
        sent.append(send(*args))

    def by_core(core, act):
        for cc in range(2):
            @pl.when(core == cc)
            def _():
                act(cc * SHARED)

    def post_cut(core, src, dst, r, to):
        i = s_idx.take(1)
        by_core(core, lambda cut: send(src(cut), dst(cut), r, to, i))
        sent_cut.append((core, src, i))

    def got(dst, r):
        pltpu.make_async_remote_copy(
            src_ref=dst, dst_ref=dst, send_sem=ss.at[0], recv_sem=rs.at[r],
            device_id=other_core, device_id_type=MESH,
        ).wait_recv()

    def local(src, dst):
        cp = pltpu.make_async_copy(src, dst, ls.at[l_idx.take(1)])
        cp.start()
        return cp

    r_g0 = r_idx.take(1)
    r_g1 = r_idx.take(1)
    def g_part(cc):
        return lambda cut: g_ref.at[:, pl.ds(pl.multiple_of(cc * SHIFT + cut, 128), WIN - cut)]

    def g_slot(cut):
        return Gb.at[0, c, x, zh, :, pl.ds(cut, WIN - cut)]

    g_local = local(g_part(c)(0), Gb.at[0, c, x, zh])
    post_cut(oc, g_part(oc), g_slot, r_g0, other_core)
    post_cut(c, g_part(c), g_slot, r_g1, dev(hh=zn))
    post_cut(oc, g_part(oc), g_slot, r_g1, dev(hh=zn, cc=oc))

    r_w = r_idx.take(1 + NP)
    s_w = s_idx.take(3)

    def w_cols(cc, j):
        return pl.ds(pl.multiple_of(cc * SHIFT + PO[j], 128), PW[j])

    def send_w(j):
        for cc, yy in ((0, ya), (1, yb)):
            cut = cc * SHARED if j == 0 else 0
            n = PW[j] - cut
            src = w_ref.at[:, pl.ds(cc * SHIFT + PO[j] + cut, n)]
            send(src, Wb.at[2 + c, :, pl.ds(PO[j] + cut, n)], r_w + 1 + j, dev(yy=yy, cc=cc), s_w + 1 + cc)

    r_y = r_idx.take(2)
    r_xp = r_idx.take(4)
    r_xm = r_idx.take(4)
    r_f = r_idx.take(4)

    def unit(p, xx, h):
        return lambda cut: Gb.at[p, :, xx, h, :, pl.ds(cut, WIN - cut)]

    def got_unit(p, xx, h, r):
        by_core(c, lambda cut: got(unit(p, xx, h)(cut), r))

    def to_x(p, k, h):
        post_cut(c, unit(p, x, h), unit(p, x, h), r_xp + 2 * p + k, dev(xx=xp))
        post_cut(c, unit(p, x, h), unit(p, x, h), r_xm + 2 * p + k, dev(xx=xm))

    def forward_up(k, h):
        got_unit(0, xm, h, r_xp + k)
        post_cut(c, unit(0, xm, h), unit(0, xm, h), r_f + k, dev(xx=xp))

    def forward_down(k, h):
        got_unit(1, xp, h, r_xm + 2 + k)
        post_cut(c, unit(1, xp, h), unit(1, xp, h), r_f + 2 + k, dev(xx=xm))

    def to_partner(k, h):
        post_cut(c, unit(0, x, h), unit(1, x, h), r_y + k, dev(yy=tp))

    def from_partner(k, h):
        got_unit(1, x, h, r_y + k)

    g_local.wait()
    by_core(c, lambda cut: got(Gb.at[0, oc, x, zh, :, pl.ds(cut, WIN - cut)], r_g0))
    to_partner(0, zh)
    to_x(0, 0, zh)

    r_c = r_idx.take(8)
    half = lax.rem(zl, 2)

    def x_block(q, blk):
        return XT.at[pl.ds(2 * q, 2), :, pl.ds(pl.multiple_of(blk * 256, 256), 256)]

    def x_group(q, yy, cc):
        chip = (1 - q) * yy + q * w_pair(yy, cc)
        return ctx_ref.at[pl.ds(2 * chip, 2)]

    def got_x(q, blk):
        got(x_block(q, blk), r_c + 2 * blk + q)

    def transpose_x(s, blk):
        t = XT[s, :, blk * 256:(blk + 1) * 256].T
        Xb[s, blk] = t.reshape(4, 64, ROWS)

    def send_context(y_to, cc):
        post(x_group(half, y_to, cc), x_block(half, 2 + c), r_c + 2 * (2 + c) + half, dev(yy=y_to, cc=cc))

    send_context(tp, c)
    x_locals = []
    for q in range(2):
        x_locals.append(local(x_group(q, y, c), x_block(q, c)))
        post(x_group(q, y, oc), x_block(q, c), r_c + 2 * c + q, other_core)

    w_locals = []
    for j in range(NP):
        cols = pl.ds(PO[j], PW[j])
        w_locals.append(local(w_ref.at[:, w_cols(c, j)], Wb.at[c, :, cols]))
        send(w_ref.at[:, w_cols(oc, j)], Wb.at[c, :, cols], r_w, other_core, s_w)


    from_partner(0, zh)
    to_x(1, 0, zh)
    send_context(wp, oc)
    send_w(0)
    forward_up(0, zh)
    for cp in x_locals:
        cp.wait()
    for q in range(2):
        got_x(q, oc)
    for blk in range(2):
        for sl in range(4):
            transpose_x(sl, blk)
    for blk in (2, 3):
        got_x(half, blk)
        post(x_block(half, blk), x_block(half, blk), r_c + 2 * blk + half, dev(ll=flip(zl)))
    for blk in (2, 3):
        for sl in range(2):
            transpose_x(2 * half + sl, blk)
    forward_down(0, zh)

    got_unit(0, x, zn, r_g1)
    to_partner(1, zn)
    to_x(0, 1, zn)
    for j in range(1, NP):
        send_w(j)
    from_partner(1, zn)
    to_x(1, 1, zn)

    for blk in (2, 3):
        got_x(1 - half, blk)
        for sl in range(2):
            transpose_x(2 * (1 - half) + sl, blk)
    for cp in w_locals:
        cp.wait()
    got(Wb.at[oc], r_w)

    def project(j):
        @pl.loop(0, 4)
        def _(blk):
            total = None
            for sl in range(4):
                a = Xb[sl, blk].reshape(256, ROWS)
                part = jnp.dot(a, Wb[sl, :, PO[j]:PO[j] + PW[j]], preferred_element_type=F32)
                total = part if total is None else total + part
            PF[j][blk] = total.reshape(4, 64, PW[j])

    r_a = r_idx.take(2 * NP)
    r_b1 = r_idx.take(2 * NP)
    r_b2 = r_idx.take(2 * NP)
    to_xp, to_xm = dev(xx=xp), dev(xx=xm)

    def drain(src, s):
        pltpu.make_async_remote_copy(
            src_ref=src, dst_ref=src, send_sem=ss.at[s], recv_sem=rs.at[0],
            device_id=other_core, device_id_type=MESH,
        ).wait_send()

    def got_w(j):
        if j > 0:
            got(Wb.at[2:4, :, pl.ds(PO[j], PW[j])], r_w + 1 + j)
            return
        by_core(c, lambda cut: got(Wb.at[2:4, :, pl.ds(cut, PW[0] - cut)], r_w + 1))
        keep = (c == 0).astype(BF16)
        for s in range(2):
            Wb[s, :, 0:SHARED] = Wb[s, :, 0:SHARED] * keep

    def project_chunk(j):
        got_w(j)
        project(j)

    def part(ref, j, *where):
        return lambda cut: ref[j].at[(*where, slice(None), slice(None), pl.ds(cut, PW[j] - cut))]

    def post_part(j, src, dst, where, r, to):
        a, b = part(src, j, *where), part(dst, j, *where)
        if j == 0:
            post_cut(c, a, b, r, to)
        else:
            post(a(0), b(0), r, to)

    def got_part(j, dst, where, r):
        a = part(dst, j, *where)
        if j == 0:
            by_core(c, lambda cut: got(a(cut), r))
        else:
            got(a(0), r)

    def post_a(j):
        bufA[j][...] = PF[j][:, x2].astype(BF16).reshape(2, 2, 64, PW[j])
        post_part(j, bufA, RA, (0,), r_a + 2 * j, to_xp)
        post_part(j, bufA, RA, (1,), r_a + 2 * j + 1, to_xm)

    def post_b(j):
        bufB1[j][1] = PF[j][2:4, xp].astype(BF16)
        post_part(j, bufB1, RB1, (1,), r_b1 + 2 * j + 1, to_xp)
        bufB2[j][0] = PF[j][0:2, xm].astype(BF16)
        post_part(j, bufB2, RB2, (0,), r_b2 + 2 * j, to_xm)

    def pass_on(j):
        got_part(j, RA, (0,), r_a + 2 * j)
        bufB1[j][0] = (PF[j][0:2, xp] + RA[j][0].astype(F32)).astype(BF16)
        post_part(j, bufB1, RB1, (0,), r_b1 + 2 * j, to_xp)
        got_part(j, RA, (1,), r_a + 2 * j + 1)
        bufB2[j][1] = (PF[j][2:4, xm] + RA[j][1].astype(F32)).astype(BF16)
        post_part(j, bufB2, RB2, (1,), r_b2 + 2 * j + 1, to_xm)

    r_dy, r_dc, r_dz = r_idx.take(4), r_idx.take(4), r_idx.take(4)
    s_dc = s_idx.take(4)
    r_rl = r_idx.take(2)
    s_dz = s_idx.take(6)
    n1, n2 = 3 - x, flip(x)
    blocks = (x, n1, n2, x2)

    def back(k, first=0, last=4):
        d = blocks[k]

        @pl.loop(first, last)
        def _(s):
            g = Gb[:, :, d].reshape(256, WIN)
            t = lax.dot_general(g, Wb[s], (((1,), (1,)), ((), ())),
                                preferred_element_type=F32).astype(BF16)
            t = jnp.concatenate([t, jnp.zeros((256, 256 - ROWS), BF16)], axis=1)
            t = t.reshape(2, 2, 64, 256)
            OWN[k, s] = t[0]
            DY[k, s] = t[1]

        if last == 4:
            post(DY.at[k], RDY.at[k], r_dy + k, dev(yy=tp))

    r_wg = r_idx.take(4)
    s_wg = s_idx.take(3)

    def grad(s, j):
        cols = pl.ds(pl.multiple_of(j * CW, 128), CW)
        b = Gb[:, :, :, :, :, cols].reshape(1024, CW)
        return jnp.dot(XT[s], b, preferred_element_type=F32).astype(BF16)

    own_groups = (y, wp)
    got_groups = (tp, w_pair(tp, c))

    def to_core(k):
        got(RDY.at[k], r_dy + k)
        for q in range(2):
            for part, group in ((OWN, own_groups[q]), (RDY, got_groups[q])):
                send(part.at[k, pl.ds(2 * q, 2), oc], RDC.at[k, group], r_dc + k, other_core, s_dc + k)

    def to_ao(k):
        d = blocks[k]
        got(RDC.at[k], r_dc + k)
        for q in range(2):
            for part, group in ((OWN, own_groups[q]), (RDY, got_groups[q])):
                TZ[d, group] = (part[k, 2 * q:2 * q + 2, c].astype(F32)
                                + RDC[k, group].astype(F32)).astype(BF16)

        neighbour = 1 + lax.div(zl, 3)
        relay = jnp.logical_and(jnp.logical_not(middle), jnp.logical_and(d != zl, d != neighbour))
        held = jnp.logical_and(middle, jnp.logical_or(d == far, d == mate))

        @pl.when(relay)
        def _():
            r = lax.min(lax.rem(d, 3), 1)
            send(TZ.at[d], RL.at[r], r_rl + r, dev(ll=neighbour), s_dz + k)

        @pl.when(jnp.logical_not(jnp.logical_or(relay, jnp.logical_or(held, d == zl))))
        def _():
            send(TZ.at[d], RDZ.at[zl], r_dz + zl, dev(ll=d), s_dz + k)

        @pl.when(d == zl)
        def _():
            RDZ[zl] = TZ[d]

    def relay_on(*ks):
        for r, d in ((0, far), (1, mate)):
            due = d == blocks[ks[0]]
            for k in ks[1:]:
                due = jnp.logical_or(due, d == blocks[k])

            @pl.when(jnp.logical_and(middle, due))
            def _():
                got(RL.at[r], r_rl + r)
                TZ[d] = (TZ[d].astype(F32) + RL[r].astype(F32)).astype(BF16)
                send(TZ.at[d], RDZ.at[zl], r_dz + zl, dev(ll=d), s_dz + 4 + r)

    def grad_other(core):
        to = dev(yy=wp, cc=core)

        @pl.loop(0, NC)
        def _(j):
            DWs[core, j] = grad(2 + core, j)
            send(DWs.at[core, j], RW.at[c, 1, j], r_wg + 2 * c + 1, to, s_wg + core)

    def grad_core():
        @pl.loop(0, NC)
        def _(j):
            DWs[2, j] = grad(oc, j)
            send(DWs.at[2, j], RW.at[c, 0, j], r_wg + 2 * c, other_core, s_wg + 2)

    def grad_own():
        @pl.loop(0, NC)
        def _(j):
            RW[c, 0, j] = grad(c, j)

    r_py, r_pz, r_pc = r_idx.take(NP), r_idx.take(NP + 1), r_idx.take(NP)

    def to_y(j):
        got_part(j, RB1, (1,), r_b1 + 2 * j + 1)
        got_part(j, RB2, (1,), r_b2 + 2 * j + 1)
        v = PF[j][2:4, x] + RB1[j][1].astype(F32) + RB2[j][1].astype(F32)
        bufY[j][...] = v.astype(BF16).reshape(2, 2, TOK, PW[j])
        post_part(j, bufY, RY, (slice(None),), r_py + j, dev(yy=tp))

    def post_z(j, core):
        def rows(ref, i):
            return lambda cut: ref[j].at[i, :, pl.ds(cut, PW[j] - cut)]

        if j == 0:
            post_cut(c, rows(bufZ, core), rows(RZ, c), r_pz + NP * c, dev(hh=zn, cc=core))
        else:
            post(bufZ[j].at[core], RZ[j].at[c], r_pz + j, dev(hh=zn, cc=core))

    def to_z(j):
        got_part(j, RB1, (0,), r_b1 + 2 * j)
        got_part(j, RB2, (0,), r_b2 + 2 * j)
        v = PF[j][0:2, x] + RB1[j][0].astype(F32) + RB2[j][0].astype(F32)
        got_part(j, RY, (slice(None),), r_py + j)
        v = v.reshape(2, 2, TOK, PW[j]) + RY[j][...].astype(F32)
        accP[j][...] = v
        bufZ[j][...] = accP[j][:, zn].astype(BF16)
        for core in (c, oc):
            post_z(j, core)
        bufC[j][...] = accP[j][oc, zh]
        post(bufC[j], RC[j], r_pc + j, other_core)

    def finish_update(j):
        got(RC[j], r_pc + j)
        if j == 0:
            got(RZ[0].at[0], r_pz)
            got(RZ[0].at[1, :, pl.ds(SHARED, PW[0] - SHARED)], r_pz + NP)
        else:
            got(RZ[j], r_pz + j)
        for w in (1, 0):
            cols = slice(w * SHIFT + PO[j], w * SHIFT + PO[j] + PW[j])
            v = jnp.where(c == w, accP[j][c, zh], RC[j][...]) + RZ[j][w].astype(F32)
            upd_ref[:, cols] = (res_ref[:, cols].astype(F32) + v).astype(BF16)

    def finish_weight_grad():
        got(RW.at[oc, 0], r_wg + 2 * oc)
        for w in range(2):
            got(RW.at[w, 1], r_wg + 2 * w + 1)

        for w in (1, 0):
            @pl.loop(0, NC)
            def _(j):
                cols = pl.ds(pl.multiple_of(w * SHIFT + j * CW, 128), CW)
                WG[:, cols] = (RW[w, 0, j].astype(F32) + RW[w, 1, j].astype(F32)).astype(BF16)

        return local(WG, wg_ref)

    def finish_context_grad():
        for m in (1, 2, 3):
            src = lax.rem(zl + m, 4)

            @pl.when(src != absent)
            def _():
                got(RDZ.at[src], r_dz + src)

        total = RDZ[0].astype(F32)
        for m in (1, 2, 3):
            total = total + RDZ[m].astype(F32)
        total = total.astype(BF16).reshape(8, 64, 256)
        CG[...] = jnp.concatenate([total[g][:, :ROWS] for g in range(8)], axis=1)
        return local(CG, cg_ref)

    project_chunk(0)
    forward_up(1, zn)
    post_a(0)
    back(0, 0, 2)
    forward_down(1, zn)
    post_b(0)
    for j in range(1, NP):
        got_w(j)
    back(0, 2, 4)
    for h, k in ((zh, 0), (zn, 1)):
        got_unit(1, xm, h, r_xp + 2 + k)
        got_unit(0, xp, h, r_xm + k)
    back(1)
    project(1)
    post_a(1)
    back(2)
    pass_on(0)
    post_b(1)
    to_core(0)
    for k, h in ((0, zh), (1, zn)):
        got_unit(0, x2, h, r_f + k)
        got_unit(1, x2, h, r_f + 2 + k)
    back(3)
    to_ao(0)
    to_core(1)
    grad_other(0)
    to_ao(1)
    to_core(2)
    grad_other(1)
    to_ao(2)
    pass_on(1)
    to_core(3)
    relay_on(0, 1)
    project(2)
    project(3)
    post_a(2)
    post_a(3)
    post_b(2)
    post_b(3)
    to_y(0)
    to_ao(3)

    grad_core()
    relay_on(2)
    grad_own()
    to_z(0)
    relay_on(3)
    to_y(1)
    pass_on(2)
    pass_on(3)
    to_z(1)
    to_y(2)
    to_y(3)
    wg_out = finish_weight_grad()
    to_z(2)
    to_z(3)
    finish_update(0)
    finish_update(1)
    cg_out = finish_context_grad()
    finish_update(2)
    finish_update(3)

    wg_out.wait()
    cg_out.wait()
    for cp in sent:
        cp.wait_send()
    for cc in range(2):
        for core, src, i in sent_cut:
            @pl.when(core == cc)
            def _():
                drain(src(cc * SHARED), i)

    for s in range(3):
        drain(DWs.at[s], s_wg + s)
    for k in range(4):
        drain(RDC.at[k], s_dc + k)
    for to, n in ((0, WIN), (1, WIN), (2, WIN - SHARED)):
        drain(Wb.at[0, :, pl.ds(0, n)], s_w + to)
    for k in range(4):
        d = blocks[k]

        @pl.when(jnp.logical_not(jnp.logical_or(d == zl, jnp.logical_and(middle, jnp.logical_or(d == far, d == mate)))))
        def _():
            drain(TZ.at[d], s_dz + k)

    @pl.when(middle)
    def _():
        drain(TZ.at[far], s_dz + 4)
        drain(TZ.at[mate], s_dz + 5)


def hand_over(a, b, d, a_out, b_out, d_out, va, vb, vd, sems):
    moves = [(d.at[:, pl.ds(o, n)], vd.at[:, pl.ds(o, n)], d_out.at[:, pl.ds(o, n)])
             for o, n in ((0, 1024), (1024, 1024), (2048, 1024), (3072, 640))]
    moves += [(a, va, a_out), (b, vb, b_out)]
    arrive = [pltpu.make_async_copy(src, mid, sems.at[0, i]) for i, (src, mid, _) in enumerate(moves)]
    leave = [pltpu.make_async_copy(mid, dst, sems.at[1, i]) for i, (_, mid, dst) in enumerate(moves)]
    for cp in arrive:
        cp.start()
    for first, second in zip(arrive, leave):
        first.wait()
        second.start()
    for cp in leave:
        cp.wait()


def per_device(residual, context, proj_weight, out_grad):
    vmem = pl.BlockSpec(memory_space=pltpu.VMEM)
    anywhere = pl.BlockSpec(memory_space=pl.ANY)
    shape = jax.ShapeDtypeStruct
    updated, context_grad, weight_grad = pl.pallas_call(
        kernel,
        out_shape=(
            shape((TOK, D_ROW), BF16),
            shape((64, 8 * ROWS), BF16),
            shape((ROWS, D_ROW), BF16),
        ),
        in_specs=[vmem, anywhere, anywhere, anywhere],
        out_specs=(vmem, anywhere, anywhere),
        scratch_shapes=[
            pltpu.VMEM((4, ROWS, WIN), BF16),
            pltpu.VMEM((2, 2, 4, 2, TOK, WIN), BF16),
            pltpu.VMEM((4, 4, 4, 64, ROWS), BF16),
            pltpu.VMEM((4, ROWS, 1024), BF16),
            [pltpu.VMEM((2, 2, 64, w), BF16) for w in PW],
            [pltpu.VMEM((2, 2, 64, w), BF16) for w in PW],
            [pltpu.VMEM((2, 2, 64, w), BF16) for w in PW],
            [pltpu.VMEM((2, 2, 64, w), BF16) for w in PW],
            [pltpu.VMEM((2, 2, 64, w), BF16) for w in PW],
            [pltpu.VMEM((2, 2, 64, w), BF16) for w in PW],
            [pltpu.VMEM((4, 4, 64, w), F32) for w in PW],
            [pltpu.VMEM((2, 2, TOK, w), F32) for w in PW],
            [pltpu.VMEM((2, 2, TOK, w), BF16) for w in PW],
            [pltpu.VMEM((2, 2, TOK, w), BF16) for w in PW],
            [pltpu.VMEM((2, TOK, w), BF16) for w in PW],
            [pltpu.VMEM((2, TOK, w), BF16) for w in PW],
            [pltpu.VMEM((TOK, w), F32) for w in PW],
            [pltpu.VMEM((TOK, w), F32) for w in PW],
            pltpu.VMEM((4, 4, 2, 64, 256), BF16),
            pltpu.VMEM((4, 4, 2, 64, 256), BF16),
            pltpu.VMEM((4, 4, 2, 64, 256), BF16),
            pltpu.VMEM((4, 4, 2, 64, 256), BF16),
            pltpu.VMEM((4, 4, 2, 64, 256), BF16),
            pltpu.VMEM((4, 4, 2, 64, 256), BF16),
            pltpu.VMEM((2, 4, 2, 64, 256), BF16),
            pltpu.VMEM((3, NC, ROWS, CW), BF16),
            pltpu.VMEM((2, 2, NC, ROWS, CW), BF16),
            pltpu.VMEM((ROWS, D_ROW), BF16),
            pltpu.VMEM((64, 8 * ROWS), BF16),
            pltpu.SemaphoreType.DMA((S_SEMS,)),
            pltpu.SemaphoreType.DMA((R_SEMS,)),
            pltpu.SemaphoreType.DMA((L_SEMS,)),
        ],
        compiler_params=pltpu.CompilerParams(
            collective_id=0, has_side_effects=True, vmem_limit_bytes=60 * 2**20
        ),
        cost_estimate=pl.CostEstimate(
            flops=6 * 1024 * 928 * WIN, bytes_accessed=8 * 2**20, transcendentals=0
        ),
    )(residual, context.T.reshape(8, ROWS, 256), proj_weight[0], out_grad)
    updated, context_grad, weight_grad = pl.pallas_call(
        hand_over,
        out_shape=(
            shape((TOK, D_ROW), BF16),
            shape((64, 8 * ROWS), BF16),
            shape((ROWS, D_ROW), BF16),
        ),
        in_specs=[anywhere] * 3,
        out_specs=(anywhere,) * 3,
        scratch_shapes=[
            pltpu.VMEM((TOK, D_ROW), BF16),
            pltpu.VMEM((64, 8 * ROWS), BF16),
            pltpu.VMEM((ROWS, D_ROW), BF16),
            pltpu.SemaphoreType.DMA((2, 6)),
        ],
    )(updated, context_grad, weight_grad)
    return updated, context_grad, weight_grad[None]


def solution(mesh):
    in_specs = (P(("ia", "wa"), "ao"), P("ia", "wa"), P("wa", "ia", "ao"), P(("ia", "wa"), "ao"))
    out_specs = (P(("ia", "wa"), "ao"), P(("ia", "ao"), "wa"), P("wa", "ia", "ao"))
    return jax.shard_map(
        per_device, mesh=mesh, in_specs=in_specs, out_specs=out_specs, check_vma=False
    )
```

```python
import jax
import jax.numpy as jnp
from jax import lax
from jax.experimental import pallas as pl
from jax.experimental.pallas import tpu as pltpu
from jax.sharding import PartitionSpec as P

MESH = pl.DeviceIdType.MESH
BF16 = jnp.bfloat16
F32 = jnp.float32

ROWS = 232
D_ROW = 3712
SHIFT = 1792
WIN = 1920
SHARED = 128
NC = 3
CW = WIN // NC
PW = (768, 512, 384, 256)
PO = (0, 768, 1280, 1664)
NP = len(PW)
TOK = 32


class Sems:
    def __init__(self):
        self.n = 0

    def take(self, count):
        base = self.n
        self.n += count
        return base


S_SEMS, R_SEMS, L_SEMS = 83, 84, 9


def kernel(
    res_ref, ctx_ref, w_ref, g_ref,
    upd_ref, cg_ref, wg_ref,
    Wb, Gb, Xb, XT,
    bufA, RA, bufB1, bufB2, RB1, RB2, PF, accP,
    bufY, RY, bufZ, RZ, bufC, RC,
    OWN, DY, RDY, RDC, TZ, RDZ, RL,
    DWs, RW, WG, CG,
    ss, rs, ls,
):
    ia = lax.axis_index("ia")
    wa = lax.axis_index("wa")
    zl = lax.axis_index("ao")
    y, c = lax.div(ia, 2), lax.rem(ia, 2)
    x, zh = lax.div(wa, 2), lax.rem(wa, 2)
    oc, zn = 1 - c, 1 - zh

    def flip(v):
        return v + 1 - 2 * lax.rem(v, 2)

    ya, yb = flip(y), 3 - y

    def w_pair(yy, cc):
        return (1 - cc) * flip(yy) + cc * (3 - yy)

    def t_pair(yy, cc):
        return cc * flip(yy) + (1 - cc) * (3 - yy)

    wp, tp = w_pair(y, c), t_pair(y, c)
    xp, xm, x2 = lax.rem(x + 1, 4), lax.rem(x + 3, 4), lax.rem(x + 2, 4)

    def dev(yy=y, cc=c, xx=x, hh=zh, ll=zl):
        return (2 * yy + cc, 2 * xx + hh, ll)

    other_core = dev(cc=oc)
    partners = [
        other_core,
        dev(yy=ya, cc=0), dev(yy=ya, cc=1), dev(yy=yb, cc=0), dev(yy=yb, cc=1),
        dev(xx=xp), dev(xx=xm),
        dev(hh=zn), dev(hh=zn, cc=oc),
    ] + [dev(ll=lax.rem(zl + m, 4)) for m in (1, 2, 3)]

    middle = lax.rem(zl, 3) != 0
    far = 3 * (1 - lax.rem(zl + 1, 2))

    mate = 3 - zl
    absent = 3 * (1 - lax.div(zl, 2))
    RDZ[absent] = jnp.zeros((4, 2, 64, 256), BF16)

    @pl.when(c == 1)
    def _():
        Gb[:, :, :, :, :, 0:SHARED] = jnp.zeros((2, 2, 4, 2, TOK, SHARED), BF16)
        Wb[2:4, :, 0:SHARED] = jnp.zeros((2, ROWS, SHARED), BF16)


    barrier = pltpu.get_barrier_semaphore()
    for p in partners:
        pl.semaphore_signal(barrier, inc=1, device_id=p, device_id_type=MESH)
    pl.semaphore_wait(barrier, len(partners))

    s_idx, r_idx, l_idx = Sems(), Sems(), Sems()
    sent = []
    sent_cut = []

    def send(src, dst, r, to, s=None):
        if s is None:
            s = s_idx.take(1)
        cp = pltpu.make_async_remote_copy(
            src_ref=src, dst_ref=dst, send_sem=ss.at[s], recv_sem=rs.at[r],
            device_id=to, device_id_type=MESH,
        )
        cp.start()
        return cp

    def post(*args):
        sent.append(send(*args))

    def by_core(core, act):
        for cc in range(2):
            @pl.when(core == cc)
            def _():
                act(cc * SHARED)

    def post_cut(core, src, dst, r, to):
        i = s_idx.take(1)
        by_core(core, lambda cut: send(src(cut), dst(cut), r, to, i))
        sent_cut.append((core, src, i))

    def got(dst, r):
        pltpu.make_async_remote_copy(
            src_ref=dst, dst_ref=dst, send_sem=ss.at[0], recv_sem=rs.at[r],
            device_id=other_core, device_id_type=MESH,
        ).wait_recv()

    def local(src, dst):
        cp = pltpu.make_async_copy(src, dst, ls.at[l_idx.take(1)])
        cp.start()
        return cp

    r_g0 = r_idx.take(1)
    r_g1 = r_idx.take(1)
    def g_part(cc):
        return lambda cut: g_ref.at[:, pl.ds(pl.multiple_of(cc * SHIFT + cut, 128), WIN - cut)]

    def g_slot(cut):
        return Gb.at[0, c, x, zh, :, pl.ds(cut, WIN - cut)]

    g_local = local(g_part(c)(0), Gb.at[0, c, x, zh])
    post_cut(oc, g_part(oc), g_slot, r_g0, other_core)
    post_cut(c, g_part(c), g_slot, r_g1, dev(hh=zn))
    post_cut(oc, g_part(oc), g_slot, r_g1, dev(hh=zn, cc=oc))

    r_w = r_idx.take(1 + NP)
    s_w = s_idx.take(3)

    def w_cols(cc, j):
        return pl.ds(pl.multiple_of(cc * SHIFT + PO[j], 128), PW[j])

    def send_w(j):
        for cc, yy in ((0, ya), (1, yb)):
            cut = cc * SHARED if j == 0 else 0
            n = PW[j] - cut
            src = w_ref.at[:, pl.ds(cc * SHIFT + PO[j] + cut, n)]
            send(src, Wb.at[2 + c, :, pl.ds(PO[j] + cut, n)], r_w + 1 + j, dev(yy=yy, cc=cc), s_w + 1 + cc)

    r_y = r_idx.take(2)
    r_xp = r_idx.take(4)
    r_xm = r_idx.take(4)
    r_f = r_idx.take(4)

    def unit(p, xx, h):
        return lambda cut: Gb.at[p, :, xx, h, :, pl.ds(cut, WIN - cut)]

    def got_unit(p, xx, h, r):
        by_core(c, lambda cut: got(unit(p, xx, h)(cut), r))

    def to_x(p, k, h):
        post_cut(c, unit(p, x, h), unit(p, x, h), r_xp + 2 * p + k, dev(xx=xp))
        post_cut(c, unit(p, x, h), unit(p, x, h), r_xm + 2 * p + k, dev(xx=xm))

    def forward_up(k, h):
        got_unit(0, xm, h, r_xp + k)
        post_cut(c, unit(0, xm, h), unit(0, xm, h), r_f + k, dev(xx=xp))

    def forward_down(k, h):
        got_unit(1, xp, h, r_xm + 2 + k)
        post_cut(c, unit(1, xp, h), unit(1, xp, h), r_f + 2 + k, dev(xx=xm))

    def to_partner(k, h):
        post_cut(c, unit(0, x, h), unit(1, x, h), r_y + k, dev(yy=tp))

    def from_partner(k, h):
        got_unit(1, x, h, r_y + k)

    g_local.wait()
    by_core(c, lambda cut: got(Gb.at[0, oc, x, zh, :, pl.ds(cut, WIN - cut)], r_g0))
    to_partner(0, zh)
    to_x(0, 0, zh)

    r_c = r_idx.take(8)
    half = lax.rem(zl, 2)

    def x_block(q, blk):
        return XT.at[pl.ds(2 * q, 2), :, pl.ds(pl.multiple_of(blk * 256, 256), 256)]

    def x_group(q, yy, cc):
        chip = (1 - q) * yy + q * w_pair(yy, cc)
        return ctx_ref.at[pl.ds(2 * chip, 2)]

    def got_x(q, blk):
        got(x_block(q, blk), r_c + 2 * blk + q)

    def transpose_x(s, blk):
        t = XT[s, :, blk * 256:(blk + 1) * 256].T
        Xb[s, blk] = t.reshape(4, 64, ROWS)

    def send_context(y_to, cc):
        post(x_group(half, y_to, cc), x_block(half, 2 + c), r_c + 2 * (2 + c) + half, dev(yy=y_to, cc=cc))

    send_context(tp, c)
    x_locals = []
    for q in range(2):
        x_locals.append(local(x_group(q, y, c), x_block(q, c)))
        post(x_group(q, y, oc), x_block(q, c), r_c + 2 * c + q, other_core)

    w_locals = []
    for j in range(NP):
        cols = pl.ds(PO[j], PW[j])
        w_locals.append(local(w_ref.at[:, w_cols(c, j)], Wb.at[c, :, cols]))
        send(w_ref.at[:, w_cols(oc, j)], Wb.at[c, :, cols], r_w, other_core, s_w)


    from_partner(0, zh)
    to_x(1, 0, zh)
    send_context(wp, oc)
    send_w(0)
    forward_up(0, zh)
    for cp in x_locals:
        cp.wait()
    for q in range(2):
        got_x(q, oc)
    for blk in range(2):
        for sl in range(4):
            transpose_x(sl, blk)
    for blk in (2, 3):
        got_x(half, blk)
        post(x_block(half, blk), x_block(half, blk), r_c + 2 * blk + half, dev(ll=flip(zl)))
    for blk in (2, 3):
        for sl in range(2):
            transpose_x(2 * half + sl, blk)
    forward_down(0, zh)

    got_unit(0, x, zn, r_g1)
    to_partner(1, zn)
    to_x(0, 1, zn)
    for j in range(1, NP):
        send_w(j)
    from_partner(1, zn)
    to_x(1, 1, zn)

    for blk in (2, 3):
        got_x(1 - half, blk)
        for sl in range(2):
            transpose_x(2 * (1 - half) + sl, blk)
    for cp in w_locals:
        cp.wait()
    got(Wb.at[oc], r_w)

    def project(j):
        @pl.loop(0, 4)
        def _(blk):
            total = None
            for sl in range(4):
                a = Xb[sl, blk].reshape(256, ROWS)
                part = jnp.dot(a, Wb[sl, :, PO[j]:PO[j] + PW[j]], preferred_element_type=F32)
                total = part if total is None else total + part
            PF[j][blk] = total.reshape(4, 64, PW[j])

    r_a = r_idx.take(2 * NP)
    r_b1 = r_idx.take(2 * NP)
    r_b2 = r_idx.take(2 * NP)
    to_xp, to_xm = dev(xx=xp), dev(xx=xm)

    def drain(src, s):
        pltpu.make_async_remote_copy(
            src_ref=src, dst_ref=src, send_sem=ss.at[s], recv_sem=rs.at[0],
            device_id=other_core, device_id_type=MESH,
        ).wait_send()

    def got_w(j):
        if j > 0:
            got(Wb.at[2:4, :, pl.ds(PO[j], PW[j])], r_w + 1 + j)
            return
        by_core(c, lambda cut: got(Wb.at[2:4, :, pl.ds(cut, PW[0] - cut)], r_w + 1))
        keep = (c == 0).astype(BF16)
        for s in range(2):
            Wb[s, :, 0:SHARED] = Wb[s, :, 0:SHARED] * keep

    def project_chunk(j):
        got_w(j)
        project(j)

    def part(ref, j, *where):
        return lambda cut: ref[j].at[(*where, slice(None), slice(None), pl.ds(cut, PW[j] - cut))]

    def post_part(j, src, dst, where, r, to):
        a, b = part(src, j, *where), part(dst, j, *where)
        if j == 0:
            post_cut(c, a, b, r, to)
        else:
            post(a(0), b(0), r, to)

    def got_part(j, dst, where, r):
        a = part(dst, j, *where)
        if j == 0:
            by_core(c, lambda cut: got(a(cut), r))
        else:
            got(a(0), r)

    def post_a(j):
        bufA[j][...] = PF[j][:, x2].astype(BF16).reshape(2, 2, 64, PW[j])
        post_part(j, bufA, RA, (0,), r_a + 2 * j, to_xp)
        post_part(j, bufA, RA, (1,), r_a + 2 * j + 1, to_xm)

    def post_b(j):
        bufB1[j][1] = PF[j][2:4, xp].astype(BF16)
        post_part(j, bufB1, RB1, (1,), r_b1 + 2 * j + 1, to_xp)
        bufB2[j][0] = PF[j][0:2, xm].astype(BF16)
        post_part(j, bufB2, RB2, (0,), r_b2 + 2 * j, to_xm)

    def pass_on(j):
        got_part(j, RA, (0,), r_a + 2 * j)
        bufB1[j][0] = (PF[j][0:2, xp] + RA[j][0].astype(F32)).astype(BF16)
        post_part(j, bufB1, RB1, (0,), r_b1 + 2 * j, to_xp)
        got_part(j, RA, (1,), r_a + 2 * j + 1)
        bufB2[j][1] = (PF[j][2:4, xm] + RA[j][1].astype(F32)).astype(BF16)
        post_part(j, bufB2, RB2, (1,), r_b2 + 2 * j + 1, to_xm)

    r_dy, r_dc, r_dz = r_idx.take(4), r_idx.take(4), r_idx.take(4)
    s_dc = s_idx.take(4)
    r_rl = r_idx.take(2)
    s_dz = s_idx.take(6)
    n1, n2 = 3 - x, flip(x)
    blocks = (x, n1, n2, x2)

    def back(k, first=0, last=4):
        d = blocks[k]

        @pl.loop(first, last)
        def _(s):
            g = Gb[:, :, d].reshape(256, WIN)
            t = lax.dot_general(g, Wb[s], (((1,), (1,)), ((), ())),
                                preferred_element_type=F32).astype(BF16)
            t = jnp.concatenate([t, jnp.zeros((256, 256 - ROWS), BF16)], axis=1)
            t = t.reshape(2, 2, 64, 256)
            OWN[k, s] = t[0]
            DY[k, s] = t[1]

        if last == 4:
            post(DY.at[k], RDY.at[k], r_dy + k, dev(yy=tp))

    r_wg = r_idx.take(4)
    s_wg = s_idx.take(3)

    def grad(s, j):
        cols = pl.ds(pl.multiple_of(j * CW, 128), CW)
        b = Gb[:, :, :, :, :, cols].reshape(1024, CW)
        return jnp.dot(XT[s], b, preferred_element_type=F32).astype(BF16)

    own_groups = (y, wp)
    got_groups = (tp, w_pair(tp, c))

    def to_core(k):
        got(RDY.at[k], r_dy + k)
        for q in range(2):
            for part, group in ((OWN, own_groups[q]), (RDY, got_groups[q])):
                send(part.at[k, pl.ds(2 * q, 2), oc], RDC.at[k, group], r_dc + k, other_core, s_dc + k)

    def to_ao(k):
        d = blocks[k]
        got(RDC.at[k], r_dc + k)
        for q in range(2):
            for part, group in ((OWN, own_groups[q]), (RDY, got_groups[q])):
                TZ[d, group] = (part[k, 2 * q:2 * q + 2, c].astype(F32)
                                + RDC[k, group].astype(F32)).astype(BF16)

        neighbour = 1 + lax.div(zl, 3)
        relay = jnp.logical_and(jnp.logical_not(middle), jnp.logical_and(d != zl, d != neighbour))
        held = jnp.logical_and(middle, jnp.logical_or(d == far, d == mate))

        @pl.when(relay)
        def _():
            r = lax.min(lax.rem(d, 3), 1)
            send(TZ.at[d], RL.at[r], r_rl + r, dev(ll=neighbour), s_dz + k)

        @pl.when(jnp.logical_not(jnp.logical_or(relay, jnp.logical_or(held, d == zl))))
        def _():
            send(TZ.at[d], RDZ.at[zl], r_dz + zl, dev(ll=d), s_dz + k)

        @pl.when(d == zl)
        def _():
            RDZ[zl] = TZ[d]

    def relay_on(*ks):
        for r, d in ((0, far), (1, mate)):
            due = d == blocks[ks[0]]
            for k in ks[1:]:
                due = jnp.logical_or(due, d == blocks[k])

            @pl.when(jnp.logical_and(middle, due))
            def _():
                got(RL.at[r], r_rl + r)
                TZ[d] = (TZ[d].astype(F32) + RL[r].astype(F32)).astype(BF16)
                send(TZ.at[d], RDZ.at[zl], r_dz + zl, dev(ll=d), s_dz + 4 + r)

    def grad_other(core):
        to = dev(yy=wp, cc=core)

        @pl.loop(0, NC)
        def _(j):
            DWs[core, j] = grad(2 + core, j)
            send(DWs.at[core, j], RW.at[c, 1, j], r_wg + 2 * c + 1, to, s_wg + core)

    def grad_core():
        @pl.loop(0, NC)
        def _(j):
            DWs[2, j] = grad(oc, j)
            send(DWs.at[2, j], RW.at[c, 0, j], r_wg + 2 * c, other_core, s_wg + 2)

    def grad_own():
        @pl.loop(0, NC)
        def _(j):
            RW[c, 0, j] = grad(c, j)

    r_py, r_pz, r_pc = r_idx.take(NP), r_idx.take(NP + 1), r_idx.take(NP)

    def to_y(j):
        got_part(j, RB1, (1,), r_b1 + 2 * j + 1)
        got_part(j, RB2, (1,), r_b2 + 2 * j + 1)
        v = PF[j][2:4, x] + RB1[j][1].astype(F32) + RB2[j][1].astype(F32)
        bufY[j][...] = v.astype(BF16).reshape(2, 2, TOK, PW[j])
        post_part(j, bufY, RY, (slice(None),), r_py + j, dev(yy=tp))

    def post_z(j, core):
        def rows(ref, i):
            return lambda cut: ref[j].at[i, :, pl.ds(cut, PW[j] - cut)]

        if j == 0:
            post_cut(c, rows(bufZ, core), rows(RZ, c), r_pz + NP * c, dev(hh=zn, cc=core))
        else:
            post(bufZ[j].at[core], RZ[j].at[c], r_pz + j, dev(hh=zn, cc=core))

    def to_z(j):
        got_part(j, RB1, (0,), r_b1 + 2 * j)
        got_part(j, RB2, (0,), r_b2 + 2 * j)
        v = PF[j][0:2, x] + RB1[j][0].astype(F32) + RB2[j][0].astype(F32)
        got_part(j, RY, (slice(None),), r_py + j)
        v = v.reshape(2, 2, TOK, PW[j]) + RY[j][...].astype(F32)
        accP[j][...] = v
        bufZ[j][...] = accP[j][:, zn].astype(BF16)
        for core in (c, oc):
            post_z(j, core)
        bufC[j][...] = accP[j][oc, zh]
        post(bufC[j], RC[j], r_pc + j, other_core)

    def finish_update(j):
        got(RC[j], r_pc + j)
        if j == 0:
            got(RZ[0].at[0], r_pz)
            got(RZ[0].at[1, :, pl.ds(SHARED, PW[0] - SHARED)], r_pz + NP)
        else:
            got(RZ[j], r_pz + j)
        for w in (1, 0):
            cols = slice(w * SHIFT + PO[j], w * SHIFT + PO[j] + PW[j])
            v = jnp.where(c == w, accP[j][c, zh], RC[j][...]) + RZ[j][w].astype(F32)
            upd_ref[:, cols] = (res_ref[:, cols].astype(F32) + v).astype(BF16)

    def finish_weight_grad():
        got(RW.at[oc, 0], r_wg + 2 * oc)
        for w in range(2):
            got(RW.at[w, 1], r_wg + 2 * w + 1)

        for w in (1, 0):
            @pl.loop(0, NC)
            def _(j):
                cols = pl.ds(pl.multiple_of(w * SHIFT + j * CW, 128), CW)
                WG[:, cols] = (RW[w, 0, j].astype(F32) + RW[w, 1, j].astype(F32)).astype(BF16)

        return local(WG, wg_ref)

    def finish_context_grad():
        for m in (1, 2, 3):
            src = lax.rem(zl + m, 4)

            @pl.when(src != absent)
            def _():
                got(RDZ.at[src], r_dz + src)

        total = RDZ[0].astype(F32)
        for m in (1, 2, 3):
            total = total + RDZ[m].astype(F32)
        total = total.astype(BF16).reshape(8, 64, 256)
        CG[...] = jnp.concatenate([total[g][:, :ROWS] for g in range(8)], axis=1)
        return local(CG, cg_ref)

    project_chunk(0)
    forward_up(1, zn)
    post_a(0)
    back(0, 0, 2)
    forward_down(1, zn)
    post_b(0)
    for j in range(1, NP):
        got_w(j)
    back(0, 2, 4)
    for h, k in ((zh, 0), (zn, 1)):
        got_unit(1, xm, h, r_xp + 2 + k)
        got_unit(0, xp, h, r_xm + k)
    back(1)
    project(1)
    post_a(1)
    back(2)
    pass_on(0)
    post_b(1)
    to_core(0)
    for k, h in ((0, zh), (1, zn)):
        got_unit(0, x2, h, r_f + k)
        got_unit(1, x2, h, r_f + 2 + k)
    back(3)
    to_ao(0)
    to_core(1)
    grad_other(0)
    to_ao(1)
    to_core(2)
    grad_other(1)
    to_ao(2)
    pass_on(1)
    to_core(3)
    relay_on(0, 1)
    project(2)
    project(3)
    post_a(2)
    post_a(3)
    post_b(2)
    post_b(3)
    to_y(0)
    to_ao(3)

    grad_core()
    relay_on(2)
    grad_own()
    relay_on(3)
    to_z(0)
    to_y(1)
    pass_on(2)
    pass_on(3)
    to_y(2)
    to_y(3)
    to_z(1)
    to_z(2)
    to_z(3)
    wg_out = finish_weight_grad()
    finish_update(0)
    finish_update(1)
    cg_out = finish_context_grad()
    finish_update(2)
    finish_update(3)

    wg_out.wait()
    cg_out.wait()
    for cp in sent:
        cp.wait_send()
    for cc in range(2):
        for core, src, i in sent_cut:
            @pl.when(core == cc)
            def _():
                drain(src(cc * SHARED), i)

    for s in range(3):
        drain(DWs.at[s], s_wg + s)
    for k in range(4):
        drain(RDC.at[k], s_dc + k)
    for to, n in ((0, WIN), (1, WIN), (2, WIN - SHARED)):
        drain(Wb.at[0, :, pl.ds(0, n)], s_w + to)
    for k in range(4):
        d = blocks[k]

        @pl.when(jnp.logical_not(jnp.logical_or(d == zl, jnp.logical_and(middle, jnp.logical_or(d == far, d == mate)))))
        def _():
            drain(TZ.at[d], s_dz + k)

    @pl.when(middle)
    def _():
        drain(TZ.at[far], s_dz + 4)
        drain(TZ.at[mate], s_dz + 5)


def hand_over(a, b, d, a_out, b_out, d_out, va, vb, vd, sems):
    moves = [(d.at[:, pl.ds(o, n)], vd.at[:, pl.ds(o, n)], d_out.at[:, pl.ds(o, n)])
             for o, n in ((0, 1024), (1024, 1024), (2048, 1024), (3072, 640))]
    moves += [(a, va, a_out), (b, vb, b_out)]
    arrive = [pltpu.make_async_copy(src, mid, sems.at[0, i]) for i, (src, mid, _) in enumerate(moves)]
    leave = [pltpu.make_async_copy(mid, dst, sems.at[1, i]) for i, (_, mid, dst) in enumerate(moves)]
    for cp in arrive:
        cp.start()
    for first, second in zip(arrive, leave):
        first.wait()
        second.start()
    for cp in leave:
        cp.wait()


def per_device(residual, context, proj_weight, out_grad):
    vmem = pl.BlockSpec(memory_space=pltpu.VMEM)
    anywhere = pl.BlockSpec(memory_space=pl.ANY)
    shape = jax.ShapeDtypeStruct
    updated, context_grad, weight_grad = pl.pallas_call(
        kernel,
        out_shape=(
            shape((TOK, D_ROW), BF16),
            shape((64, 8 * ROWS), BF16),
            shape((ROWS, D_ROW), BF16),
        ),
        in_specs=[vmem, anywhere, anywhere, anywhere],
        out_specs=(vmem, anywhere, anywhere),
        scratch_shapes=[
            pltpu.VMEM((4, ROWS, WIN), BF16),
            pltpu.VMEM((2, 2, 4, 2, TOK, WIN), BF16),
            pltpu.VMEM((4, 4, 4, 64, ROWS), BF16),
            pltpu.VMEM((4, ROWS, 1024), BF16),
            [pltpu.VMEM((2, 2, 64, w), BF16) for w in PW],
            [pltpu.VMEM((2, 2, 64, w), BF16) for w in PW],
            [pltpu.VMEM((2, 2, 64, w), BF16) for w in PW],
            [pltpu.VMEM((2, 2, 64, w), BF16) for w in PW],
            [pltpu.VMEM((2, 2, 64, w), BF16) for w in PW],
            [pltpu.VMEM((2, 2, 64, w), BF16) for w in PW],
            [pltpu.VMEM((4, 4, 64, w), F32) for w in PW],
            [pltpu.VMEM((2, 2, TOK, w), F32) for w in PW],
            [pltpu.VMEM((2, 2, TOK, w), BF16) for w in PW],
            [pltpu.VMEM((2, 2, TOK, w), BF16) for w in PW],
            [pltpu.VMEM((2, TOK, w), BF16) for w in PW],
            [pltpu.VMEM((2, TOK, w), BF16) for w in PW],
            [pltpu.VMEM((TOK, w), F32) for w in PW],
            [pltpu.VMEM((TOK, w), F32) for w in PW],
            pltpu.VMEM((4, 4, 2, 64, 256), BF16),
            pltpu.VMEM((4, 4, 2, 64, 256), BF16),
            pltpu.VMEM((4, 4, 2, 64, 256), BF16),
            pltpu.VMEM((4, 4, 2, 64, 256), BF16),
            pltpu.VMEM((4, 4, 2, 64, 256), BF16),
            pltpu.VMEM((4, 4, 2, 64, 256), BF16),
            pltpu.VMEM((2, 4, 2, 64, 256), BF16),
            pltpu.VMEM((3, NC, ROWS, CW), BF16),
            pltpu.VMEM((2, 2, NC, ROWS, CW), BF16),
            pltpu.VMEM((ROWS, D_ROW), BF16),
            pltpu.VMEM((64, 8 * ROWS), BF16),
            pltpu.SemaphoreType.DMA((S_SEMS,)),
            pltpu.SemaphoreType.DMA((R_SEMS,)),
            pltpu.SemaphoreType.DMA((L_SEMS,)),
        ],
        compiler_params=pltpu.CompilerParams(
            collective_id=0, has_side_effects=True, vmem_limit_bytes=60 * 2**20
        ),
        cost_estimate=pl.CostEstimate(
            flops=6 * 1024 * 928 * WIN, bytes_accessed=8 * 2**20, transcendentals=0
        ),
    )(residual, context.T.reshape(8, ROWS, 256), proj_weight[0], out_grad)
    updated, context_grad, weight_grad = pl.pallas_call(
        hand_over,
        out_shape=(
            shape((TOK, D_ROW), BF16),
            shape((64, 8 * ROWS), BF16),
            shape((ROWS, D_ROW), BF16),
        ),
        in_specs=[anywhere] * 3,
        out_specs=(anywhere,) * 3,
        scratch_shapes=[
            pltpu.VMEM((TOK, D_ROW), BF16),
            pltpu.VMEM((64, 8 * ROWS), BF16),
            pltpu.VMEM((ROWS, D_ROW), BF16),
            pltpu.SemaphoreType.DMA((2, 6)),
        ],
    )(updated, context_grad, weight_grad)
    return updated, context_grad, weight_grad[None]


def solution(mesh):
    in_specs = (P(("ia", "wa"), "ao"), P("ia", "wa"), P("wa", "ia", "ao"), P(("ia", "wa"), "ao"))
    out_specs = (P(("ia", "wa"), "ao"), P(("ia", "ao"), "wa"), P("wa", "ia", "ao"))
    return jax.shard_map(
        per_device, mesh=mesh, in_specs=in_specs, out_specs=out_specs, check_vma=False
    )
```

```python
import jax
import jax.numpy as jnp
from jax import lax
from jax.experimental import pallas as pl
from jax.experimental.pallas import tpu as pltpu
from jax.sharding import PartitionSpec as P

MESH = pl.DeviceIdType.MESH
BF16 = jnp.bfloat16
F32 = jnp.float32

ROWS = 232
D_ROW = 3712
SHIFT = 1792
WIN = 1920
SHARED = 128
NC = 3
CW = WIN // NC
PW = (768, 512, 384, 256)
PO = (0, 768, 1280, 1664)
NP = len(PW)
TOK = 32


class Sems:
    def __init__(self):
        self.n = 0

    def take(self, count):
        base = self.n
        self.n += count
        return base


S_SEMS, R_SEMS, L_SEMS = 66, 84, 9


def kernel(
    res_ref, ctx_ref, w_ref, g_ref,
    upd_ref, cg_ref, wg_ref,
    Wb, Gb, Xb, XT,
    bufA, RA, bufB1, bufB2, RB1, RB2, PF, accP,
    bufY, RY, bufZ, RZ, bufC, RC,
    OWN, DY, RDY, RDC, TZ, RDZ, RL,
    DWs, RW, WG, CG,
    ss, rs, ls,
):
    ia = lax.axis_index("ia")
    wa = lax.axis_index("wa")
    zl = lax.axis_index("ao")
    y, c = lax.div(ia, 2), lax.rem(ia, 2)
    x, zh = lax.div(wa, 2), lax.rem(wa, 2)
    oc, zn = 1 - c, 1 - zh

    def flip(v):
        return v + 1 - 2 * lax.rem(v, 2)

    ya, yb = flip(y), 3 - y

    def w_pair(yy, cc):
        return (1 - cc) * flip(yy) + cc * (3 - yy)

    def t_pair(yy, cc):
        return cc * flip(yy) + (1 - cc) * (3 - yy)

    wp, tp = w_pair(y, c), t_pair(y, c)
    xp, xm, x2 = lax.rem(x + 1, 4), lax.rem(x + 3, 4), lax.rem(x + 2, 4)

    def dev(yy=y, cc=c, xx=x, hh=zh, ll=zl):
        return (2 * yy + cc, 2 * xx + hh, ll)

    other_core = dev(cc=oc)
    partners = [
        other_core,
        dev(yy=ya, cc=0), dev(yy=ya, cc=1), dev(yy=yb, cc=0), dev(yy=yb, cc=1),
        dev(xx=xp), dev(xx=xm),
        dev(hh=zn), dev(hh=zn, cc=oc),
    ] + [dev(ll=lax.rem(zl + m, 4)) for m in (1, 2, 3)]

    middle = lax.rem(zl, 3) != 0
    far = 3 * (1 - lax.rem(zl + 1, 2))

    mate = 3 - zl
    absent = 3 * (1 - lax.div(zl, 2))
    RDZ[absent] = jnp.zeros((4, 2, 64, 256), BF16)

    @pl.when(c == 1)
    def _():
        Gb[:, :, :, :, :, 0:SHARED] = jnp.zeros((2, 2, 4, 2, TOK, SHARED), BF16)
        Wb[2:4, :, 0:SHARED] = jnp.zeros((2, ROWS, SHARED), BF16)


    barrier = pltpu.get_barrier_semaphore()
    for p in partners:
        pl.semaphore_signal(barrier, inc=1, device_id=p, device_id_type=MESH)
    pl.semaphore_wait(barrier, len(partners))

    s_idx, r_idx, l_idx = Sems(), Sems(), Sems()
    sent = []
    sent_cut = []

    def send(src, dst, r, to, s=None):
        if s is None:
            s = s_idx.take(1)
        cp = pltpu.make_async_remote_copy(
            src_ref=src, dst_ref=dst, send_sem=ss.at[s], recv_sem=rs.at[r],
            device_id=to, device_id_type=MESH,
        )
        cp.start()
        return cp

    def post(*args):
        sent.append(send(*args))

    def by_core(core, act):
        for cc in range(2):
            @pl.when(core == cc)
            def _():
                act(cc * SHARED)

    def post_cut(core, src, dst, r, to, group=None):
        i = s_idx.take(1) if group is None else group
        by_core(core, lambda cut: send(src(cut), dst(cut), r, to, i))
        if group is None:
            sent_cut.append((core, src, i))

    def got(dst, r):
        pltpu.make_async_remote_copy(
            src_ref=dst, dst_ref=dst, send_sem=ss.at[0], recv_sem=rs.at[r],
            device_id=other_core, device_id_type=MESH,
        ).wait_recv()

    def local(src, dst):
        cp = pltpu.make_async_copy(src, dst, ls.at[l_idx.take(1)])
        cp.start()
        return cp

    r_g0 = r_idx.take(1)
    r_g1 = r_idx.take(1)
    def g_part(cc):
        return lambda cut: g_ref.at[:, pl.ds(pl.multiple_of(cc * SHIFT + cut, 128), WIN - cut)]

    def g_slot(cut):
        return Gb.at[0, c, x, zh, :, pl.ds(cut, WIN - cut)]

    g_local = local(g_part(c)(0), Gb.at[0, c, x, zh])
    post_cut(oc, g_part(oc), g_slot, r_g0, other_core)
    post_cut(c, g_part(c), g_slot, r_g1, dev(hh=zn))
    post_cut(oc, g_part(oc), g_slot, r_g1, dev(hh=zn, cc=oc))

    r_w = r_idx.take(1 + NP)
    s_w = s_idx.take(3)

    def w_cols(cc, j):
        return pl.ds(pl.multiple_of(cc * SHIFT + PO[j], 128), PW[j])

    def send_w(j):
        for cc, yy in ((0, ya), (1, yb)):
            cut = cc * SHARED if j == 0 else 0
            n = PW[j] - cut
            src = w_ref.at[:, pl.ds(cc * SHIFT + PO[j] + cut, n)]
            send(src, Wb.at[2 + c, :, pl.ds(PO[j] + cut, n)], r_w + 1 + j, dev(yy=yy, cc=cc), s_w + 1 + cc)

    r_y = r_idx.take(2)
    r_xp = r_idx.take(4)
    r_xm = r_idx.take(4)
    r_f = r_idx.take(4)

    s_x, s_f, s_y = s_idx.take(1), s_idx.take(1), s_idx.take(1)

    def unit(p, xx, h):
        return lambda cut: Gb.at[p, :, xx, h, :, pl.ds(cut, WIN - cut)]

    def got_unit(p, xx, h, r):
        by_core(c, lambda cut: got(unit(p, xx, h)(cut), r))

    def to_x(p, k, h):
        post_cut(c, unit(p, x, h), unit(p, x, h), r_xp + 2 * p + k, dev(xx=xp), s_x)
        post_cut(c, unit(p, x, h), unit(p, x, h), r_xm + 2 * p + k, dev(xx=xm), s_x)

    def forward_up(k, h):
        got_unit(0, xm, h, r_xp + k)
        post_cut(c, unit(0, xm, h), unit(0, xm, h), r_f + k, dev(xx=xp), s_f)

    def forward_down(k, h):
        got_unit(1, xp, h, r_xm + 2 + k)
        post_cut(c, unit(1, xp, h), unit(1, xp, h), r_f + 2 + k, dev(xx=xm), s_f)

    def to_partner(k, h):
        post_cut(c, unit(0, x, h), unit(1, x, h), r_y + k, dev(yy=tp), s_y)

    def from_partner(k, h):
        got_unit(1, x, h, r_y + k)

    g_local.wait()
    by_core(c, lambda cut: got(Gb.at[0, oc, x, zh, :, pl.ds(cut, WIN - cut)], r_g0))
    to_partner(0, zh)
    to_x(0, 0, zh)

    r_c = r_idx.take(8)
    half = lax.rem(zl, 2)

    def x_block(q, blk):
        return XT.at[pl.ds(2 * q, 2), :, pl.ds(pl.multiple_of(blk * 256, 256), 256)]

    def x_group(q, yy, cc):
        chip = (1 - q) * yy + q * w_pair(yy, cc)
        return ctx_ref.at[pl.ds(2 * chip, 2)]

    def got_x(q, blk):
        got(x_block(q, blk), r_c + 2 * blk + q)

    def transpose_x(s, blk):
        t = XT[s, :, blk * 256:(blk + 1) * 256].T
        Xb[s, blk] = t.reshape(4, 64, ROWS)

    def send_context(y_to, cc):
        post(x_group(half, y_to, cc), x_block(half, 2 + c), r_c + 2 * (2 + c) + half, dev(yy=y_to, cc=cc))

    send_context(tp, c)
    x_locals = []
    for q in range(2):
        x_locals.append(local(x_group(q, y, c), x_block(q, c)))
        post(x_group(q, y, oc), x_block(q, c), r_c + 2 * c + q, other_core)

    w_locals = []
    for j in range(NP):
        cols = pl.ds(PO[j], PW[j])
        w_locals.append(local(w_ref.at[:, w_cols(c, j)], Wb.at[c, :, cols]))
        send(w_ref.at[:, w_cols(oc, j)], Wb.at[c, :, cols], r_w, other_core, s_w)


    from_partner(0, zh)
    to_x(1, 0, zh)
    send_context(wp, oc)
    send_w(0)
    forward_up(0, zh)
    for cp in x_locals:
        cp.wait()
    for q in range(2):
        got_x(q, oc)
    for blk in range(2):
        for sl in range(4):
            transpose_x(sl, blk)
    for blk in (2, 3):
        got_x(half, blk)
        post(x_block(half, blk), x_block(half, blk), r_c + 2 * blk + half, dev(ll=flip(zl)))
    for blk in (2, 3):
        for sl in range(2):
            transpose_x(2 * half + sl, blk)
    forward_down(0, zh)

    got_unit(0, x, zn, r_g1)
    to_partner(1, zn)
    to_x(0, 1, zn)
    for j in range(1, NP):
        send_w(j)
    from_partner(1, zn)
    to_x(1, 1, zn)

    for blk in (2, 3):
        got_x(1 - half, blk)
        for sl in range(2):
            transpose_x(2 * (1 - half) + sl, blk)
    for cp in w_locals:
        cp.wait()
    got(Wb.at[oc], r_w)

    def project(j):
        @pl.loop(0, 4)
        def _(blk):
            total = None
            for sl in range(4):
                a = Xb[sl, blk].reshape(256, ROWS)
                part = jnp.dot(a, Wb[sl, :, PO[j]:PO[j] + PW[j]], preferred_element_type=F32)
                total = part if total is None else total + part
            PF[j][blk] = total.reshape(4, 64, PW[j])

    r_a = r_idx.take(2 * NP)
    r_b1 = r_idx.take(2 * NP)
    r_b2 = r_idx.take(2 * NP)
    to_xp, to_xm = dev(xx=xp), dev(xx=xm)

    def drain(src, s):
        pltpu.make_async_remote_copy(
            src_ref=src, dst_ref=src, send_sem=ss.at[s], recv_sem=rs.at[0],
            device_id=other_core, device_id_type=MESH,
        ).wait_send()

    def got_w(j):
        if j > 0:
            got(Wb.at[2:4, :, pl.ds(PO[j], PW[j])], r_w + 1 + j)
            return
        by_core(c, lambda cut: got(Wb.at[2:4, :, pl.ds(cut, PW[0] - cut)], r_w + 1))
        keep = (c == 0).astype(BF16)
        for s in range(2):
            Wb[s, :, 0:SHARED] = Wb[s, :, 0:SHARED] * keep

    def project_chunk(j):
        got_w(j)
        project(j)

    def part(ref, j, *where):
        return lambda cut: ref[j].at[(*where, slice(None), slice(None), pl.ds(cut, PW[j] - cut))]

    def post_part(j, src, dst, where, r, to):
        a, b = part(src, j, *where), part(dst, j, *where)
        if j == 0:
            post_cut(c, a, b, r, to)
        else:
            post(a(0), b(0), r, to)

    def got_part(j, dst, where, r):
        a = part(dst, j, *where)
        if j == 0:
            by_core(c, lambda cut: got(a(cut), r))
        else:
            got(a(0), r)

    def post_a(j):
        bufA[j][...] = PF[j][:, x2].astype(BF16).reshape(2, 2, 64, PW[j])
        post_part(j, bufA, RA, (0,), r_a + 2 * j, to_xp)
        post_part(j, bufA, RA, (1,), r_a + 2 * j + 1, to_xm)

    def post_b(j):
        bufB1[j][1] = PF[j][2:4, xp].astype(BF16)
        post_part(j, bufB1, RB1, (1,), r_b1 + 2 * j + 1, to_xp)
        bufB2[j][0] = PF[j][0:2, xm].astype(BF16)
        post_part(j, bufB2, RB2, (0,), r_b2 + 2 * j, to_xm)

    def pass_on(j):
        got_part(j, RA, (0,), r_a + 2 * j)
        bufB1[j][0] = (PF[j][0:2, xp] + RA[j][0].astype(F32)).astype(BF16)
        post_part(j, bufB1, RB1, (0,), r_b1 + 2 * j, to_xp)
        got_part(j, RA, (1,), r_a + 2 * j + 1)
        bufB2[j][1] = (PF[j][2:4, xm] + RA[j][1].astype(F32)).astype(BF16)
        post_part(j, bufB2, RB2, (1,), r_b2 + 2 * j + 1, to_xm)

    r_dy, r_dc, r_dz = r_idx.take(4), r_idx.take(4), r_idx.take(4)
    s_dc, s_dy = s_idx.take(1), s_idx.take(1)
    r_rl = r_idx.take(2)
    s_dz = s_idx.take(6)
    n1, n2 = 3 - x, flip(x)
    blocks = (x, n1, n2, x2)

    def back(k, first=0, last=4):
        d = blocks[k]

        @pl.loop(first, last)
        def _(s):
            g = Gb[:, :, d].reshape(256, WIN)
            t = lax.dot_general(g, Wb[s], (((1,), (1,)), ((), ())),
                                preferred_element_type=F32).astype(BF16)
            t = jnp.concatenate([t, jnp.zeros((256, 256 - ROWS), BF16)], axis=1)
            t = t.reshape(2, 2, 64, 256)
            OWN[k, s] = t[0]
            DY[k, s] = t[1]

        if last == 4:
            send(DY.at[k], RDY.at[k], r_dy + k, dev(yy=tp), s_dy)

    r_wg = r_idx.take(4)
    s_wg = s_idx.take(3)

    def grad(s, j):
        cols = pl.ds(pl.multiple_of(j * CW, 128), CW)
        b = Gb[:, :, :, :, :, cols].reshape(1024, CW)
        return jnp.dot(XT[s], b, preferred_element_type=F32).astype(BF16)

    own_groups = (y, wp)
    got_groups = (tp, w_pair(tp, c))

    def to_core(k):
        got(RDY.at[k], r_dy + k)
        for q in range(2):
            for part, group in ((OWN, own_groups[q]), (RDY, got_groups[q])):
                send(part.at[k, pl.ds(2 * q, 2), oc], RDC.at[k, group], r_dc + k, other_core, s_dc)

    def to_ao(k):
        d = blocks[k]
        got(RDC.at[k], r_dc + k)
        for q in range(2):
            for part, group in ((OWN, own_groups[q]), (RDY, got_groups[q])):
                TZ[d, group] = (part[k, 2 * q:2 * q + 2, c].astype(F32)
                                + RDC[k, group].astype(F32)).astype(BF16)

        neighbour = 1 + lax.div(zl, 3)
        relay = jnp.logical_and(jnp.logical_not(middle), jnp.logical_and(d != zl, d != neighbour))
        held = jnp.logical_and(middle, jnp.logical_or(d == far, d == mate))

        @pl.when(relay)
        def _():
            r = lax.min(lax.rem(d, 3), 1)
            send(TZ.at[d], RL.at[r], r_rl + r, dev(ll=neighbour), s_dz + k)

        @pl.when(jnp.logical_not(jnp.logical_or(relay, jnp.logical_or(held, d == zl))))
        def _():
            send(TZ.at[d], RDZ.at[zl], r_dz + zl, dev(ll=d), s_dz + k)

        @pl.when(d == zl)
        def _():
            RDZ[zl] = TZ[d]

    def relay_on(*ks):
        for r, d in ((0, far), (1, mate)):
            due = d == blocks[ks[0]]
            for k in ks[1:]:
                due = jnp.logical_or(due, d == blocks[k])

            @pl.when(jnp.logical_and(middle, due))
            def _():
                got(RL.at[r], r_rl + r)
                TZ[d] = (TZ[d].astype(F32) + RL[r].astype(F32)).astype(BF16)
                send(TZ.at[d], RDZ.at[zl], r_dz + zl, dev(ll=d), s_dz + 4 + r)

    def grad_other(core):
        to = dev(yy=wp, cc=core)

        @pl.loop(0, NC)
        def _(j):
            DWs[core, j] = grad(2 + core, j)
            send(DWs.at[core, j], RW.at[c, 1, j], r_wg + 2 * c + 1, to, s_wg + core)

    def grad_core():
        @pl.loop(0, NC)
        def _(j):
            DWs[2, j] = grad(oc, j)
            send(DWs.at[2, j], RW.at[c, 0, j], r_wg + 2 * c, other_core, s_wg + 2)

    def grad_own():
        @pl.loop(0, NC)
        def _(j):
            RW[c, 0, j] = grad(c, j)

    r_py, r_pz, r_pc = r_idx.take(NP), r_idx.take(NP + 1), r_idx.take(NP)

    def to_y(j):
        got_part(j, RB1, (1,), r_b1 + 2 * j + 1)
        got_part(j, RB2, (1,), r_b2 + 2 * j + 1)
        v = PF[j][2:4, x] + RB1[j][1].astype(F32) + RB2[j][1].astype(F32)
        bufY[j][...] = v.astype(BF16).reshape(2, 2, TOK, PW[j])
        post_part(j, bufY, RY, (slice(None),), r_py + j, dev(yy=tp))

    def post_z(j, core):
        def rows(ref, i):
            return lambda cut: ref[j].at[i, :, pl.ds(cut, PW[j] - cut)]

        if j == 0:
            post_cut(c, rows(bufZ, core), rows(RZ, c), r_pz + NP * c, dev(hh=zn, cc=core))
        else:
            post(bufZ[j].at[core], RZ[j].at[c], r_pz + j, dev(hh=zn, cc=core))

    def to_z(j):
        got_part(j, RB1, (0,), r_b1 + 2 * j)
        got_part(j, RB2, (0,), r_b2 + 2 * j)
        v = PF[j][0:2, x] + RB1[j][0].astype(F32) + RB2[j][0].astype(F32)
        got_part(j, RY, (slice(None),), r_py + j)
        v = v.reshape(2, 2, TOK, PW[j]) + RY[j][...].astype(F32)
        accP[j][...] = v
        bufZ[j][...] = accP[j][:, zn].astype(BF16)
        for core in (c, oc):
            post_z(j, core)
        bufC[j][...] = accP[j][oc, zh]
        post(bufC[j], RC[j], r_pc + j, other_core)

    def finish_update(j):
        got(RC[j], r_pc + j)
        if j == 0:
            got(RZ[0].at[0], r_pz)
            got(RZ[0].at[1, :, pl.ds(SHARED, PW[0] - SHARED)], r_pz + NP)
        else:
            got(RZ[j], r_pz + j)
        for w in (1, 0):
            cols = slice(w * SHIFT + PO[j], w * SHIFT + PO[j] + PW[j])
            v = jnp.where(c == w, accP[j][c, zh], RC[j][...]) + RZ[j][w].astype(F32)
            upd_ref[:, cols] = (res_ref[:, cols].astype(F32) + v).astype(BF16)

    def finish_weight_grad():
        got(RW.at[oc, 0], r_wg + 2 * oc)
        for w in range(2):
            got(RW.at[w, 1], r_wg + 2 * w + 1)

        for w in (1, 0):
            @pl.loop(0, NC)
            def _(j):
                cols = pl.ds(pl.multiple_of(w * SHIFT + j * CW, 128), CW)
                WG[:, cols] = (RW[w, 0, j].astype(F32) + RW[w, 1, j].astype(F32)).astype(BF16)

        return local(WG, wg_ref)

    def finish_context_grad():
        for m in (1, 2, 3):
            src = lax.rem(zl + m, 4)

            @pl.when(src != absent)
            def _():
                got(RDZ.at[src], r_dz + src)

        total = RDZ[0].astype(F32)
        for m in (1, 2, 3):
            total = total + RDZ[m].astype(F32)
        total = total.astype(BF16).reshape(8, 64, 256)
        CG[...] = jnp.concatenate([total[g][:, :ROWS] for g in range(8)], axis=1)
        return local(CG, cg_ref)

    project_chunk(0)
    forward_up(1, zn)
    post_a(0)
    back(0, 0, 2)
    forward_down(1, zn)
    post_b(0)
    for j in range(1, NP):
        got_w(j)
    back(0, 2, 4)
    for h, k in ((zh, 0), (zn, 1)):
        got_unit(1, xm, h, r_xp + 2 + k)
        got_unit(0, xp, h, r_xm + k)
    back(1)
    project(1)
    post_a(1)
    back(2)
    pass_on(0)
    post_b(1)
    to_core(0)
    for k, h in ((0, zh), (1, zn)):
        got_unit(0, x2, h, r_f + k)
        got_unit(1, x2, h, r_f + 2 + k)
    back(3)
    to_ao(0)
    to_core(1)
    grad_other(0)
    to_ao(1)
    to_core(2)
    grad_other(1)
    to_ao(2)
    pass_on(1)
    to_core(3)
    relay_on(0, 1)
    project(2)
    project(3)
    post_a(2)
    post_a(3)
    post_b(2)
    post_b(3)
    to_y(0)
    to_ao(3)

    grad_core()
    relay_on(2)
    grad_own()
    relay_on(3)
    to_z(0)
    to_y(1)
    pass_on(2)
    pass_on(3)
    to_y(2)
    to_y(3)
    to_z(1)
    to_z(2)
    to_z(3)
    wg_out = finish_weight_grad()
    finish_update(0)
    finish_update(1)
    cg_out = finish_context_grad()
    finish_update(2)
    finish_update(3)

    wg_out.wait()
    cg_out.wait()
    for cp in sent:
        cp.wait_send()
    sent_cut.append((c, lambda cut: Gb.at[:, :, 0:2, :, :, pl.ds(cut, WIN - cut)], s_x))
    sent_cut.append((c, lambda cut: Gb.at[:, :, 0, :, :, pl.ds(cut, WIN - cut)], s_f))
    sent_cut.append((c, lambda cut: Gb.at[0, :, 0, :, :, pl.ds(cut, WIN - cut)], s_y))
    for cc in range(2):
        for core, src, i in sent_cut:
            @pl.when(core == cc)
            def _():
                drain(src(cc * SHARED), i)

    for s in range(3):
        drain(DWs.at[s], s_wg + s)
    drain(RDC, s_dc)
    drain(DY, s_dy)
    for to, n in ((0, WIN), (1, WIN), (2, WIN - SHARED)):
        drain(Wb.at[0, :, pl.ds(0, n)], s_w + to)
    for k in range(4):
        d = blocks[k]

        @pl.when(jnp.logical_not(jnp.logical_or(d == zl, jnp.logical_and(middle, jnp.logical_or(d == far, d == mate)))))
        def _():
            drain(TZ.at[d], s_dz + k)

    @pl.when(middle)
    def _():
        drain(TZ.at[far], s_dz + 4)
        drain(TZ.at[mate], s_dz + 5)


def hand_over(a, b, d, a_out, b_out, d_out, va, vb, vd, sems):
    moves = [(d.at[:, pl.ds(o, n)], vd.at[:, pl.ds(o, n)], d_out.at[:, pl.ds(o, n)])
             for o, n in ((0, 1024), (1024, 1024), (2048, 1024), (3072, 640))]
    moves += [(a, va, a_out), (b, vb, b_out)]
    arrive = [pltpu.make_async_copy(src, mid, sems.at[0, i]) for i, (src, mid, _) in enumerate(moves)]
    leave = [pltpu.make_async_copy(mid, dst, sems.at[1, i]) for i, (_, mid, dst) in enumerate(moves)]
    for cp in arrive:
        cp.start()
    for first, second in zip(arrive, leave):
        first.wait()
        second.start()
    for cp in leave:
        cp.wait()


def per_device(residual, context, proj_weight, out_grad):
    vmem = pl.BlockSpec(memory_space=pltpu.VMEM)
    anywhere = pl.BlockSpec(memory_space=pl.ANY)
    shape = jax.ShapeDtypeStruct
    updated, context_grad, weight_grad = pl.pallas_call(
        kernel,
        out_shape=(
            shape((TOK, D_ROW), BF16),
            shape((64, 8 * ROWS), BF16),
            shape((ROWS, D_ROW), BF16),
        ),
        in_specs=[vmem, anywhere, anywhere, anywhere],
        out_specs=(vmem, anywhere, anywhere),
        scratch_shapes=[
            pltpu.VMEM((4, ROWS, WIN), BF16),
            pltpu.VMEM((2, 2, 4, 2, TOK, WIN), BF16),
            pltpu.VMEM((4, 4, 4, 64, ROWS), BF16),
            pltpu.VMEM((4, ROWS, 1024), BF16),
            [pltpu.VMEM((2, 2, 64, w), BF16) for w in PW],
            [pltpu.VMEM((2, 2, 64, w), BF16) for w in PW],
            [pltpu.VMEM((2, 2, 64, w), BF16) for w in PW],
            [pltpu.VMEM((2, 2, 64, w), BF16) for w in PW],
            [pltpu.VMEM((2, 2, 64, w), BF16) for w in PW],
            [pltpu.VMEM((2, 2, 64, w), BF16) for w in PW],
            [pltpu.VMEM((4, 4, 64, w), F32) for w in PW],
            [pltpu.VMEM((2, 2, TOK, w), F32) for w in PW],
            [pltpu.VMEM((2, 2, TOK, w), BF16) for w in PW],
            [pltpu.VMEM((2, 2, TOK, w), BF16) for w in PW],
            [pltpu.VMEM((2, TOK, w), BF16) for w in PW],
            [pltpu.VMEM((2, TOK, w), BF16) for w in PW],
            [pltpu.VMEM((TOK, w), F32) for w in PW],
            [pltpu.VMEM((TOK, w), F32) for w in PW],
            pltpu.VMEM((4, 4, 2, 64, 256), BF16),
            pltpu.VMEM((4, 4, 2, 64, 256), BF16),
            pltpu.VMEM((4, 4, 2, 64, 256), BF16),
            pltpu.VMEM((4, 4, 2, 64, 256), BF16),
            pltpu.VMEM((4, 4, 2, 64, 256), BF16),
            pltpu.VMEM((4, 4, 2, 64, 256), BF16),
            pltpu.VMEM((2, 4, 2, 64, 256), BF16),
            pltpu.VMEM((3, NC, ROWS, CW), BF16),
            pltpu.VMEM((2, 2, NC, ROWS, CW), BF16),
            pltpu.VMEM((ROWS, D_ROW), BF16),
            pltpu.VMEM((64, 8 * ROWS), BF16),
            pltpu.SemaphoreType.DMA((S_SEMS,)),
            pltpu.SemaphoreType.DMA((R_SEMS,)),
            pltpu.SemaphoreType.DMA((L_SEMS,)),
        ],
        compiler_params=pltpu.CompilerParams(
            collective_id=0, has_side_effects=True, vmem_limit_bytes=60 * 2**20
        ),
        cost_estimate=pl.CostEstimate(
            flops=6 * 1024 * 928 * WIN, bytes_accessed=8 * 2**20, transcendentals=0
        ),
    )(residual, context.T.reshape(8, ROWS, 256), proj_weight[0], out_grad)
    updated, context_grad, weight_grad = pl.pallas_call(
        hand_over,
        out_shape=(
            shape((TOK, D_ROW), BF16),
            shape((64, 8 * ROWS), BF16),
            shape((ROWS, D_ROW), BF16),
        ),
        in_specs=[anywhere] * 3,
        out_specs=(anywhere,) * 3,
        scratch_shapes=[
            pltpu.VMEM((TOK, D_ROW), BF16),
            pltpu.VMEM((64, 8 * ROWS), BF16),
            pltpu.VMEM((ROWS, D_ROW), BF16),
            pltpu.SemaphoreType.DMA((2, 6)),
        ],
    )(updated, context_grad, weight_grad)
    return updated, context_grad, weight_grad[None]


def solution(mesh):
    in_specs = (P(("ia", "wa"), "ao"), P("ia", "wa"), P("wa", "ia", "ao"), P(("ia", "wa"), "ao"))
    out_specs = (P(("ia", "wa"), "ao"), P(("ia", "ao"), "wa"), P("wa", "ia", "ao"))
    return jax.shard_map(
        per_device, mesh=mesh, in_specs=in_specs, out_specs=out_specs, check_vma=False
    )
```

```python
import jax
import jax.numpy as jnp
from jax import lax
from jax.experimental import pallas as pl
from jax.experimental.pallas import tpu as pltpu
from jax.sharding import PartitionSpec as P

MESH = pl.DeviceIdType.MESH
BF16 = jnp.bfloat16
F32 = jnp.float32

ROWS = 232
D_ROW = 3712
SHIFT = 1792
WIN = 1920
SHARED = 128
NC = 3
CW = WIN // NC
PW = (768, 512, 384, 256)
PO = (0, 768, 1280, 1664)
NP = len(PW)
TOK = 32


class Sems:
    def __init__(self):
        self.n = 0

    def take(self, count):
        base = self.n
        self.n += count
        return base


S_SEMS, R_SEMS, L_SEMS = 83, 84, 9


def kernel(
    res_ref, ctx_ref, w_ref, g_ref,
    upd_ref, cg_ref, wg_ref,
    Wb, Gb, Xb, XT,
    bufA, RA, bufB1, bufB2, RB1, RB2, PF, accP,
    bufY, RY, bufZ, RZ, bufC, RC,
    OWN, DY, RDY, RDC, TZ, RDZ, RL,
    DWs, RW, WG, CG,
    ss, rs, ls,
):
    ia = lax.axis_index("ia")
    wa = lax.axis_index("wa")
    zl = lax.axis_index("ao")
    y, c = lax.div(ia, 2), lax.rem(ia, 2)
    x, zh = lax.div(wa, 2), lax.rem(wa, 2)
    oc, zn = 1 - c, 1 - zh

    def flip(v):
        return v + 1 - 2 * lax.rem(v, 2)

    ya, yb = flip(y), 3 - y

    def w_pair(yy, cc):
        return (1 - cc) * flip(yy) + cc * (3 - yy)

    def t_pair(yy, cc):
        return cc * flip(yy) + (1 - cc) * (3 - yy)

    wp, tp = w_pair(y, c), t_pair(y, c)
    xp, xm, x2 = lax.rem(x + 1, 4), lax.rem(x + 3, 4), lax.rem(x + 2, 4)

    def dev(yy=y, cc=c, xx=x, hh=zh, ll=zl):
        return (2 * yy + cc, 2 * xx + hh, ll)

    other_core = dev(cc=oc)
    partners = [
        other_core,
        dev(yy=ya, cc=0), dev(yy=ya, cc=1), dev(yy=yb, cc=0), dev(yy=yb, cc=1),
        dev(xx=xp), dev(xx=xm),
        dev(hh=zn), dev(hh=zn, cc=oc),
    ] + [dev(ll=lax.rem(zl + m, 4)) for m in (1, 2, 3)]

    middle = lax.rem(zl, 3) != 0
    far = 3 * (1 - lax.rem(zl + 1, 2))

    mate = 3 - zl
    absent = 3 * (1 - lax.div(zl, 2))
    RDZ[absent] = jnp.zeros((4, 2, 64, 256), BF16)

    @pl.when(c == 1)
    def _():
        Gb[:, :, :, :, :, 0:SHARED] = jnp.zeros((2, 2, 4, 2, TOK, SHARED), BF16)
        Wb[2:4, :, 0:SHARED] = jnp.zeros((2, ROWS, SHARED), BF16)


    barrier = pltpu.get_barrier_semaphore()
    for p in partners:
        pl.semaphore_signal(barrier, inc=1, device_id=p, device_id_type=MESH)
    pl.semaphore_wait(barrier, len(partners))

    s_idx, r_idx, l_idx = Sems(), Sems(), Sems()
    sent = []
    sent_cut = []

    def send(src, dst, r, to, s=None):
        if s is None:
            s = s_idx.take(1)
        cp = pltpu.make_async_remote_copy(
            src_ref=src, dst_ref=dst, send_sem=ss.at[s], recv_sem=rs.at[r],
            device_id=to, device_id_type=MESH,
        )
        cp.start()
        return cp

    def post(*args):
        sent.append(send(*args))

    def by_core(core, act):
        for cc in range(2):
            @pl.when(core == cc)
            def _():
                act(cc * SHARED)

    def post_cut(core, src, dst, r, to):
        i = s_idx.take(1)
        by_core(core, lambda cut: send(src(cut), dst(cut), r, to, i))
        sent_cut.append((core, src, i))

    def got(dst, r):
        pltpu.make_async_remote_copy(
            src_ref=dst, dst_ref=dst, send_sem=ss.at[0], recv_sem=rs.at[r],
            device_id=other_core, device_id_type=MESH,
        ).wait_recv()

    def local(src, dst):
        cp = pltpu.make_async_copy(src, dst, ls.at[l_idx.take(1)])
        cp.start()
        return cp

    r_g0 = r_idx.take(1)
    r_g1 = r_idx.take(1)
    def g_part(cc):
        return lambda cut: g_ref.at[:, pl.ds(pl.multiple_of(cc * SHIFT + cut, 128), WIN - cut)]

    def g_slot(cut):
        return Gb.at[0, c, x, zh, :, pl.ds(cut, WIN - cut)]

    g_local = local(g_part(c)(0), Gb.at[0, c, x, zh])
    post_cut(oc, g_part(oc), g_slot, r_g0, other_core)
    post_cut(c, g_part(c), g_slot, r_g1, dev(hh=zn))
    post_cut(oc, g_part(oc), g_slot, r_g1, dev(hh=zn, cc=oc))

    r_w = r_idx.take(1 + NP)
    s_w = s_idx.take(3)

    def w_cols(cc, j):
        return pl.ds(pl.multiple_of(cc * SHIFT + PO[j], 128), PW[j])

    def send_w(j):
        for cc, yy in ((0, ya), (1, yb)):
            cut = cc * SHARED if j == 0 else 0
            n = PW[j] - cut
            src = w_ref.at[:, pl.ds(cc * SHIFT + PO[j] + cut, n)]
            send(src, Wb.at[2 + c, :, pl.ds(PO[j] + cut, n)], r_w + 1 + j, dev(yy=yy, cc=cc), s_w + 1 + cc)

    r_y = r_idx.take(2)
    r_xp = r_idx.take(4)
    r_xm = r_idx.take(4)
    r_f = r_idx.take(4)

    def unit(p, xx, h):
        return lambda cut: Gb.at[p, :, xx, h, :, pl.ds(cut, WIN - cut)]

    def got_unit(p, xx, h, r):
        by_core(c, lambda cut: got(unit(p, xx, h)(cut), r))

    def to_x(p, k, h):
        post_cut(c, unit(p, x, h), unit(p, x, h), r_xp + 2 * p + k, dev(xx=xp))
        post_cut(c, unit(p, x, h), unit(p, x, h), r_xm + 2 * p + k, dev(xx=xm))

    def forward_up(k, h):
        got_unit(0, xm, h, r_xp + k)
        post_cut(c, unit(0, xm, h), unit(0, xm, h), r_f + k, dev(xx=xp))

    def forward_down(k, h):
        got_unit(1, xp, h, r_xm + 2 + k)
        post_cut(c, unit(1, xp, h), unit(1, xp, h), r_f + 2 + k, dev(xx=xm))

    def to_partner(k, h):
        post_cut(c, unit(0, x, h), unit(1, x, h), r_y + k, dev(yy=tp))

    def from_partner(k, h):
        got_unit(1, x, h, r_y + k)

    g_local.wait()
    by_core(c, lambda cut: got(Gb.at[0, oc, x, zh, :, pl.ds(cut, WIN - cut)], r_g0))
    to_partner(0, zh)
    to_x(0, 0, zh)

    r_c = r_idx.take(8)
    half = lax.rem(zl, 2)

    def x_block(q, blk):
        return XT.at[pl.ds(2 * q, 2), :, pl.ds(pl.multiple_of(blk * 256, 256), 256)]

    def x_group(q, yy, cc):
        chip = (1 - q) * yy + q * w_pair(yy, cc)
        return ctx_ref.at[pl.ds(2 * chip, 2)]

    def got_x(q, blk):
        got(x_block(q, blk), r_c + 2 * blk + q)

    def transpose_x(s, blk):
        t = XT[s, :, blk * 256:(blk + 1) * 256].T
        Xb[s, blk] = t.reshape(4, 64, ROWS)

    def send_context(y_to, cc):
        post(x_group(half, y_to, cc), x_block(half, 2 + c), r_c + 2 * (2 + c) + half, dev(yy=y_to, cc=cc))

    send_context(tp, c)
    x_locals = []
    for q in range(2):
        x_locals.append(local(x_group(q, y, c), x_block(q, c)))
        post(x_group(q, y, oc), x_block(q, c), r_c + 2 * c + q, other_core)

    w_locals = []
    for j in range(NP):
        cols = pl.ds(PO[j], PW[j])
        w_locals.append(local(w_ref.at[:, w_cols(c, j)], Wb.at[c, :, cols]))
        send(w_ref.at[:, w_cols(oc, j)], Wb.at[c, :, cols], r_w, other_core, s_w)


    from_partner(0, zh)
    to_x(1, 0, zh)
    send_context(wp, oc)
    send_w(0)
    forward_up(0, zh)
    for cp in x_locals:
        cp.wait()
    for q in range(2):
        got_x(q, oc)
    for blk in range(2):
        for sl in range(4):
            transpose_x(sl, blk)
    for blk in (2, 3):
        got_x(half, blk)
        post(x_block(half, blk), x_block(half, blk), r_c + 2 * blk + half, dev(ll=flip(zl)))
    for blk in (2, 3):
        for sl in range(2):
            transpose_x(2 * half + sl, blk)
    forward_down(0, zh)

    got_unit(0, x, zn, r_g1)
    to_partner(1, zn)
    to_x(0, 1, zn)
    for j in range(1, NP):
        send_w(j)
    from_partner(1, zn)
    to_x(1, 1, zn)

    for blk in (2, 3):
        got_x(1 - half, blk)
        for sl in range(2):
            transpose_x(2 * (1 - half) + sl, blk)
    for cp in w_locals:
        cp.wait()
    got(Wb.at[oc], r_w)

    def project(j):
        @pl.loop(0, 4)
        def _(blk):
            total = None
            for sl in range(4):
                a = Xb[sl, blk].reshape(256, ROWS)
                part = jnp.dot(a, Wb[sl, :, PO[j]:PO[j] + PW[j]], preferred_element_type=F32)
                total = part if total is None else total + part
            PF[j][blk] = total.reshape(4, 64, PW[j])

    r_a = r_idx.take(2 * NP)
    r_b1 = r_idx.take(2 * NP)
    r_b2 = r_idx.take(2 * NP)
    to_xp, to_xm = dev(xx=xp), dev(xx=xm)

    def drain(src, s):
        pltpu.make_async_remote_copy(
            src_ref=src, dst_ref=src, send_sem=ss.at[s], recv_sem=rs.at[0],
            device_id=other_core, device_id_type=MESH,
        ).wait_send()

    def got_w(j):
        if j > 0:
            got(Wb.at[2:4, :, pl.ds(PO[j], PW[j])], r_w + 1 + j)
            return
        by_core(c, lambda cut: got(Wb.at[2:4, :, pl.ds(cut, PW[0] - cut)], r_w + 1))
        keep = (c == 0).astype(BF16)
        for s in range(2):
            Wb[s, :, 0:SHARED] = Wb[s, :, 0:SHARED] * keep

    def project_chunk(j):
        got_w(j)
        project(j)

    def part(ref, j, *where):
        return lambda cut: ref[j].at[(*where, slice(None), slice(None), pl.ds(cut, PW[j] - cut))]

    def post_part(j, src, dst, where, r, to):
        a, b = part(src, j, *where), part(dst, j, *where)
        if j == 0:
            post_cut(c, a, b, r, to)
        else:
            post(a(0), b(0), r, to)

    def got_part(j, dst, where, r):
        a = part(dst, j, *where)
        if j == 0:
            by_core(c, lambda cut: got(a(cut), r))
        else:
            got(a(0), r)

    def post_a(j):
        bufA[j][...] = PF[j][:, x2].astype(BF16).reshape(2, 2, 64, PW[j])
        post_part(j, bufA, RA, (0,), r_a + 2 * j, to_xp)
        post_part(j, bufA, RA, (1,), r_a + 2 * j + 1, to_xm)

    def post_b(j):
        bufB1[j][1] = PF[j][2:4, xp].astype(BF16)
        post_part(j, bufB1, RB1, (1,), r_b1 + 2 * j + 1, to_xp)
        bufB2[j][0] = PF[j][0:2, xm].astype(BF16)
        post_part(j, bufB2, RB2, (0,), r_b2 + 2 * j, to_xm)

    def pass_on(j):
        got_part(j, RA, (0,), r_a + 2 * j)
        bufB1[j][0] = (PF[j][0:2, xp] + RA[j][0].astype(F32)).astype(BF16)
        post_part(j, bufB1, RB1, (0,), r_b1 + 2 * j, to_xp)
        got_part(j, RA, (1,), r_a + 2 * j + 1)
        bufB2[j][1] = (PF[j][2:4, xm] + RA[j][1].astype(F32)).astype(BF16)
        post_part(j, bufB2, RB2, (1,), r_b2 + 2 * j + 1, to_xm)

    r_dy, r_dc, r_dz = r_idx.take(4), r_idx.take(4), r_idx.take(4)
    s_dc = s_idx.take(4)
    r_rl = r_idx.take(2)
    s_dz = s_idx.take(6)
    n1, n2 = 3 - x, flip(x)
    blocks = (x, n1, n2, x2)

    def back(k, first=0, last=4):
        d = blocks[k]

        @pl.loop(first, last)
        def _(s):
            g = Gb[:, :, d].reshape(256, WIN)
            t = lax.dot_general(g, Wb[s], (((1,), (1,)), ((), ())),
                                preferred_element_type=F32).astype(BF16)
            t = jnp.concatenate([t, jnp.zeros((256, 256 - ROWS), BF16)], axis=1)
            t = t.reshape(2, 2, 64, 256)
            OWN[k, s] = t[0]
            DY[k, s] = t[1]

        if last == 4:
            post(DY.at[k], RDY.at[k], r_dy + k, dev(yy=tp))

    r_wg = r_idx.take(4)
    s_wg = s_idx.take(3)

    def grad(s, j):
        cols = pl.ds(pl.multiple_of(j * CW, 128), CW)
        b = Gb[:, :, :, :, :, cols].reshape(1024, CW)
        return jnp.dot(XT[s], b, preferred_element_type=F32).astype(BF16)

    own_groups = (y, wp)
    got_groups = (tp, w_pair(tp, c))

    def to_core(k):
        got(RDY.at[k], r_dy + k)
        for q in range(2):
            for part, group in ((OWN, own_groups[q]), (RDY, got_groups[q])):
                send(part.at[k, pl.ds(2 * q, 2), oc], RDC.at[k, group], r_dc + k, other_core, s_dc + k)

    def to_ao(k):
        d = blocks[k]
        got(RDC.at[k], r_dc + k)
        for q in range(2):
            for part, group in ((OWN, own_groups[q]), (RDY, got_groups[q])):
                TZ[d, group] = (part[k, 2 * q:2 * q + 2, c].astype(F32)
                                + RDC[k, group].astype(F32)).astype(BF16)

        neighbour = 1 + lax.div(zl, 3)
        relay = jnp.logical_and(jnp.logical_not(middle), jnp.logical_and(d != zl, d != neighbour))
        held = jnp.logical_and(middle, jnp.logical_or(d == far, d == mate))

        @pl.when(relay)
        def _():
            r = lax.min(lax.rem(d, 3), 1)
            send(TZ.at[d], RL.at[r], r_rl + r, dev(ll=neighbour), s_dz + k)

        @pl.when(jnp.logical_not(jnp.logical_or(relay, jnp.logical_or(held, d == zl))))
        def _():
            send(TZ.at[d], RDZ.at[zl], r_dz + zl, dev(ll=d), s_dz + k)

        @pl.when(d == zl)
        def _():
            RDZ[zl] = TZ[d]

    def relay_on(*ks):
        for r, d in ((0, far), (1, mate)):
            due = d == blocks[ks[0]]
            for k in ks[1:]:
                due = jnp.logical_or(due, d == blocks[k])

            @pl.when(jnp.logical_and(middle, due))
            def _():
                got(RL.at[r], r_rl + r)
                TZ[d] = (TZ[d].astype(F32) + RL[r].astype(F32)).astype(BF16)
                send(TZ.at[d], RDZ.at[zl], r_dz + zl, dev(ll=d), s_dz + 4 + r)

    def grad_other(core):
        to = dev(yy=wp, cc=core)

        @pl.loop(0, NC)
        def _(j):
            DWs[core, j] = grad(2 + core, j)
            send(DWs.at[core, j], RW.at[c, 1, j], r_wg + 2 * c + 1, to, s_wg + core)

    def grad_core():
        @pl.loop(0, NC)
        def _(j):
            DWs[2, j] = grad(oc, j)
            send(DWs.at[2, j], RW.at[c, 0, j], r_wg + 2 * c, other_core, s_wg + 2)

    def grad_own():
        @pl.loop(0, NC)
        def _(j):
            RW[c, 0, j] = grad(c, j)

    r_py, r_pz, r_pc = r_idx.take(NP), r_idx.take(NP + 1), r_idx.take(NP)

    def to_y(j):
        got_part(j, RB1, (1,), r_b1 + 2 * j + 1)
        got_part(j, RB2, (1,), r_b2 + 2 * j + 1)
        v = PF[j][2:4, x] + RB1[j][1].astype(F32) + RB2[j][1].astype(F32)
        bufY[j][...] = v.astype(BF16).reshape(2, 2, TOK, PW[j])
        post_part(j, bufY, RY, (slice(None),), r_py + j, dev(yy=tp))

    def post_z(j, core):
        def rows(ref, i):
            return lambda cut: ref[j].at[i, :, pl.ds(cut, PW[j] - cut)]

        if j == 0:
            post_cut(c, rows(bufZ, core), rows(RZ, c), r_pz + NP * c, dev(hh=zn, cc=core))
        else:
            post(bufZ[j].at[core], RZ[j].at[c], r_pz + j, dev(hh=zn, cc=core))

    def to_z(j):
        got_part(j, RB1, (0,), r_b1 + 2 * j)
        got_part(j, RB2, (0,), r_b2 + 2 * j)
        v = PF[j][0:2, x] + RB1[j][0].astype(F32) + RB2[j][0].astype(F32)
        got_part(j, RY, (slice(None),), r_py + j)
        v = v.reshape(2, 2, TOK, PW[j]) + RY[j][...].astype(F32)
        accP[j][...] = v
        bufZ[j][...] = accP[j][:, zn].astype(BF16)
        for core in (c, oc):
            post_z(j, core)
        bufC[j][...] = accP[j][oc, zh]
        post(bufC[j], RC[j], r_pc + j, other_core)

    def finish_update(j):
        got(RC[j], r_pc + j)
        if j == 0:
            got(RZ[0].at[0], r_pz)
            got(RZ[0].at[1, :, pl.ds(SHARED, PW[0] - SHARED)], r_pz + NP)
        else:
            got(RZ[j], r_pz + j)
        for w in (1, 0):
            cols = slice(w * SHIFT + PO[j], w * SHIFT + PO[j] + PW[j])
            v = jnp.where(c == w, accP[j][c, zh], RC[j][...]) + RZ[j][w].astype(F32)
            upd_ref[:, cols] = (res_ref[:, cols].astype(F32) + v).astype(BF16)

    def finish_weight_grad():
        got(RW.at[oc, 0], r_wg + 2 * oc)
        for w in range(2):
            got(RW.at[w, 1], r_wg + 2 * w + 1)

        for w in (1, 0):
            @pl.loop(0, NC)
            def _(j):
                cols = pl.ds(pl.multiple_of(w * SHIFT + j * CW, 128), CW)
                WG[:, cols] = (RW[w, 0, j].astype(F32) + RW[w, 1, j].astype(F32)).astype(BF16)

        return local(WG, wg_ref)

    def finish_context_grad():
        for m in (1, 2, 3):
            src = lax.rem(zl + m, 4)

            @pl.when(src != absent)
            def _():
                got(RDZ.at[src], r_dz + src)

        total = RDZ[0].astype(F32)
        for m in (1, 2, 3):
            total = total + RDZ[m].astype(F32)
        total = total.astype(BF16).reshape(8, 64, 256)
        CG[...] = jnp.concatenate([total[g][:, :ROWS] for g in range(8)], axis=1)
        return local(CG, cg_ref)

    project_chunk(0)
    forward_up(1, zn)
    post_a(0)
    back(0, 0, 2)
    forward_down(1, zn)
    post_b(0)
    for j in range(1, NP):
        got_w(j)
    back(0, 2, 4)
    for h, k in ((zh, 0), (zn, 1)):
        got_unit(1, xm, h, r_xp + 2 + k)
        got_unit(0, xp, h, r_xm + k)
    back(1)
    project(1)
    post_a(1)
    back(2)
    pass_on(0)
    post_b(1)
    to_core(0)
    for k, h in ((0, zh), (1, zn)):
        got_unit(0, x2, h, r_f + k)
        got_unit(1, x2, h, r_f + 2 + k)
    back(3)
    to_ao(0)
    to_core(1)
    grad_other(0)
    to_ao(1)
    to_core(2)
    grad_other(1)
    to_ao(2)
    pass_on(1)
    to_core(3)
    relay_on(0, 1)
    project(2)
    to_ao(3)
    project(3)
    post_a(2)
    post_a(3)
    post_b(2)
    post_b(3)
    to_y(0)

    grad_core()
    relay_on(2)
    grad_own()
    relay_on(3)
    to_z(0)
    to_y(1)
    pass_on(2)
    pass_on(3)
    to_y(2)
    to_y(3)
    to_z(1)
    to_z(2)
    to_z(3)
    wg_out = finish_weight_grad()
    finish_update(0)
    finish_update(1)
    cg_out = finish_context_grad()
    finish_update(2)
    finish_update(3)

    wg_out.wait()
    cg_out.wait()
    for cp in sent:
        cp.wait_send()
    for cc in range(2):
        for core, src, i in sent_cut:
            @pl.when(core == cc)
            def _():
                drain(src(cc * SHARED), i)

    for s in range(3):
        drain(DWs.at[s], s_wg + s)
    for k in range(4):
        drain(RDC.at[k], s_dc + k)
    for to, n in ((0, WIN), (1, WIN), (2, WIN - SHARED)):
        drain(Wb.at[0, :, pl.ds(0, n)], s_w + to)
    for k in range(4):
        d = blocks[k]

        @pl.when(jnp.logical_not(jnp.logical_or(d == zl, jnp.logical_and(middle, jnp.logical_or(d == far, d == mate)))))
        def _():
            drain(TZ.at[d], s_dz + k)

    @pl.when(middle)
    def _():
        drain(TZ.at[far], s_dz + 4)
        drain(TZ.at[mate], s_dz + 5)


def hand_over(a, b, d, a_out, b_out, d_out, va, vb, vd, sems):
    moves = [(d.at[:, pl.ds(o, n)], vd.at[:, pl.ds(o, n)], d_out.at[:, pl.ds(o, n)])
             for o, n in ((0, 768), (768, 768), (1536, 768), (2304, 768), (3072, 384), (3456, 256))]
    moves += [(a, va, a_out), (b, vb, b_out)]
    arrive = [pltpu.make_async_copy(src, mid, sems.at[0, i]) for i, (src, mid, _) in enumerate(moves)]
    leave = [pltpu.make_async_copy(mid, dst, sems.at[1, i]) for i, (_, mid, dst) in enumerate(moves)]
    for cp in arrive:
        cp.start()
    for first, second in zip(arrive, leave):
        first.wait()
        second.start()
    for cp in leave:
        cp.wait()


def per_device(residual, context, proj_weight, out_grad):
    vmem = pl.BlockSpec(memory_space=pltpu.VMEM)
    anywhere = pl.BlockSpec(memory_space=pl.ANY)
    shape = jax.ShapeDtypeStruct
    updated, context_grad, weight_grad = pl.pallas_call(
        kernel,
        out_shape=(
            shape((TOK, D_ROW), BF16),
            shape((64, 8 * ROWS), BF16),
            shape((ROWS, D_ROW), BF16),
        ),
        in_specs=[vmem, anywhere, anywhere, anywhere],
        out_specs=(vmem, anywhere, anywhere),
        scratch_shapes=[
            pltpu.VMEM((4, ROWS, WIN), BF16),
            pltpu.VMEM((2, 2, 4, 2, TOK, WIN), BF16),
            pltpu.VMEM((4, 4, 4, 64, ROWS), BF16),
            pltpu.VMEM((4, ROWS, 1024), BF16),
            [pltpu.VMEM((2, 2, 64, w), BF16) for w in PW],
            [pltpu.VMEM((2, 2, 64, w), BF16) for w in PW],
            [pltpu.VMEM((2, 2, 64, w), BF16) for w in PW],
            [pltpu.VMEM((2, 2, 64, w), BF16) for w in PW],
            [pltpu.VMEM((2, 2, 64, w), BF16) for w in PW],
            [pltpu.VMEM((2, 2, 64, w), BF16) for w in PW],
            [pltpu.VMEM((4, 4, 64, w), F32) for w in PW],
            [pltpu.VMEM((2, 2, TOK, w), F32) for w in PW],
            [pltpu.VMEM((2, 2, TOK, w), BF16) for w in PW],
            [pltpu.VMEM((2, 2, TOK, w), BF16) for w in PW],
            [pltpu.VMEM((2, TOK, w), BF16) for w in PW],
            [pltpu.VMEM((2, TOK, w), BF16) for w in PW],
            [pltpu.VMEM((TOK, w), F32) for w in PW],
            [pltpu.VMEM((TOK, w), F32) for w in PW],
            pltpu.VMEM((4, 4, 2, 64, 256), BF16),
            pltpu.VMEM((4, 4, 2, 64, 256), BF16),
            pltpu.VMEM((4, 4, 2, 64, 256), BF16),
            pltpu.VMEM((4, 4, 2, 64, 256), BF16),
            pltpu.VMEM((4, 4, 2, 64, 256), BF16),
            pltpu.VMEM((4, 4, 2, 64, 256), BF16),
            pltpu.VMEM((2, 4, 2, 64, 256), BF16),
            pltpu.VMEM((3, NC, ROWS, CW), BF16),
            pltpu.VMEM((2, 2, NC, ROWS, CW), BF16),
            pltpu.VMEM((ROWS, D_ROW), BF16),
            pltpu.VMEM((64, 8 * ROWS), BF16),
            pltpu.SemaphoreType.DMA((S_SEMS,)),
            pltpu.SemaphoreType.DMA((R_SEMS,)),
            pltpu.SemaphoreType.DMA((L_SEMS,)),
        ],
        compiler_params=pltpu.CompilerParams(
            collective_id=0, has_side_effects=True, vmem_limit_bytes=60 * 2**20
        ),
        cost_estimate=pl.CostEstimate(
            flops=6 * 1024 * 928 * WIN, bytes_accessed=8 * 2**20, transcendentals=0
        ),
    )(residual, context.T.reshape(8, ROWS, 256), proj_weight[0], out_grad)
    updated, context_grad, weight_grad = pl.pallas_call(
        hand_over,
        out_shape=(
            shape((TOK, D_ROW), BF16),
            shape((64, 8 * ROWS), BF16),
            shape((ROWS, D_ROW), BF16),
        ),
        in_specs=[anywhere] * 3,
        out_specs=(anywhere,) * 3,
        scratch_shapes=[
            pltpu.VMEM((TOK, D_ROW), BF16),
            pltpu.VMEM((64, 8 * ROWS), BF16),
            pltpu.VMEM((ROWS, D_ROW), BF16),
            pltpu.SemaphoreType.DMA((2, 8)),
        ],
    )(updated, context_grad, weight_grad)
    return updated, context_grad, weight_grad[None]


def solution(mesh):
    in_specs = (P(("ia", "wa"), "ao"), P("ia", "wa"), P("wa", "ia", "ao"), P(("ia", "wa"), "ao"))
    out_specs = (P(("ia", "wa"), "ao"), P(("ia", "ao"), "wa"), P("wa", "ia", "ao"))
    return jax.shard_map(
        per_device, mesh=mesh, in_specs=in_specs, out_specs=out_specs, check_vma=False
    )
```
